256 devices in a mesh: wide: 64 (over z_hi, y, x), narrow: 4 (over z_lo, core).
Axes of the slice: x: 4, y: 4, z: 8 (z_hi: 4, z_lo: 2; z = z_hi * 2 + z_lo), core: 2. Of those that a mesh axis runs over, the one named last changes fastest.
Arguments:
- inputs: bfloat16 [1, 64, 32, 16, 512], P(None, 'wide', 'narrow'), may hold values from -6 to 6
- norm_params: float32 [2, 512], replicated, may hold values from -1 to 1.5
- w_qkv: bfloat16 [512, 1536], replicated, may hold values from -2 to 2
- w_proj: bfloat16 [512, 512], replicated, may hold values from -0.25 to 0.25
- upstream: bfloat16 [1, 64, 32, 16, 512], P(None, 'wide', 'narrow'), may hold values from -16 to 16
Outputs:
- output: bfloat16 [1, 64, 32, 16, 512], P(None, 'wide', 'narrow')
- grad_inputs: bfloat16 [1, 64, 32, 16, 512], P(None, 'wide', 'narrow')
- grad_qkv: float32 [512, 1536], P(None, 'wide')
- grad_proj: float32 [512, 512], P(None, 'wide')
- grad_norm: float32 [2, 512], P(None, 'wide')
The draws below stay inside these ranges and needn't reach their ends.
All inputs are finite; a program needn't handle non-finite values.
Results may differ from the reference program's by a relative error of at most 0.023.
The reference program's roundings to bfloat16 on the way count: a program that leaves them out, or rounds other values in their place, can miss the bound.
Values may be sent and summed in bfloat16 or wider, within the bound.
No kernel may reach another device: no remote copies, remote signals or barrier semaphores. Data moves between devices by JAX's collectives and lax.ppermute only.
A program may use at most 128 MiB of HBM per device.

```python
import jax
import jax.numpy as jnp
from jax import lax

HEADS = 16
HEAD_DIM = 32
C = 512
WIN = 8
BATCH = 1
YCELLS = 16
ZCELLS = 64
XCELLS = 32


def draw_norm_params(key, part):
    key = jax.random.fold_in(key, 13)
    gain_key, offset_key = jax.random.split(key)
    channels = HEADS * HEAD_DIM
    gains = jax.random.uniform(gain_key, (channels,), jnp.float32, 0.6, 1.4)
    offsets = jnp.clip(0.4 * jax.random.normal(offset_key, (channels,), jnp.float32), -1.0, 1.0)
    return jnp.stack([gains, offsets])


def draw_w_qkv(key, part):
    key = jax.random.fold_in(key, 7)
    weight_key = jax.random.fold_in(key, 0)
    channels = HEADS * HEAD_DIM
    weights = jax.random.normal(weight_key, (channels, 3 * channels), jnp.float32) * channels ** (-0.5)
    return jnp.clip(weights, -2.0, 2.0).astype(jnp.bfloat16)


def with_spikes(drawn, rng, source, target, parts, factor):
    def block_of(position):
        return (jnp.arange(drawn.shape[position]) // (drawn.shape[position] // parts)).reshape((-1,) + (1,) * (drawn.ndim - 1 - position))

    first = jax.random.permutation(rng, parts)[block_of(target)]
    other_side = (block_of(target) + parts // 2) % parts
    return jnp.where((block_of(source) == first) | (block_of(source) == other_side), factor * drawn, drawn)


def steps_of(key, shape, pieces, least, top_value):
    level, own = 1.0, jax.random.fold_in(key, 6)
    for position, blocks in pieces:
        steps = jnp.exp(jax.random.uniform(jax.random.fold_in(own, position), (blocks,), jnp.float32, least / len(pieces), top_value / len(pieces)))
        level = level * jnp.repeat(steps, shape[position] // blocks).reshape([-1 if axis == position else 1 for axis in range(len(shape))])
    return level


def centred(stream_key, extent, spread, reach, cuts=(), held_as=jnp.bfloat16):
    entries = jax.random.normal(stream_key, extent, jnp.float32) * spread
    if len(cuts) > 0:
        entries = steps_of(stream_key, extent, cuts, -0.22, 0.18) * entries
    return jnp.clip(entries, min=-reach, max=reach).astype(held_as)


def gaussian_with(own_key, shape, scale, most, shards, heavy, held_as=jnp.bfloat16):
    array = scale * jax.random.normal(own_key, shape, jnp.float32)
    if shards:
        array = array * steps_of(own_key, shape, shards, -0.22, 0.18)
    return jnp.clip(with_spikes(array, jax.random.fold_in(own_key, 3), *heavy), -most, most).astype(held_as)


def setup_inputs(seed: int = 0) -> dict:
    key_list = jax.random.split(jax.random.key(seed), 6)
    inputs = centred(key_list[0], (BATCH, ZCELLS, XCELLS, YCELLS, C), 1.0, 6.0, ((1, 64), (2, 4)))
    norm_params = draw_norm_params(jax.random.fold_in(key_list[5], 71), 0)
    w_qkv = draw_w_qkv(jax.random.fold_in(key_list[5], 71), 0)
    w_proj = centred(key_list[3], (C, C), C ** -0.5, 0.25)
    upstream = gaussian_with(key_list[4], (BATCH, ZCELLS, XCELLS, YCELLS, C), 1.0, 16.0, ((1, 64), (2, 4)), (1, 4, 64, 4.0))
    return dict(inputs=inputs, norm_params=norm_params, w_qkv=w_qkv, w_proj=w_proj, upstream=upstream)


def normalize(field_in, norm_params):
    floats = field_in.astype(jnp.float32)
    average = lax.optimization_barrier(jnp.mean(floats, -1, keepdims=True))
    centered = floats - average
    variance = lax.optimization_barrier(jnp.mean(centered * centered, -1, keepdims=True))
    inv_scale = lax.rsqrt(variance + 1e-05)
    unit_field = centered * inv_scale
    return (unit_field, inv_scale, unit_field * norm_params[0] + norm_params[1])

def normalize_back(d_normed, unit_field, inv_scale, norm_params):
    d_unit = d_normed * norm_params[0]
    first_mean = lax.optimization_barrier(jnp.mean(d_unit, -1, keepdims=True))
    second_mean = lax.optimization_barrier(jnp.mean(d_unit * unit_field, -1, keepdims=True))
    return inv_scale * (d_unit - first_mean - unit_field * second_mean)

def region_of(coords, count):
    return jnp.where(coords < count - WIN, 0, jnp.where(coords < count - WIN // 2, 1, 2)).astype(jnp.int32)

def split_heads(rows):
    return rows.reshape(rows.shape[:-1] + (HEADS, HEAD_DIM))

def merge_heads(rows):
    return rows.reshape(rows.shape[:-2] + (HEADS * HEAD_DIM,))

def attend(queries, key_rows, value_rows, same_label, upstream_att):
    scaling = HEAD_DIM ** (-0.5)
    allowed = jnp.expand_dims(same_label, -3)
    queries = queries.astype(jnp.float32)
    key_rows = key_rows.astype(jnp.float32)
    value_rows = value_rows.astype(jnp.float32)
    upstream_att = upstream_att.astype(jnp.float32)
    scores = jnp.einsum('...qhd,...khd->...hqk', queries, key_rows) * scaling
    scores = jnp.where(allowed, scores, -1e+30)
    highest = lax.optimization_barrier(jnp.max(scores, -1, keepdims=True))
    weights = jnp.where(allowed, jnp.exp(scores - highest), 0.0)
    attention = weights / lax.optimization_barrier(jnp.sum(weights, -1, keepdims=True))
    attention_low = attention.astype(jnp.bfloat16).astype(jnp.float32)
    attended = jnp.einsum('...hqk,...khd->...qhd', attention_low, value_rows).astype(jnp.bfloat16)
    d_attention = jnp.einsum('...qhd,...khd->...hqk', upstream_att, value_rows)
    row_inner = lax.optimization_barrier(jnp.sum(attention * d_attention, -1, keepdims=True))
    d_scores = (attention * (d_attention - row_inner) * scaling).astype(jnp.bfloat16).astype(jnp.float32)
    d_query = jnp.einsum('...hqk,...khd->...qhd', d_scores, key_rows)
    d_key = jnp.einsum('...hqk,...qhd->...khd', d_scores, queries)
    d_value = jnp.einsum('...hqk,...qhd->...khd', attention_low, upstream_att)
    return (attended, d_query, d_key, d_value)

def to_windows(field_in):
    batches, z_cells, x_cells, y_cells, feature = field_in.shape
    split = field_in.reshape(batches, z_cells // WIN, WIN, x_cells // WIN, WIN, y_cells // WIN, WIN, feature)
    return split.transpose(0, 1, 3, 5, 2, 4, 6, 7).reshape(-1, WIN ** 3, feature)

def from_windows(blocks, grid):
    batches, z_cells, x_cells, y_cells = grid
    feature = blocks.shape[-1]
    split = blocks.reshape(batches, z_cells // WIN, x_cells // WIN, y_cells // WIN, WIN, WIN, WIN, feature)
    return split.transpose(0, 1, 4, 2, 5, 3, 6, 7).reshape(batches, z_cells, x_cells, y_cells, feature)

def reference(inputs, norm_params, w_qkv, w_proj, upstream):
    midway = WIN // 2
    channels = HEADS * HEAD_DIM
    grid = inputs.shape[:4]
    batches, z_cells, x_cells, y_cells = grid
    shifted = jnp.roll(inputs, (-midway, -midway, -midway), (1, 2, 3))
    rolled_up = jnp.roll(upstream, (-midway, -midway, -midway), (1, 2, 3))
    z_region = region_of(jnp.arange(z_cells, dtype=jnp.int32), z_cells)
    x_region = region_of(jnp.arange(x_cells, dtype=jnp.int32), x_cells)
    y_region = region_of(jnp.arange(y_cells, dtype=jnp.int32), y_cells)
    rolled_labels = 9 * z_region[:, None, None] + 3 * x_region[None, :, None] + y_region[None, None, :]
    unit_field, inv_scale, scaled = normalize(shifted, norm_params)
    normed = scaled.astype(jnp.bfloat16)
    flat_normed = normed.reshape(-1, channels)
    qkv = jnp.dot(flat_normed, w_qkv, preferred_element_type=jnp.float32).astype(jnp.bfloat16)
    flat_up = rolled_up.reshape(-1, channels)
    upstream_att = jnp.dot(flat_up, w_proj.T, preferred_element_type=jnp.float32).astype(jnp.bfloat16)
    qkv_windows = to_windows(qkv.reshape(grid + (3 * channels,)))
    att_windows = to_windows(upstream_att.reshape(grid + (channels,)))
    label_windows = to_windows(rolled_labels[None, :, :, :, None])[:, :, 0]
    label_windows = jnp.tile(label_windows, (batches, 1))

    def one_window(items):
        block, att_block, block_labels = items
        same_label = block_labels[:, None] == block_labels[None, :]
        queries = split_heads(block[:, :channels])
        key_rows = split_heads(block[:, channels:2 * channels])
        value_rows = split_heads(block[:, 2 * channels:])
        attended, d_query, d_key, d_value = attend(queries, key_rows, value_rows, same_label, split_heads(att_block))
        gradients = jnp.concatenate([merge_heads(d_query), merge_heads(d_key), merge_heads(d_value)], -1)
        return (merge_heads(attended), gradients)
    attended, d_qkv = lax.map(one_window, (qkv_windows, att_windows, label_windows))
    attended = from_windows(attended, grid).reshape(-1, channels)
    d_qkv = from_windows(d_qkv, grid).reshape(-1, 3 * channels)
    projected = jnp.dot(attended, w_proj, preferred_element_type=jnp.float32).astype(jnp.bfloat16)
    projected = projected.reshape(grid + (channels,))
    grad_proj = jnp.dot(attended.T, flat_up, preferred_element_type=jnp.float32)
    grad_qkv = jnp.dot(flat_normed.astype(jnp.float32).T, d_qkv, precision=lax.Precision.HIGHEST)
    d_normed = jnp.dot(d_qkv, w_qkv.astype(jnp.float32).T, precision=lax.Precision.HIGHEST)
    flat_unit = unit_field.reshape(-1, channels)
    flat_inv = inv_scale.reshape(-1, 1)
    grad_norm = jnp.stack([lax.optimization_barrier(jnp.sum(d_normed * flat_unit, 0)), lax.optimization_barrier(jnp.sum(d_normed, 0))])
    d_shifted = normalize_back(d_normed, flat_unit, flat_inv, norm_params).astype(jnp.bfloat16)
    d_shifted = d_shifted.reshape(grid + (channels,))
    back_proj = jnp.roll(projected, (midway, midway, midway), (1, 2, 3))
    back_grad = jnp.roll(d_shifted, (midway, midway, midway), (1, 2, 3))
    output = (inputs.astype(jnp.float32) + back_proj.astype(jnp.float32)).astype(jnp.bfloat16)
    grad_inputs = (upstream.astype(jnp.float32) + back_grad.astype(jnp.float32)).astype(jnp.bfloat16)
    return (output, grad_inputs, grad_qkv, grad_proj, grad_norm)
```

```python
import jax
import jax.numpy as jnp
from jax import lax
from jax.experimental import pallas as pl
from jax.experimental.pallas import tpu as pltpu
from jax.sharding import PartitionSpec as P

HEADS = 16
HEAD_DIM = 32
C = 512
WIN = 8
RING = 4
OWN = C // RING
SLAB = 128
TOKENS = RING * SLAB
BLOCK = 256
SCALE = HEAD_DIM**-0.5
LOG2E = 1.4426950408889634
F32 = jnp.float32
BF16 = jnp.bfloat16


def move(value, target):
    pairs = []
    for place in range(64):
        for column in range(4):
            to_place, to_column = target(place, column)
            pairs.append((place * 4 + column, (to_place % 64) * 4 + to_column % 4))
    return lax.ppermute(value, ("wide", "narrow"), pairs)


def partner_of(place):
    return place + 4 if (place // 4) % 2 else place - 4


def along_x(steps):
    return lambda p, n: (p // 4 * 4 + (p + steps) % 4, n)


def other_core(p, n):
    return (p, n ^ 1)


def plane_groups():
    return [
        [(16 * z + member) * 4 + column for member in range(16)]
        for z in range(4)
        for column in range(4)
    ]


def along_z(steps):
    return lambda p, n: (p + 16 * steps, n)


def other_z(p, n):
    return (p, n ^ 2)


def exchange(value, groups):
    return lax.all_to_all(value, ("wide", "narrow"), 0, 0, axis_index_groups=groups)


def dot(a, b):
    return lax.dot_general(a, b, (((1,), (0,)), ((), ())), preferred_element_type=F32)


def dot_nt(a, b):
    return lax.dot_general(a, b, (((1,), (1,)), ((), ())), preferred_element_type=F32)


def unit_of(rows):
    floats = rows.astype(F32)
    average = jnp.mean(floats, -1, keepdims=True)
    centered = floats - average
    variance = jnp.mean(centered * centered, -1, keepdims=True)
    inv_scale = lax.rsqrt(variance + 1e-05)
    return centered * inv_scale, inv_scale


def two_terms(value):
    high = value.astype(BF16)
    low = (value - high.astype(F32)).astype(BF16)
    return high, low


def own_columns(w_qkv, x):
    start = pl.multiple_of(OWN * x, OWN)
    return jnp.concatenate(
        [w_qkv[:, pl.ds(pl.multiple_of(start + C * third, OWN), OWN)] for third in range(3)], 1
    )


def project(parts, norm, w_qkv, w_proj, member):
    unit, _ = unit_of(jnp.concatenate([part[0] for part in parts], 0))
    normed = (unit * norm[0:1, :] + norm[1:2, :]).astype(BF16)
    qkv = dot(normed, own_columns(w_qkv, member)).astype(BF16)
    rows = w_proj[pl.ds(pl.multiple_of(OWN * member, OWN), OWN), :]
    cotangent = dot_nt(jnp.concatenate([part[1] for part in parts], 0), rows).astype(BF16)
    return normed, qkv, cotangent


def first_kernel(flags, p0, p1, p2, p3, norm, w_qkv, w_proj, normed_ref, qkv_ref, up_ref):
    normed_ref[...], qkv_ref[...], up_ref[...] = project(
        (p0, p1, p2, p3), norm, w_qkv, w_proj, flags[3]
    )


def attention_kernel(
    flags, p0, p1, p2, p3, normed0, qkv0, up0, norm, w_qkv, w_proj,
    r0, r1, r2, r3, dt_ref, at_ref, normed1,
):
    normed1[...], qkv1, up1 = project((p0, p1, p2, p3), norm, w_qkv, w_proj, flags[3])
    qkv = jnp.concatenate([qkv0[...], qkv1], 0)
    cotangent = jnp.concatenate([up0[...], up1], 0)
    queries = qkv[:, :OWN]
    keys = qkv[:, OWN : 2 * OWN]
    values = qkv[:, 2 * OWN :]
    queries_t = queries.T
    cotangent_t = cotangent.T
    keys_t = keys.T
    values_t = values.T
    head_of_lane = lax.broadcasted_iota(jnp.int32, (TOKENS, OWN), 1) // HEAD_DIM

    def label(shape, dim):
        token = lax.broadcasted_iota(jnp.int32, shape, dim)
        row = token // 256
        half = (token // 32) % 2
        low_y = (token // 4) % 2
        return row * flags[0] + half * flags[1] + low_y * flags[2]

    key_label = label((TOKENS, 1), 0)
    query_label = label((1, TOKENS), 1)
    d_key = jnp.zeros((TOKENS, OWN), F32)
    d_value = jnp.zeros((TOKENS, OWN), F32)
    for block in range(TOKENS // BLOCK):
        span = slice(block * BLOCK, (block + 1) * BLOCK)
        allowed = key_label == query_label[:, span]
        for head in range(RING):
            chosen = head_of_lane == head
            rows = slice(head * HEAD_DIM, (head + 1) * HEAD_DIM)
            key_head = jnp.where(chosen, keys, jnp.zeros_like(keys))
            value_head = jnp.where(chosen, values, jnp.zeros_like(values))
            scores = jnp.where(allowed, dot(key_head, queries_t[:, span]), -1e30)
            highest = jnp.max(scores, 0, keepdims=True)
            weights = jnp.exp2((scores - highest) * (SCALE * LOG2E))
            probs = weights * (1.0 / jnp.sum(weights, 0, keepdims=True))
            probs_low = probs.astype(BF16)
            d_probs = dot(value_head, cotangent_t[:, span])
            inner = jnp.sum(probs * d_probs, 0, keepdims=True)
            d_scores = (probs * ((d_probs - inner) * SCALE)).astype(BF16)
            at_ref[rows, span] = dot(values_t[rows], probs_low).astype(BF16)
            dt_ref[rows, span] = dot(keys_t[rows], d_scores)
            query_head = jnp.where(chosen[span], queries[span], jnp.zeros_like(queries[span]))
            cotangent_head = jnp.where(
                chosen[span], cotangent[span], jnp.zeros_like(cotangent[span])
            )
            d_key += dot(d_scores, query_head)
            d_value += dot(probs_low, cotangent_head)
    dt_ref[OWN : 2 * OWN, :] = d_key.T
    dt_ref[2 * OWN :, :] = d_value.T
    d_query = dt_ref[:OWN, :].T.astype(BF16)
    attended = at_ref[...].T
    for member, r_ref in enumerate((r0, r1, r2, r3)):
        for part in range(2):
            rows = slice(256 * part + 64 * member, 256 * part + 64 * member + 64)
            to = slice(64 * part, 64 * part + 64)
            r_ref[to, :OWN] = d_query[rows]
            r_ref[to, OWN : 2 * OWN] = d_key[rows].astype(BF16)
            r_ref[to, 2 * OWN : 3 * OWN] = d_value[rows].astype(BF16)
            r_ref[to, 3 * OWN :] = attended[rows]


def gradient_kernel(
    spot, p0, p1, p2, p3, p4, p5, p6, p7, dt_ref, at_ref, normed0, normed1, w_qkv,
    keep, send, g_ref, p_ref, n_ref,
):
    x, core = spot[0], spot[2]
    parts = (p0, p1, p2, p3, p4, p5, p6, p7)
    d_high, d_low = two_terms(dt_ref[...])
    normed = jnp.concatenate([normed0[...], normed1[...]], 0)
    g_ref[...] = dot(d_high, normed) + dot(d_low, normed)
    columns = own_columns(w_qkv, x)
    gain_row = jnp.zeros((1, C), F32)
    offset_row = jnp.zeros((1, C), F32)
    for piece in range(4):
        rows = jnp.concatenate([parts[2 * piece][0], parts[2 * piece + 1][0]], 0)
        high, low = two_terms(dt_ref[:, piece * SLAB : (piece + 1) * SLAB].T)
        d_normed = dot_nt(high, columns) + dot_nt(low, columns)
        gain_row += jnp.sum(d_normed * unit_of(rows)[0], 0, keepdims=True)
        offset_row += jnp.sum(d_normed, 0, keepdims=True)
    p_ref[...] = dot(at_ref[...], jnp.concatenate([part[1] for part in parts], 0)).T
    row = lax.broadcasted_iota(jnp.int32, (128, C), 0)
    n_ref[...] = jnp.where(row == 0, gain_row, jnp.where(row == 1, offset_row, 0.0)).T
    for ahead, out in ((0, keep), (1, send)):
        to_core = core if ahead == 0 else 1 - core
        wide_lanes = pl.ds(pl.multiple_of(256 * to_core, 256), 256)
        for to_y in range(4):
            for to_x in range(4):
                member = 4 * to_y + to_x
                for slot in range(3):
                    residue = 12 * to_y + 3 * to_x + slot
                    third_of = lax.rem(residue // 16 - x + 6, 3)
                    start = pl.multiple_of(128 * third_of + 8 * (residue % 16), 8)
                    out[member, 8 * slot : 8 * slot + 8, :] = g_ref[pl.ds(start, 8), wide_lanes]
                for z in range(4):
                    rows = slice(128 * z + 8 * member, 128 * z + 8 * member + 8)
                    lanes = slice(64 * z, 64 * z + 64)
                    piece = p_ref[rows, :]
                    out[member, 24:32, lanes] = jnp.where(
                        to_core == 0, piece[:, :64], piece[:, 64:]
                    )
                    out[member, 32:40, lanes] = n_ref[rows, :64]


def z_parts_kernel(spot, pieces, *outs):
    x, y, z = spot[0], spot[1], spot[3]
    members = [
        (pieces[j] + pieces[4 + j]) + (pieces[8 + j] + pieces[12 + j]) for j in range(4)
    ]
    total = (members[0] + members[1]) + (members[2] + members[3])
    for to_z in range(4):
        block = []
        for slot in range(3):
            rows = slice(8 * slot, 8 * slot + 8)
            owner = lax.rem(48 * to_z + 12 * y + 3 * x + slot, 64) // 16
            picked = members[0][rows]
            for j in range(1, 4):
                picked = jnp.where(owner == j, members[j][rows], picked)
            block.append(picked)
        lanes = slice(64 * to_z, 64 * to_z + 64)
        block.append(jnp.concatenate([part[24:32, lanes] for part in members], 1))
        block.append(jnp.concatenate([total[32:40, lanes], jnp.zeros((8, 192), F32)], 1))
        block = jnp.concatenate(block, 0)
        outs[0][...] = jnp.where(z == to_z, block, outs[0][...]) if to_z else block
        for steps in range(1, 4):
            ahead = lax.rem(to_z - z + 4, 4) == steps
            outs[steps][...] = jnp.where(ahead, block, outs[steps][...]) if to_z else block


def last_kernel(spot, mine, theirs, g_out, p_out, n_out):
    swap = spot[2] == 1
    low = jnp.where(swap, theirs[...], mine[...])
    high = jnp.where(swap, mine[...], theirs[...])
    g_out[:, :256] = low[:24]
    g_out[:, 256:] = high[:24]
    for member in range(4):
        lanes = slice(64 * member, 64 * member + 64)
        p_out[:, 128 * member : 128 * member + 128] = jnp.concatenate(
            [low[24:32, lanes], high[24:32, lanes]], 1
        )
    n_out[...] = low[32:40, :128].T[:2]


def token_kernel(spot, own0, own1, r0, r1, r2, r3, w_qkv, w_proj, norm, out):
    x = spot[0]
    projected = jnp.zeros((SLAB, C), F32)
    d_normed = jnp.zeros((SLAB, C), F32)
    for r_ref, steps in ((r0, 0), (r1, 3), (r2, 1), (r3, 2)):
        member = lax.rem(x + steps, 4)
        start = pl.multiple_of(OWN * member, OWN)
        projected += dot(r_ref[:, 3 * OWN :], w_proj[pl.ds(start, OWN), :])
        for third in range(3):
            lanes = slice(third * OWN, (third + 1) * OWN)
            columns = w_qkv[:, pl.ds(pl.multiple_of(start + C * third, OWN), OWN)]
            d_normed += dot_nt(r_ref[:, lanes], columns)
    out[0] = projected.astype(BF16)
    unit, inv_scale = unit_of(jnp.concatenate([own0[0], own1[0]], 0))
    d_unit = d_normed * norm[0:1, :]
    first_mean = jnp.mean(d_unit, -1, keepdims=True)
    second_mean = jnp.mean(d_unit * unit, -1, keepdims=True)
    out[1] = (inv_scale * (d_unit - first_mean - unit * second_mean)).astype(BF16)


def call(kernel, scalars, arrays, outs, scratch=(), flops=0, moved=0, room=8):
    smem = pl.BlockSpec(memory_space=pltpu.SMEM)
    vmem = pl.BlockSpec(memory_space=pltpu.VMEM)
    return pl.pallas_call(
        kernel,
        out_shape=[jax.ShapeDtypeStruct(shape, dtype) for shape, dtype in outs],
        in_specs=[smem] + [vmem] * len(arrays),
        out_specs=[vmem] * len(outs),
        scratch_shapes=list(scratch),
        compiler_params=pltpu.CompilerParams(vmem_limit_bytes=room * 2**20),
        cost_estimate=pl.CostEstimate(flops=flops, bytes_accessed=moved, transcendentals=0),
        name=kernel.__name__,
    )(scalars, *arrays)


def on_device(inputs, norm_params, w_qkv, w_proj, upstream):
    place = lax.axis_index("wide")
    column = lax.axis_index("narrow")
    x, y, z = place % 4, place // 4 % 4, place // 16
    core = column % 2
    row = 1 - y % 2
    window = (place - 4) % 64 // 8
    spot = jnp.stack([x, y, core, z]).astype(jnp.int32)
    flags = jnp.stack([4 * (window == 7), 2 * (column == 3), row, x]).astype(jnp.int32)

    upper_y = (jnp.arange(8)[:, None] < 4) != (row == 1)
    both = jnp.stack([inputs[0, 0], upstream[0, 0]]).reshape(2, 8, 2, 8, C)
    other = jnp.where(upper_y, both[:, :, 0], both[:, :, 1])
    other_in = move(other[:, 4:], lambda p, n: (partner_of(p), n))
    cross_in = move(other[:, :4], lambda p, n: (partner_of(p), n - 1))
    both, other = lax.optimization_barrier((both, other))
    mine = jnp.where(upper_y, both[:, :, 1], both[:, :, 0])
    lower_in = move(mine[:, :4], lambda p, n: (p, n - 1))

    part0 = jnp.stack([mine[:, 4:], lower_in], 1).reshape(2, SLAB // 2, C)
    parts0 = [part0] + [move(part0, along_x(steps)) for steps in (1, -1, 2)]
    part1 = jnp.stack([other_in, cross_in], 1).reshape(2, SLAB // 2, C)
    parts1 = [part1] + [move(part1, along_x(steps)) for steps in (1, -1, 2)]
    half = TOKENS // 2
    normed0, qkv0, up0 = call(
        first_kernel,
        flags,
        (*parts0, norm_params, w_qkv, w_proj),
        [((half, C), BF16), ((half, 3 * OWN), BF16), ((half, OWN), BF16)],
        flops=10_000_000_000,
        moved=3_000_000,
    )
    r_own, r_left, r_right, r_far, d_t, a_t, normed1 = call(
        attention_kernel,
        flags,
        (*parts1, normed0, qkv0, up0, norm_params, w_qkv, w_proj),
        [((SLAB, C), BF16)] * 4
        + [((3 * OWN, TOKENS), F32), ((OWN, TOKENS), BF16), ((half, C), BF16)],
        flops=1_200_000_000,
        moved=6_000_000,
    )

    from_right = move(r_left, along_x(-1))
    from_left = move(r_right, along_x(1))
    from_far = move(r_far, along_x(2))
    keep, send = call(
        gradient_kernel,
        spot,
        (*parts0, *parts1, d_t, a_t, normed0, normed1, w_qkv),
        [((16, 40, 256), F32)] * 2,
        scratch=[
            pltpu.VMEM((3 * OWN, C), F32),
            pltpu.VMEM((C, OWN), F32),
            pltpu.VMEM((C, 128), F32),
        ],
        flops=20_000_000_000,
        moved=6_000_000,
    )
    send, from_left, from_right = lax.optimization_barrier((send, from_left, from_right))
    halves, from_far = lax.optimization_barrier((keep + move(send, other_core), from_far))
    plane = exchange(halves, plane_groups())
    (back,) = call(
        token_kernel,
        spot,
        (part0, part1, r_own, from_left, from_right, from_far, w_qkv, w_proj, norm_params),
        [((2, SLAB, C), BF16)],
        flops=500_000_000,
        moved=4_000_000,
    )
    back = back.reshape(2, 4, 4, 8, C)
    lower = move(back[:, 1], lambda p, n: (p, n + 1))
    other_upper = move(back[:, 2], lambda p, n: (partner_of(p), n))
    other_lower = move(back[:, 3], lambda p, n: (partner_of(p), n + 1))

    z_parts = call(z_parts_kernel, spot, (plane,), [((40, 256), F32)] * 4)
    line = [z_parts[0]] + [move(z_parts[steps], along_z(steps)) for steps in (1, 2, 3)]
    line = (line[0] + line[1]) + (line[2] + line[3])
    share = line + move(line, other_z)
    grad_qkv, grad_proj, grad_norm = call(
        last_kernel,
        spot,
        (share, move(share, other_core)),
        [((24, C), F32), ((8, C), F32), ((2, 8), F32)],
    )

    own_full = jnp.concatenate([lower, back[:, 0]], 1)
    other_full = jnp.concatenate([other_lower, other_upper], 1)
    first = jnp.where(upper_y, other_full, own_full)
    second = jnp.where(upper_y, own_full, other_full)
    added = jnp.stack([first, second], 2).reshape(2, 8, 16, C).astype(F32)
    output = (inputs.astype(F32) + added[0]).astype(BF16)
    grad_inputs = (upstream.astype(F32) + added[1]).astype(BF16)
    return (output, grad_inputs, grad_qkv.T, grad_proj.T, grad_norm)


def solution(mesh):
    in_specs = (
        P(None, "wide", "narrow", None, None),
        P(),
        P(),
        P(),
        P(None, "wide", "narrow", None, None),
    )
    out_specs = (
        P(None, "wide", "narrow", None, None),
        P(None, "wide", "narrow", None, None),
        P(None, "wide"),
        P(None, "wide"),
        P(None, "wide"),
    )
    return jax.shard_map(
        on_device, mesh=mesh, in_specs=in_specs, out_specs=out_specs, check_vma=False
    )
```

```python
import jax
import jax.numpy as jnp
from jax import lax
from jax.experimental import pallas as pl
from jax.experimental.pallas import tpu as pltpu
from jax.sharding import PartitionSpec as P

HEADS = 16
HEAD_DIM = 32
C = 512
WIN = 8
RING = 4
OWN = C // RING
SLAB = 128
TOKENS = RING * SLAB
BLOCK = 256
CHUNK = 64
SCALE = HEAD_DIM**-0.5
LOG2E = 1.4426950408889634
F32 = jnp.float32
BF16 = jnp.bfloat16


def move(value, target):
    pairs = []
    for place in range(64):
        for column in range(4):
            to_place, to_column = target(place, column)
            pairs.append((place * 4 + column, (to_place % 64) * 4 + to_column % 4))
    return lax.ppermute(value, ("wide", "narrow"), pairs)


def partner_of(place):
    return place + 4 if (place // 4) % 2 else place - 4


def along_x(steps):
    return lambda p, n: (p // 4 * 4 + (p + steps) % 4, n)


def other_core(p, n):
    return (p, n ^ 1)


def plane_groups():
    return [
        [(16 * z + member) * 4 + column for member in range(16)]
        for z in range(4)
        for column in range(4)
    ]


def along_z(steps):
    return lambda p, n: (p + 16 * steps, n)


def other_z(p, n):
    return (p, n ^ 2)


def other_both(p, n):
    return (p, n ^ 3)


def exchange(value, groups):
    return lax.all_to_all(value, ("wide", "narrow"), 0, 0, axis_index_groups=groups)


def dot(a, b):
    return lax.dot_general(a, b, (((1,), (0,)), ((), ())), preferred_element_type=F32)


def dot_nt(a, b):
    return lax.dot_general(a, b, (((1,), (1,)), ((), ())), preferred_element_type=F32)


def unit_of(rows):
    floats = rows.astype(F32)
    average = jnp.mean(floats, -1, keepdims=True)
    centered = floats - average
    variance = jnp.mean(centered * centered, -1, keepdims=True)
    inv_scale = lax.rsqrt(variance + 1e-05)
    return centered * inv_scale, inv_scale


def two_terms(value):
    high = value.astype(BF16)
    low = (value - high.astype(F32)).astype(BF16)
    return high, low


def own_columns(w_qkv, x):
    start = pl.multiple_of(OWN * x, OWN)
    return jnp.concatenate(
        [w_qkv[:, pl.ds(pl.multiple_of(start + C * third, OWN), OWN)] for third in range(3)], 1
    )


def project(parts, norm, w_qkv, w_proj, member):
    unit, _ = unit_of(jnp.concatenate([part[0] for part in parts], 0))
    normed = (unit * norm[0:1, :] + norm[1:2, :]).astype(BF16)
    qkv = dot(normed, own_columns(w_qkv, member)).astype(BF16)
    rows = w_proj[pl.ds(pl.multiple_of(OWN * member, OWN), OWN), :]
    cotangent = dot_nt(jnp.concatenate([part[1] for part in parts], 0), rows).astype(BF16)
    return normed, qkv, cotangent


def first_kernel(flags, p0, p1, p2, p3, norm, w_qkv, w_proj, normed_ref, qkv_ref, up_ref):
    normed_ref[...], qkv_ref[...], up_ref[...] = project(
        (p0, p1, p2, p3), norm, w_qkv, w_proj, flags[3]
    )


def attention_kernel(
    flags, p0, p1, p2, p3, normed0, qkv0, up0, norm, w_qkv, w_proj,
    r0, r1, r2, r3, dt_ref, at_ref, normed1,
):
    normed1[...], qkv1, up1 = project((p0, p1, p2, p3), norm, w_qkv, w_proj, flags[3])
    qkv = jnp.concatenate([qkv0[...], qkv1], 0)
    cotangent = jnp.concatenate([up0[...], up1], 0)
    queries = qkv[:, :OWN]
    keys = qkv[:, OWN : 2 * OWN]
    values = qkv[:, 2 * OWN :]
    queries_t = queries.T
    cotangent_t = cotangent.T
    keys_t = keys.T
    values_t = values.T
    head_of_lane = lax.broadcasted_iota(jnp.int32, (TOKENS, OWN), 1) // HEAD_DIM

    def label(shape, dim):
        token = lax.broadcasted_iota(jnp.int32, shape, dim)
        row = token // 256
        half = (token // 32) % 2
        low_y = (token // 4) % 2
        return row * flags[0] + half * flags[1] + low_y * flags[2]

    key_label = label((TOKENS, 1), 0)
    query_label = label((1, TOKENS), 1)
    d_key = jnp.zeros((TOKENS, OWN), F32)
    d_value = jnp.zeros((TOKENS, OWN), F32)
    for block in range(TOKENS // BLOCK):
        span = slice(block * BLOCK, (block + 1) * BLOCK)
        allowed = key_label == query_label[:, span]
        for head in range(RING):
            chosen = head_of_lane == head
            rows = slice(head * HEAD_DIM, (head + 1) * HEAD_DIM)
            key_head = jnp.where(chosen, keys, jnp.zeros_like(keys))
            value_head = jnp.where(chosen, values, jnp.zeros_like(values))
            scores = jnp.where(allowed, dot(key_head, queries_t[:, span]), -1e30)
            highest = jnp.max(scores, 0, keepdims=True)
            d_probs = dot(value_head, cotangent_t[:, span])
            weights = []
            total = jnp.zeros((8, BLOCK), F32)
            inner = jnp.zeros((8, BLOCK), F32)
            for start in range(0, TOKENS, CHUNK):
                part = slice(start, start + CHUNK)
                weight = jnp.exp2((scores[part] - highest) * (SCALE * LOG2E))
                total += jnp.sum(weight.reshape(CHUNK // 8, 8, BLOCK), 0)
                inner += jnp.sum((weight * d_probs[part]).reshape(CHUNK // 8, 8, BLOCK), 0)
                weights.append(weight)
            over = 1.0 / jnp.sum(total, 0, keepdims=True)
            inner = jnp.sum(inner, 0, keepdims=True) * over
            over_scaled = over * SCALE
            probs_low, d_scores = [], []
            for index, weight in enumerate(weights):
                part = slice(index * CHUNK, (index + 1) * CHUNK)
                probs_low.append((weight * over).astype(BF16))
                d_scores.append(((weight * over_scaled) * (d_probs[part] - inner)).astype(BF16))
            probs_low = jnp.concatenate(probs_low, 0)
            d_scores = jnp.concatenate(d_scores, 0)
            at_ref[rows, span] = dot(values_t[rows], probs_low).astype(BF16)
            dt_ref[rows, span] = dot(keys_t[rows], d_scores)
            query_head = jnp.where(chosen[span], queries[span], jnp.zeros_like(queries[span]))
            cotangent_head = jnp.where(
                chosen[span], cotangent[span], jnp.zeros_like(cotangent[span])
            )
            d_key += dot(d_scores, query_head)
            d_value += dot(probs_low, cotangent_head)
    dt_ref[OWN : 2 * OWN, :] = d_key.T
    dt_ref[2 * OWN :, :] = d_value.T
    d_query = dt_ref[:OWN, :].T.astype(BF16)
    attended = at_ref[...].T
    for member, r_ref in enumerate((r0, r1, r2, r3)):
        for part in range(2):
            rows = slice(256 * part + 64 * member, 256 * part + 64 * member + 64)
            to = slice(64 * part, 64 * part + 64)
            r_ref[to, :OWN] = d_query[rows]
            r_ref[to, OWN : 2 * OWN] = d_key[rows].astype(BF16)
            r_ref[to, 2 * OWN : 3 * OWN] = d_value[rows].astype(BF16)
            r_ref[to, 3 * OWN :] = attended[rows]


def gradient_kernel(
    spot, p0, p1, p2, p3, p4, p5, p6, p7, dt_ref, at_ref, normed0, normed1,
    keep, send, g_ref, p_ref,
):
    x, core = spot[0], spot[2]
    parts = (p0, p1, p2, p3, p4, p5, p6, p7)
    d_high, d_low = two_terms(dt_ref[...])
    normed = jnp.concatenate([normed0[...], normed1[...]], 0)
    g_ref[...] = dot(d_high, normed) + dot(d_low, normed)
    p_ref[...] = dot(at_ref[...], jnp.concatenate([part[1] for part in parts], 0)).T
    for ahead, out in ((0, keep), (1, send)):
        to_core = core if ahead == 0 else 1 - core
        for member in range(16):
            for side in range(2):
                lanes = pl.ds(pl.multiple_of(256 * to_core + 128 * side, 128), 128)
                for slot in range(3):
                    residue = 3 * member + slot
                    third_of = lax.rem(residue // 16 - x + 6, 3)
                    start = pl.multiple_of(128 * third_of + 8 * (residue % 16), 8)
                    top = 24 * side + 8 * slot
                    out[member, top : top + 8, :] = g_ref[pl.ds(start, 8), lanes]
            for z in range(4):
                rows = slice(128 * z + 8 * member, 128 * z + 8 * member + 8)
                piece = p_ref[rows, :]
                top = 48 + 8 * (z // 2)
                out[member, top : top + 8, 64 * (z % 2) : 64 * (z % 2) + 64] = jnp.where(
                    to_core == 0, piece[:, :64], piece[:, 64:]
                )


def norm_kernel(
    spot, p0, p1, p2, p3, p4, p5, p6, p7, r0, r1, r2, r3, w_qkv, out, n_ref
):
    parts = (p0, p1, p2, p3, p4, p5, p6, p7)
    columns = own_columns(w_qkv, spot[0])
    gain_row = jnp.zeros((1, C), F32)
    offset_row = jnp.zeros((1, C), F32)
    for member, r_ref in enumerate((r0, r1, r2, r3)):
        rows = jnp.concatenate([parts[member][0], parts[4 + member][0]], 0)
        d_normed = dot_nt(r_ref[:, : 3 * OWN], columns)
        gain_row += jnp.sum(d_normed * unit_of(rows)[0], 0, keepdims=True)
        offset_row += jnp.sum(d_normed, 0, keepdims=True)
    row = lax.broadcasted_iota(jnp.int32, (128, C), 0)
    n_ref[...] = jnp.where(row == 0, gain_row, jnp.where(row == 1, offset_row, 0.0)).T
    for member in range(16):
        for z in range(4):
            rows = slice(128 * z + 8 * member, 128 * z + 8 * member + 8)
            out[member, :, 32 * z : 32 * z + 32] = n_ref[rows, :32]


def join_kernel(spot, keep, received, norms, out):
    out[:, :64, :] = keep[...] + received[...]
    out[:, 64:, :] = norms[...]


def z_parts_kernel(spot, pieces, *outs):
    x, y, z = spot[0], spot[1], spot[3]
    members = [
        (pieces[j] + pieces[4 + j]) + (pieces[8 + j] + pieces[12 + j]) for j in range(4)
    ]
    total = (members[0][64:] + members[1][64:]) + (members[2][64:] + members[3][64:])
    for to_z in range(4):
        block = []
        for side in range(2):
            for slot in range(3):
                rows = slice(24 * side + 8 * slot, 24 * side + 8 * slot + 8)
                owner = lax.rem(48 * to_z + 12 * y + 3 * x + slot, 64) // 16
                picked = members[0][rows]
                for j in range(1, 4):
                    picked = jnp.where(owner == j, members[j][rows], picked)
                block.append(picked)
        rows = slice(48 + 8 * (to_z // 2), 56 + 8 * (to_z // 2))
        lanes = slice(64 * (to_z % 2), 64 * (to_z % 2) + 64)
        for pair in range(2):
            block.append(
                jnp.concatenate([members[2 * pair + j][rows, lanes] for j in range(2)], 1)
            )
        lanes = slice(32 * to_z, 32 * to_z + 32)
        block.append(jnp.concatenate([total[:, lanes], jnp.zeros((8, 96), F32)], 1))
        block = jnp.concatenate(block, 0)
        for steps in range(4):
            ahead = lax.rem(to_z - z + 4, 4) == steps
            outs[steps][...] = jnp.where(ahead, block, outs[steps][...]) if to_z else block


def last_kernel(spot, near, core_in, z_in, both_in, g_out, p_out, n_out):
    mine = near[...] + z_in[...]
    theirs = core_in[...] + both_in[...]
    swap = spot[2] == 1
    shares = (jnp.where(swap, theirs, mine), jnp.where(swap, mine, theirs))
    for core in range(2):
        for side in range(2):
            lanes = slice(256 * core + 128 * side, 256 * core + 128 * side + 128)
            g_out[:, lanes] = shares[core][24 * side : 24 * side + 24]
    for member in range(4):
        rows = slice(48 + 8 * (member // 2), 56 + 8 * (member // 2))
        lanes = slice(64 * (member % 2), 64 * (member % 2) + 64)
        p_out[:, 128 * member : 128 * member + 128] = jnp.concatenate(
            [share[rows, lanes] for share in shares], 1
        )
    n_out[...] = (mine[64:] + theirs[64:]).T[:2]


def upper_rows(row):
    return (lax.broadcasted_iota(jnp.int32, (4, 8, C), 1) < 4) != (row == 1)


def merge_kernel(
    spot, inputs, upstream, mine_high, mine_low, other_high, other_low, output, grad_inputs
):
    upper = upper_rows(spot[4])
    for array, (source, out) in enumerate(((inputs, output), (upstream, grad_inputs))):
        for start, other, mine in ((4, other_high, mine_high), (0, other_low, mine_low)):
            rows = source[start : start + 4].astype(F32)
            from_other = other[array].astype(F32)
            from_mine = mine[array].astype(F32)
            first = rows[:, :8] + jnp.where(upper, from_other, from_mine)
            second = rows[:, 8:] + jnp.where(upper, from_mine, from_other)
            out[start : start + 4] = jnp.concatenate([first, second], 1).astype(BF16)


def token_kernel(spot, own0, own1, r0, r1, r2, r3, w_qkv, w_proj, norm, out):
    x = spot[0]
    projected = jnp.zeros((SLAB, C), F32)
    d_normed = jnp.zeros((SLAB, C), F32)
    for r_ref, steps in ((r0, 0), (r1, 3), (r2, 1), (r3, 2)):
        member = lax.rem(x + steps, 4)
        start = pl.multiple_of(OWN * member, OWN)
        projected += dot(r_ref[:, 3 * OWN :], w_proj[pl.ds(start, OWN), :])
        for third in range(3):
            lanes = slice(third * OWN, (third + 1) * OWN)
            columns = w_qkv[:, pl.ds(pl.multiple_of(start + C * third, OWN), OWN)]
            d_normed += dot_nt(r_ref[:, lanes], columns)
    out[0] = projected.astype(BF16)
    unit, inv_scale = unit_of(jnp.concatenate([own0[0], own1[0]], 0))
    d_unit = d_normed * norm[0:1, :]
    first_mean = jnp.mean(d_unit, -1, keepdims=True)
    second_mean = jnp.mean(d_unit * unit, -1, keepdims=True)
    out[1] = (inv_scale * (d_unit - first_mean - unit * second_mean)).astype(BF16)


def call(kernel, scalars, arrays, outs, scratch=(), flops=0, moved=0, fetched=0):
    smem = pl.BlockSpec(memory_space=pltpu.SMEM)
    vmem = pl.BlockSpec(memory_space=pltpu.VMEM)
    return pl.pallas_call(
        kernel,
        out_shape=[jax.ShapeDtypeStruct(shape, dtype) for shape, dtype in outs],
        in_specs=[smem] + [pl.BlockSpec()] * fetched + [vmem] * (len(arrays) - fetched),
        out_specs=[vmem] * len(outs),
        scratch_shapes=list(scratch),
        compiler_params=pltpu.CompilerParams(vmem_limit_bytes=8 * 2**20),
        cost_estimate=pl.CostEstimate(flops=flops, bytes_accessed=moved, transcendentals=0),
        name=kernel.__name__,
    )(scalars, *arrays)


def on_device(inputs, norm_params, w_qkv, w_proj, upstream):
    place = lax.axis_index("wide")
    column = lax.axis_index("narrow")
    x, y, z = place % 4, place // 4 % 4, place // 16
    core = column % 2
    row = 1 - y % 2
    window = (place - 4) % 64 // 8
    spot = jnp.stack([x, y, core, z, row]).astype(jnp.int32)
    flags = jnp.stack([4 * (window == 7), 2 * (column == 3), row, x]).astype(jnp.int32)

    own_inputs, own_upstream = inputs[0, 0], upstream[0, 0]
    upper_y = (jnp.arange(8)[:, None] < 4) != (row == 1)
    both = jnp.stack([own_inputs, own_upstream]).reshape(2, 8, 2, 8, C)
    mine = jnp.where(upper_y, both[:, :, 1], both[:, :, 0])
    other = jnp.where(upper_y, both[:, :, 0], both[:, :, 1])
    lower_in = move(mine[:, :4], lambda p, n: (p, n - 1))
    other_in = move(other[:, 4:], lambda p, n: (partner_of(p), n))
    cross_in = move(other[:, :4], lambda p, n: (partner_of(p), n - 1))

    part0 = jnp.stack([mine[:, 4:], lower_in], 1).reshape(2, SLAB // 2, C)
    parts0 = [part0] + [move(part0, along_x(steps)) for steps in (1, -1, 2)]
    part1 = jnp.stack([other_in, cross_in], 1).reshape(2, SLAB // 2, C)
    parts1 = [part1] + [move(part1, along_x(steps)) for steps in (1, -1, 2)]
    half = TOKENS // 2
    normed0, qkv0, up0 = call(
        first_kernel,
        flags,
        (*parts0, norm_params, w_qkv, w_proj),
        [((half, C), BF16), ((half, 3 * OWN), BF16), ((half, OWN), BF16)],
        flops=10_000_000_000,
        moved=3_000_000,
    )
    r_own, r_left, r_right, r_far, d_t, a_t, normed1 = call(
        attention_kernel,
        flags,
        (*parts1, normed0, qkv0, up0, norm_params, w_qkv, w_proj),
        [((SLAB, C), BF16)] * 4
        + [((3 * OWN, TOKENS), F32), ((OWN, TOKENS), BF16), ((half, C), BF16)],
        flops=1_200_000_000,
        moved=6_000_000,
    )

    from_right = move(r_left, along_x(-1))
    from_left = move(r_right, along_x(1))
    from_far = move(r_far, along_x(2))
    keep, send = call(
        gradient_kernel,
        spot,
        (*parts0, *parts1, d_t, a_t, normed0, normed1),
        [((16, 64, 128), F32)] * 2,
        scratch=[pltpu.VMEM((3 * OWN, C), F32), pltpu.VMEM((C, OWN), F32)],
        flops=20_000_000_000,
        moved=6_000_000,
    )
    send, from_left, from_right, from_far = lax.optimization_barrier(
        (send, from_left, from_right, from_far)
    )
    received = move(send, other_core)
    (back,) = call(
        token_kernel,
        spot,
        (part0, part1, r_own, from_left, from_right, from_far, w_qkv, w_proj, norm_params),
        [((2, SLAB, C), BF16)],
        flops=500_000_000,
        moved=4_000_000,
    )
    back, r_far = lax.optimization_barrier((back, r_far))
    (norms,) = call(
        norm_kernel,
        spot,
        (*parts0, *parts1, r_own, r_left, r_right, r_far, w_qkv),
        [((16, 8, 128), F32)],
        scratch=[pltpu.VMEM((C, 128), F32)],
        flops=1_000_000_000,
        moved=2_000_000,
    )
    (halves,) = call(join_kernel, spot, (keep, received, norms), [((16, 72, 128), F32)])
    halves, back = lax.optimization_barrier((halves, back))
    plane = exchange(halves, plane_groups())
    back = back.reshape(2, 4, 4, 8, C)
    lower = move(back[:, 1], lambda p, n: (p, n + 1))
    other_upper = move(back[:, 2], lambda p, n: (partner_of(p), n))
    other_lower = move(back[:, 3], lambda p, n: (partner_of(p), n + 1))

    z_parts = call(z_parts_kernel, spot, (plane,), [((72, 128), F32)] * 4)
    output, grad_inputs = call(
        merge_kernel,
        spot,
        (own_inputs, own_upstream, back[:, 0], lower, other_upper, other_lower),
        [((8, 16, C), BF16)] * 2,
        fetched=2,
    )
    line = [z_parts[0]] + [move(z_parts[steps], along_z(steps)) for steps in (1, 2, 3)]
    line[1], line[2], line[3], output, grad_inputs = lax.optimization_barrier(
        (line[1], line[2], line[3], output, grad_inputs)
    )
    line = (line[0] + line[1]) + (line[2] + line[3])
    grad_qkv, grad_proj, grad_norm = call(
        last_kernel,
        spot,
        (line, move(line, other_core), move(line, other_z), move(line, other_both)),
        [((24, C), F32), ((8, C), F32), ((2, 8), F32)],
    )
    return (
        output[None, None], grad_inputs[None, None], grad_qkv.T, grad_proj.T, grad_norm
    )


def solution(mesh):
    in_specs = (
        P(None, "wide", "narrow", None, None),
        P(),
        P(),
        P(),
        P(None, "wide", "narrow", None, None),
    )
    out_specs = (
        P(None, "wide", "narrow", None, None),
        P(None, "wide", "narrow", None, None),
        P(None, "wide"),
        P(None, "wide"),
        P(None, "wide"),
    )
    return jax.shard_map(
        on_device, mesh=mesh, in_specs=in_specs, out_specs=out_specs, check_vma=False
    )
```

```python
import jax
import jax.numpy as jnp
from jax import lax
from jax.experimental import pallas as pl
from jax.experimental.pallas import tpu as pltpu
from jax.sharding import PartitionSpec as P

HEADS = 16
HEAD_DIM = 32
C = 512
WIN = 8
RING = 4
OWN = C // RING
SLAB = 128
TOKENS = RING * SLAB
BLOCK = 256
CHUNK = 64
SCALE = HEAD_DIM**-0.5
LOG2E = 1.4426950408889634
F32 = jnp.float32
BF16 = jnp.bfloat16


def move(value, target):
    pairs = []
    for place in range(64):
        for column in range(4):
            to_place, to_column = target(place, column)
            pairs.append((place * 4 + column, (to_place % 64) * 4 + to_column % 4))
    return lax.ppermute(value, ("wide", "narrow"), pairs)


def partner_of(place):
    return place + 4 if (place // 4) % 2 else place - 4


def along_x(steps):
    return lambda p, n: (p // 4 * 4 + (p + steps) % 4, n)


def other_core(p, n):
    return (p, n ^ 1)


def plane_groups():
    return [
        [(16 * z + member) * 4 + column for member in range(16)]
        for z in range(4)
        for column in range(4)
    ]


def along_z(steps):
    return lambda p, n: (p + 16 * steps, n)


def other_z(p, n):
    return (p, n ^ 2)


def other_both(p, n):
    return (p, n ^ 3)


def exchange(value, groups):
    return lax.all_to_all(value, ("wide", "narrow"), 0, 0, axis_index_groups=groups)


def dot(a, b):
    return lax.dot_general(a, b, (((1,), (0,)), ((), ())), preferred_element_type=F32)


def dot_nt(a, b):
    return lax.dot_general(a, b, (((1,), (1,)), ((), ())), preferred_element_type=F32)


def unit_of(rows):
    floats = rows.astype(F32)
    average = jnp.mean(floats, -1, keepdims=True)
    centered = floats - average
    variance = jnp.mean(centered * centered, -1, keepdims=True)
    inv_scale = lax.rsqrt(variance + 1e-05)
    return centered * inv_scale, inv_scale


def two_terms(value):
    high = value.astype(BF16)
    low = (value - high.astype(F32)).astype(BF16)
    return high, low


def own_columns(w_qkv, x):
    start = pl.multiple_of(OWN * x, OWN)
    return jnp.concatenate(
        [w_qkv[:, pl.ds(pl.multiple_of(start + C * third, OWN), OWN)] for third in range(3)], 1
    )


def project(parts, norm, w_qkv, w_proj, member):
    unit, _ = unit_of(jnp.concatenate([part[0] for part in parts], 0))
    normed = (unit * norm[0:1, :] + norm[1:2, :]).astype(BF16)
    qkv = dot(normed, own_columns(w_qkv, member)).astype(BF16)
    rows = w_proj[pl.ds(pl.multiple_of(OWN * member, OWN), OWN), :]
    cotangent = dot_nt(jnp.concatenate([part[1] for part in parts], 0), rows).astype(BF16)
    return normed, qkv, cotangent


def first_kernel(flags, p0, p1, p2, p3, norm, w_qkv, w_proj, normed_ref, qkv_ref, up_ref):
    normed_ref[...], qkv_ref[...], up_ref[...] = project(
        (p0, p1, p2, p3), norm, w_qkv, w_proj, flags[3]
    )


def attention_kernel(
    flags, p0, p1, p2, p3, normed0, qkv0, up0, norm, w_qkv, w_proj,
    r0, r1, r2, r3, dt_ref, at_ref, normed1,
):
    normed1[...], qkv1, up1 = project((p0, p1, p2, p3), norm, w_qkv, w_proj, flags[3])
    qkv = jnp.concatenate([qkv0[...], qkv1], 0)
    cotangent = jnp.concatenate([up0[...], up1], 0)
    queries = qkv[:, :OWN]
    keys = qkv[:, OWN : 2 * OWN]
    values = qkv[:, 2 * OWN :]
    queries_t = queries.T
    cotangent_t = cotangent.T
    keys_t = keys.T
    values_t = values.T
    head_of_lane = lax.broadcasted_iota(jnp.int32, (TOKENS, OWN), 1) // HEAD_DIM

    def label(shape, dim):
        token = lax.broadcasted_iota(jnp.int32, shape, dim)
        row = token // 256
        half = (token // 32) % 2
        low_y = (token // 4) % 2
        return row * flags[0] + half * flags[1] + low_y * flags[2]

    key_label = label((TOKENS, 1), 0)
    query_label = label((1, TOKENS), 1)
    d_key = jnp.zeros((TOKENS, OWN), F32)
    d_value = jnp.zeros((TOKENS, OWN), F32)
    for block in range(TOKENS // BLOCK):
        span = slice(block * BLOCK, (block + 1) * BLOCK)
        allowed = key_label == query_label[:, span]
        for head in range(RING):
            chosen = head_of_lane == head
            rows = slice(head * HEAD_DIM, (head + 1) * HEAD_DIM)
            key_head = jnp.where(chosen, keys, jnp.zeros_like(keys))
            value_head = jnp.where(chosen, values, jnp.zeros_like(values))
            scores = jnp.where(allowed, dot(key_head, queries_t[:, span]), -1e30)
            highest = jnp.max(scores, 0, keepdims=True)
            d_probs = dot(value_head, cotangent_t[:, span])
            weights = []
            total = jnp.zeros((8, BLOCK), F32)
            inner = jnp.zeros((8, BLOCK), F32)
            for start in range(0, TOKENS, CHUNK):
                part = slice(start, start + CHUNK)
                weight = jnp.exp2((scores[part] - highest) * (SCALE * LOG2E))
                total += jnp.sum(weight.reshape(CHUNK // 8, 8, BLOCK), 0)
                inner += jnp.sum((weight * d_probs[part]).reshape(CHUNK // 8, 8, BLOCK), 0)
                weights.append(weight)
            over = 1.0 / jnp.sum(total, 0, keepdims=True)
            inner = jnp.sum(inner, 0, keepdims=True) * over
            over_scaled = over * SCALE
            probs_low, d_scores = [], []
            for index, weight in enumerate(weights):
                part = slice(index * CHUNK, (index + 1) * CHUNK)
                probs_low.append((weight * over).astype(BF16))
                d_scores.append(((weight * over_scaled) * (d_probs[part] - inner)).astype(BF16))
            probs_low = jnp.concatenate(probs_low, 0)
            d_scores = jnp.concatenate(d_scores, 0)
            at_ref[rows, span] = dot(values_t[rows], probs_low).astype(BF16)
            dt_ref[rows, span] = dot(keys_t[rows], d_scores)
            query_head = jnp.where(chosen[span], queries[span], jnp.zeros_like(queries[span]))
            cotangent_head = jnp.where(
                chosen[span], cotangent[span], jnp.zeros_like(cotangent[span])
            )
            d_key += dot(d_scores, query_head)
            d_value += dot(probs_low, cotangent_head)
    dt_ref[OWN : 2 * OWN, :] = d_key.T
    dt_ref[2 * OWN :, :] = d_value.T
    d_query = dt_ref[:OWN, :].T.astype(BF16)
    attended = at_ref[...].T
    for member, r_ref in enumerate((r0, r1, r2, r3)):
        for part in range(2):
            rows = slice(256 * part + 64 * member, 256 * part + 64 * member + 64)
            to = slice(64 * part, 64 * part + 64)
            r_ref[to, :OWN] = d_query[rows]
            r_ref[to, OWN : 2 * OWN] = d_key[rows].astype(BF16)
            r_ref[to, 2 * OWN : 3 * OWN] = d_value[rows].astype(BF16)
            r_ref[to, 3 * OWN :] = attended[rows]


def gradient_kernel(
    spot, p0, p1, p2, p3, p4, p5, p6, p7, r0, r1, r2, r3, dt_ref, at_ref, normed0, normed1, w_qkv,
    keep, send, g_ref, p_ref, n_ref,
):
    x, core = spot[0], spot[2]
    parts = (p0, p1, p2, p3, p4, p5, p6, p7)
    d_high, d_low = two_terms(dt_ref[...])
    normed = jnp.concatenate([normed0[...], normed1[...]], 0)
    g_ref[...] = dot(d_high, normed) + dot(d_low, normed)
    p_ref[...] = dot(at_ref[...], jnp.concatenate([part[1] for part in parts], 0)).T
    columns = own_columns(w_qkv, x)
    gain_row = jnp.zeros((1, C), F32)
    offset_row = jnp.zeros((1, C), F32)
    for member, r_ref in enumerate((r0, r1, r2, r3)):
        rows = jnp.concatenate([parts[member][0], parts[4 + member][0]], 0)
        d_normed = dot_nt(r_ref[:, : 3 * OWN], columns)
        gain_row += jnp.sum(d_normed * unit_of(rows)[0], 0, keepdims=True)
        offset_row += jnp.sum(d_normed, 0, keepdims=True)
    row = lax.broadcasted_iota(jnp.int32, (128, C), 0)
    n_ref[...] = jnp.where(row == 0, gain_row, jnp.where(row == 1, offset_row, 0.0)).T
    for ahead, out in ((0, keep), (1, send)):
        to_core = core if ahead == 0 else 1 - core
        for member in range(16):
            for side in range(2):
                lanes = pl.ds(pl.multiple_of(256 * to_core + 128 * side, 128), 128)
                for slot in range(3):
                    residue = 3 * member + slot
                    third_of = lax.rem(residue // 16 - x + 6, 3)
                    start = pl.multiple_of(128 * third_of + 8 * (residue % 16), 8)
                    top = 24 * side + 8 * slot
                    out[member, top : top + 8, :] = g_ref[pl.ds(start, 8), lanes]
            for z in range(4):
                rows = slice(128 * z + 8 * member, 128 * z + 8 * member + 8)
                piece = p_ref[rows, :]
                top = 48 + 8 * (z // 2)
                out[member, top : top + 8, 64 * (z % 2) : 64 * (z % 2) + 64] = jnp.where(
                    to_core == 0, piece[:, :64], piece[:, 64:]
                )
                if ahead == 0:
                    out[member, 64:, 32 * z : 32 * z + 32] = n_ref[rows, :32]
            if ahead == 1:
                out[member, 64:, :] = jnp.zeros((8, 128), F32)


def z_parts_kernel(spot, pieces, *outs):
    x, y, z = spot[0], spot[1], spot[3]
    members = [
        (pieces[j] + pieces[4 + j]) + (pieces[8 + j] + pieces[12 + j]) for j in range(4)
    ]
    total = (members[0][64:] + members[1][64:]) + (members[2][64:] + members[3][64:])
    for to_z in range(4):
        block = []
        for side in range(2):
            for slot in range(3):
                rows = slice(24 * side + 8 * slot, 24 * side + 8 * slot + 8)
                owner = lax.rem(48 * to_z + 12 * y + 3 * x + slot, 64) // 16
                picked = members[0][rows]
                for j in range(1, 4):
                    picked = jnp.where(owner == j, members[j][rows], picked)
                block.append(picked)
        rows = slice(48 + 8 * (to_z // 2), 56 + 8 * (to_z // 2))
        lanes = slice(64 * (to_z % 2), 64 * (to_z % 2) + 64)
        for pair in range(2):
            block.append(
                jnp.concatenate([members[2 * pair + j][rows, lanes] for j in range(2)], 1)
            )
        lanes = slice(32 * to_z, 32 * to_z + 32)
        block.append(jnp.concatenate([total[:, lanes], jnp.zeros((8, 96), F32)], 1))
        block = jnp.concatenate(block, 0)
        for steps in range(4):
            ahead = lax.rem(to_z - z + 4, 4) == steps
            outs[steps][...] = jnp.where(ahead, block, outs[steps][...]) if to_z else block


def last_kernel(spot, near, core_in, z_in, both_in, g_out, p_out, n_out):
    mine = near[...] + z_in[...]
    theirs = core_in[...] + both_in[...]
    swap = spot[2] == 1
    shares = (jnp.where(swap, theirs, mine), jnp.where(swap, mine, theirs))
    for core in range(2):
        for side in range(2):
            lanes = slice(256 * core + 128 * side, 256 * core + 128 * side + 128)
            g_out[:, lanes] = shares[core][24 * side : 24 * side + 24]
    for member in range(4):
        rows = slice(48 + 8 * (member // 2), 56 + 8 * (member // 2))
        lanes = slice(64 * (member % 2), 64 * (member % 2) + 64)
        p_out[:, 128 * member : 128 * member + 128] = jnp.concatenate(
            [share[rows, lanes] for share in shares], 1
        )
    n_out[...] = (mine[64:] + theirs[64:]).T[:2]


def upper_rows(row):
    return (lax.broadcasted_iota(jnp.int32, (4, 8, C), 1) < 4) != (row == 1)


def merge_kernel(
    spot, inputs, upstream, mine_high, mine_low, other_high, other_low, output, grad_inputs
):
    upper = upper_rows(spot[4])
    for array, (source, out) in enumerate(((inputs, output), (upstream, grad_inputs))):
        for start, other, mine in ((4, other_high, mine_high), (0, other_low, mine_low)):
            rows = source[start : start + 4].astype(F32)
            from_other = other[array].astype(F32)
            from_mine = mine[array].astype(F32)
            first = rows[:, :8] + jnp.where(upper, from_other, from_mine)
            second = rows[:, 8:] + jnp.where(upper, from_mine, from_other)
            out[start : start + 4] = jnp.concatenate([first, second], 1).astype(BF16)


def token_kernel(
    spot, r0, r1, r2, r3, own0, own1, w_qkv, w_proj, norm, out
):
    x = spot[0]
    projected = jnp.zeros((SLAB, C), F32)
    d_normed = jnp.zeros((SLAB, C), F32)
    for r_ref, steps in ((r0, 0), (r1, 3), (r2, 1), (r3, 2)):
        rows = r_ref[...]
        member = lax.rem(x + steps, 4)
        start = pl.multiple_of(OWN * member, OWN)
        projected += dot(rows[:, 3 * OWN :], w_proj[pl.ds(start, OWN), :])
        for third in range(3):
            lanes = slice(third * OWN, (third + 1) * OWN)
            columns = w_qkv[:, pl.ds(pl.multiple_of(start + C * third, OWN), OWN)]
            d_normed += dot_nt(rows[:, lanes], columns)
    out[0] = projected.astype(BF16)
    unit, inv_scale = unit_of(jnp.concatenate([own0[0], own1[0]], 0))
    d_unit = d_normed * norm[0:1, :]
    first_mean = jnp.mean(d_unit, -1, keepdims=True)
    second_mean = jnp.mean(d_unit * unit, -1, keepdims=True)
    out[1] = (inv_scale * (d_unit - first_mean - unit * second_mean)).astype(BF16)


def call(kernel, scalars, arrays, outs, scratch=(), flops=0, moved=0):
    smem = pl.BlockSpec(memory_space=pltpu.SMEM)
    vmem = pl.BlockSpec(memory_space=pltpu.VMEM)
    return pl.pallas_call(
        kernel,
        out_shape=[jax.ShapeDtypeStruct(shape, dtype) for shape, dtype in outs],
        in_specs=[smem] + [vmem] * len(arrays),
        out_specs=[vmem] * len(outs),
        scratch_shapes=list(scratch),
        compiler_params=pltpu.CompilerParams(vmem_limit_bytes=8 * 2**20),
        cost_estimate=pl.CostEstimate(flops=flops, bytes_accessed=moved, transcendentals=0),
        name=kernel.__name__,
    )(scalars, *arrays)


def on_device(inputs, norm_params, w_qkv, w_proj, upstream):
    place = lax.axis_index("wide")
    column = lax.axis_index("narrow")
    x, y, z = place % 4, place // 4 % 4, place // 16
    core = column % 2
    row = 1 - y % 2
    window = (place - 4) % 64 // 8
    spot = jnp.stack([x, y, core, z, row]).astype(jnp.int32)
    flags = jnp.stack([4 * (window == 7), 2 * (column == 3), row, x]).astype(jnp.int32)

    own_inputs, own_upstream = inputs[0, 0], upstream[0, 0]
    upper_y = (jnp.arange(8)[:, None] < 4) != (row == 1)
    both = jnp.stack([own_inputs, own_upstream]).reshape(2, 8, 2, 8, C)
    mine = jnp.where(upper_y, both[:, :, 1], both[:, :, 0])
    other = jnp.where(upper_y, both[:, :, 0], both[:, :, 1])
    lower_in = move(mine[:, :4], lambda p, n: (p, n - 1))
    other_in = move(other[:, 4:], lambda p, n: (partner_of(p), n))
    cross_in = move(other[:, :4], lambda p, n: (partner_of(p), n - 1))

    part0 = jnp.stack([mine[:, 4:], lower_in], 1).reshape(2, SLAB // 2, C)
    parts0 = [part0] + [move(part0, along_x(steps)) for steps in (1, -1, 2)]
    part1 = jnp.stack([other_in, cross_in], 1).reshape(2, SLAB // 2, C)
    parts1 = [part1] + [move(part1, along_x(steps)) for steps in (1, -1, 2)]
    half = TOKENS // 2
    normed0, qkv0, up0 = call(
        first_kernel,
        flags,
        (*parts0, norm_params, w_qkv, w_proj),
        [((half, C), BF16), ((half, 3 * OWN), BF16), ((half, OWN), BF16)],
        flops=10_000_000_000,
        moved=3_000_000,
    )
    r_own, r_left, r_right, r_far, d_t, a_t, normed1 = call(
        attention_kernel,
        flags,
        (*parts1, normed0, qkv0, up0, norm_params, w_qkv, w_proj),
        [((SLAB, C), BF16)] * 4
        + [((3 * OWN, TOKENS), F32), ((OWN, TOKENS), BF16), ((half, C), BF16)],
        flops=1_200_000_000,
        moved=6_000_000,
    )

    from_right = move(r_left, along_x(-1))
    from_left = move(r_right, along_x(1))
    from_far = move(r_far, along_x(2))
    keep, send = call(
        gradient_kernel,
        spot,
        (*parts0, *parts1, r_own, r_left, r_right, r_far, d_t, a_t, normed0, normed1, w_qkv),
        [((16, 72, 128), F32)] * 2,
        scratch=[
            pltpu.VMEM((3 * OWN, C), F32),
            pltpu.VMEM((C, OWN), F32),
            pltpu.VMEM((C, 128), F32),
        ],
        flops=20_000_000_000,
        moved=6_000_000,
    )
    halves = keep + move(send, other_core)
    halves, from_left, from_right, from_far = lax.optimization_barrier(
        (halves, from_left, from_right, from_far)
    )
    plane = exchange(halves, plane_groups())
    (back,) = call(
        token_kernel,
        spot,
        (r_own, from_left, from_right, from_far, part0, part1, w_qkv, w_proj, norm_params),
        [((2, SLAB, C), BF16)],
        flops=500_000_000,
        moved=4_000_000,
    )
    back = back.reshape(2, 4, 4, 8, C)
    lower = move(back[:, 1], lambda p, n: (p, n + 1))
    other_upper = move(back[:, 2], lambda p, n: (partner_of(p), n))
    other_lower = move(back[:, 3], lambda p, n: (partner_of(p), n + 1))

    z_parts = call(z_parts_kernel, spot, (plane,), [((72, 128), F32)] * 4)
    output, grad_inputs = call(
        merge_kernel,
        spot,
        (own_inputs, own_upstream, back[:, 0], lower, other_upper, other_lower),
        [((8, 16, C), BF16)] * 2,
    )
    line = [z_parts[0]] + [move(z_parts[steps], along_z(steps)) for steps in (1, 2, 3)]
    line[1], line[2], line[3], output, grad_inputs = lax.optimization_barrier(
        (line[1], line[2], line[3], output, grad_inputs)
    )
    line = (line[0] + line[1]) + (line[2] + line[3])
    grad_qkv, grad_proj, grad_norm = call(
        last_kernel,
        spot,
        (line, move(line, other_core), move(line, other_z), move(line, other_both)),
        [((24, C), F32), ((8, C), F32), ((2, 8), F32)],
    )
    return (
        output[None, None], grad_inputs[None, None], grad_qkv.T, grad_proj.T, grad_norm
    )


def solution(mesh):
    in_specs = (
        P(None, "wide", "narrow", None, None),
        P(),
        P(),
        P(),
        P(None, "wide", "narrow", None, None),
    )
    out_specs = (
        P(None, "wide", "narrow", None, None),
        P(None, "wide", "narrow", None, None),
        P(None, "wide"),
        P(None, "wide"),
        P(None, "wide"),
    )
    return jax.shard_map(
        on_device, mesh=mesh, in_specs=in_specs, out_specs=out_specs, check_vma=False
    )
```

```python
import jax
import jax.numpy as jnp
from jax import lax
from jax.experimental import pallas as pl
from jax.experimental.pallas import tpu as pltpu
from jax.sharding import PartitionSpec as P

HEADS = 16
HEAD_DIM = 32
C = 512
WIN = 8
RING = 4
OWN = C // RING
SLAB = 128
TOKENS = RING * SLAB
BLOCK = 256
CHUNK = 64
SCALE = HEAD_DIM**-0.5
LOG2E = 1.4426950408889634
F32 = jnp.float32
BF16 = jnp.bfloat16


def move(value, target):
    pairs = []
    for place in range(64):
        for column in range(4):
            to_place, to_column = target(place, column)
            pairs.append((place * 4 + column, (to_place % 64) * 4 + to_column % 4))
    return lax.ppermute(value, ("wide", "narrow"), pairs)


def partner_of(place):
    return place + 4 if (place // 4) % 2 else place - 4


def across_x(mask):
    return lambda p, n: (p ^ mask, n)


def across_y(mask):
    return lambda p, n: (p ^ (4 * mask), n)


def across_z(mask):
    return lambda p, n: (p ^ (16 * mask), n)


def across_narrow(mask):
    return lambda p, n: (p, n ^ mask)


def dot(a, b):
    return lax.dot_general(a, b, (((1,), (0,)), ((), ())), preferred_element_type=F32)


def dot_nt(a, b):
    return lax.dot_general(a, b, (((1,), (1,)), ((), ())), preferred_element_type=F32)


def unit_of(rows):
    floats = rows.astype(F32)
    average = jnp.mean(floats, -1, keepdims=True)
    centered = floats - average
    variance = jnp.mean(centered * centered, -1, keepdims=True)
    inv_scale = lax.rsqrt(variance + 1e-05)
    return centered * inv_scale, inv_scale


def two_terms(value):
    high = value.astype(BF16)
    low = (value - high.astype(F32)).astype(BF16)
    return high, low


def own_columns(w_qkv, x):
    start = pl.multiple_of(OWN * x, OWN)
    return jnp.concatenate(
        [w_qkv[:, pl.ds(pl.multiple_of(start + C * third, OWN), OWN)] for third in range(3)], 1
    )


def project(parts, norm, w_qkv, w_proj, member):
    unit, _ = unit_of(jnp.concatenate([part[0] for part in parts], 0))
    normed = (unit * norm[0:1, :] + norm[1:2, :]).astype(BF16)
    qkv = dot(normed, own_columns(w_qkv, member)).astype(BF16)
    rows = w_proj[pl.ds(pl.multiple_of(OWN * member, OWN), OWN), :]
    cotangent = dot_nt(jnp.concatenate([part[1] for part in parts], 0), rows).astype(BF16)
    return normed, qkv, cotangent


def first_kernel(flags, p0, p1, p2, p3, norm, w_qkv, w_proj, normed_ref, qkv_ref, up_ref):
    normed_ref[...], qkv_ref[...], up_ref[...] = project(
        (p0, p1, p2, p3), norm, w_qkv, w_proj, flags[3]
    )


def attention_kernel(
    flags, p0, p1, p2, p3, normed0, qkv0, up0, norm, w_qkv, w_proj,
    r0, r1, r2, r3, dt_ref, at_ref, normed1,
):
    normed1[...], qkv1, up1 = project((p0, p1, p2, p3), norm, w_qkv, w_proj, flags[3])
    qkv = jnp.concatenate([qkv0[...], qkv1], 0)
    cotangent = jnp.concatenate([up0[...], up1], 0)
    queries = qkv[:, :OWN]
    keys = qkv[:, OWN : 2 * OWN]
    values = qkv[:, 2 * OWN :]
    queries_t = queries.T
    cotangent_t = cotangent.T
    keys_t = keys.T
    values_t = values.T
    head_of_lane = lax.broadcasted_iota(jnp.int32, (TOKENS, OWN), 1) // HEAD_DIM

    def label(shape, dim):
        token = lax.broadcasted_iota(jnp.int32, shape, dim)
        row = token // 256
        half = (token // 32) % 2
        low_y = (token // 4) % 2
        return row * flags[0] + half * flags[1] + low_y * flags[2]

    key_label = label((TOKENS, 1), 0)
    query_label = label((1, TOKENS), 1)
    d_key = jnp.zeros((TOKENS, OWN), F32)
    d_value = jnp.zeros((TOKENS, OWN), F32)
    for block in range(TOKENS // BLOCK):
        span = slice(block * BLOCK, (block + 1) * BLOCK)
        allowed = key_label == query_label[:, span]
        for head in range(RING):
            chosen = head_of_lane == head
            rows = slice(head * HEAD_DIM, (head + 1) * HEAD_DIM)
            key_head = jnp.where(chosen, keys, jnp.zeros_like(keys))
            value_head = jnp.where(chosen, values, jnp.zeros_like(values))
            scores = jnp.where(allowed, dot(key_head, queries_t[:, span]), -1e30)
            highest = jnp.max(scores, 0, keepdims=True)
            d_probs = dot(value_head, cotangent_t[:, span])
            weights = []
            total = jnp.zeros((8, BLOCK), F32)
            inner = jnp.zeros((8, BLOCK), F32)
            for start in range(0, TOKENS, CHUNK):
                part = slice(start, start + CHUNK)
                weight = jnp.exp2((scores[part] - highest) * (SCALE * LOG2E))
                total += jnp.sum(weight.reshape(CHUNK // 8, 8, BLOCK), 0)
                inner += jnp.sum((weight * d_probs[part]).reshape(CHUNK // 8, 8, BLOCK), 0)
                weights.append(weight)
            over = 1.0 / jnp.sum(total, 0, keepdims=True)
            inner = jnp.sum(inner, 0, keepdims=True) * over
            over_scaled = over * SCALE
            probs_low, d_scores = [], []
            for index, weight in enumerate(weights):
                part = slice(index * CHUNK, (index + 1) * CHUNK)
                probs_low.append((weight * over).astype(BF16))
                d_scores.append(((weight * over_scaled) * (d_probs[part] - inner)).astype(BF16))
            probs_low = jnp.concatenate(probs_low, 0)
            d_scores = jnp.concatenate(d_scores, 0)
            at_ref[rows, span] = dot(values_t[rows], probs_low).astype(BF16)
            dt_ref[rows, span] = dot(keys_t[rows], d_scores)
            query_head = jnp.where(chosen[span], queries[span], jnp.zeros_like(queries[span]))
            cotangent_head = jnp.where(
                chosen[span], cotangent[span], jnp.zeros_like(cotangent[span])
            )
            d_key += dot(d_scores, query_head)
            d_value += dot(probs_low, cotangent_head)
    dt_ref[OWN : 2 * OWN, :] = d_key.T
    dt_ref[2 * OWN :, :] = d_value.T
    d_query = dt_ref[:OWN, :].T.astype(BF16)
    attended = at_ref[...].T
    for member, r_ref in enumerate((r0, r1, r2, r3)):
        for part in range(2):
            rows = slice(256 * part + 64 * member, 256 * part + 64 * member + 64)
            to = slice(64 * part, 64 * part + 64)
            r_ref[to, :OWN] = d_query[rows]
            r_ref[to, OWN : 2 * OWN] = d_key[rows].astype(BF16)
            r_ref[to, 2 * OWN : 3 * OWN] = d_value[rows].astype(BF16)
            r_ref[to, 3 * OWN :] = attended[rows]


def gradient_kernel(
    spot, p0, p1, p2, p3, p4, p5, p6, p7, r0, r1, r2, r3, dt_ref, at_ref, normed0, normed1, w_qkv,
    keep, send, g_ref, p_ref, n_ref,
):
    x, y, core = spot[0], spot[1], spot[2]
    parts = (p0, p1, p2, p3, p4, p5, p6, p7)
    d_high, d_low = two_terms(dt_ref[...])
    normed = jnp.concatenate([normed0[...], normed1[...]], 0)
    g_ref[...] = dot(d_high, normed) + dot(d_low, normed)
    p_ref[...] = dot(at_ref[...], jnp.concatenate([part[1] for part in parts], 0)).T
    columns = own_columns(w_qkv, x)
    gain_row = jnp.zeros((1, C), F32)
    offset_row = jnp.zeros((1, C), F32)
    for member, r_ref in enumerate((r0, r1, r2, r3)):
        rows = jnp.concatenate([parts[member][0], parts[4 + member][0]], 0)
        d_normed = dot_nt(r_ref[:, : 3 * OWN], columns)
        gain_row += jnp.sum(d_normed * unit_of(rows)[0], 0, keepdims=True)
        offset_row += jnp.sum(d_normed, 0, keepdims=True)
    row = lax.broadcasted_iota(jnp.int32, (128, C), 0)
    n_ref[...] = jnp.where(row == 0, gain_row, jnp.where(row == 1, offset_row, 0.0)).T
    for ahead, out in ((0, keep), (1, send)):
        to_core = core if ahead == 0 else 1 - core
        for across in range(4):
            to_y = y ^ across
            for to_x in range(4):
                block = 4 * across + to_x
                for side in range(2):
                    lanes = pl.ds(pl.multiple_of(256 * to_core + 128 * side, 128), 128)
                    for slot in range(3):
                        residue = 12 * to_y + 3 * to_x + slot
                        third_of = lax.rem(residue // 16 - x + 6, 3)
                        start = pl.multiple_of(128 * third_of + 8 * lax.rem(residue, 16), 8)
                        top = 24 * side + 8 * slot
                        out[block, top : top + 8, :] = g_ref[pl.ds(start, 8), lanes]
                for z in range(4):
                    rows = pl.ds(pl.multiple_of(128 * z + 32 * to_y + 8 * to_x, 8), 8)
                    piece = p_ref[rows, :]
                    top = 48 + 8 * (z // 2)
                    out[block, top : top + 8, 64 * (z % 2) : 64 * (z % 2) + 64] = jnp.where(
                        to_core == 0, piece[:, :64], piece[:, 64:]
                    )
                    if ahead == 0:
                        out[block, 64:, 32 * z : 32 * z + 32] = n_ref[rows, :32]
                if ahead == 1:
                    out[block, 64:, :] = jnp.zeros((8, 128), F32)


def x_parts_kernel(spot, s0, s1, s2, s3, *outs):
    x = spot[0]
    for across, out in enumerate(outs):
        to_x = x ^ across
        out[...] = (s0[to_x] + s1[to_x]) + (s2[to_x] + s3[to_x])


def z_parts_kernel(spot, m0, m1, m2, m3, *outs):
    x, y, z = spot[0], spot[1], spot[3]
    pieces = (m0, m1, m2, m3)

    def from_member(member, rows):
        across = member ^ x
        picked = pieces[0][rows, :]
        for index in range(1, 4):
            picked = jnp.where(across == index, pieces[index][rows, :], picked)
        return picked

    total = (m0[64:, :] + m1[64:, :]) + (m2[64:, :] + m3[64:, :])
    proj = [from_member(member, slice(48, 64)) for member in range(4)]
    for to_z in range(4):
        block = []
        for side in range(2):
            for slot in range(3):
                owner = lax.rem(48 * to_z + 12 * y + 3 * x + slot, 64) // 16
                top = 24 * side + 8 * slot
                block.append(from_member(owner, slice(top, top + 8)))
        rows = slice(8 * (to_z // 2), 8 * (to_z // 2) + 8)
        lanes = slice(64 * (to_z % 2), 64 * (to_z % 2) + 64)
        for pair in range(2):
            block.append(
                jnp.concatenate([proj[2 * pair][rows, lanes], proj[2 * pair + 1][rows, lanes]], 1)
            )
        lanes = slice(32 * to_z, 32 * to_z + 32)
        block.append(jnp.concatenate([total[:, lanes], jnp.zeros((8, 96), F32)], 1))
        block = jnp.concatenate(block, 0)
        for across in range(4):
            ahead = (to_z ^ z) == across
            outs[across][...] = jnp.where(ahead, block, outs[across][...]) if to_z else block


def last_kernel(spot, near, core_in, z_in, both_in, g_out, p_out, n_out):
    mine = near[...] + z_in[...]
    theirs = core_in[...] + both_in[...]
    swap = spot[2] == 1
    shares = (jnp.where(swap, theirs, mine), jnp.where(swap, mine, theirs))
    for core in range(2):
        for side in range(2):
            lanes = slice(256 * core + 128 * side, 256 * core + 128 * side + 128)
            g_out[:, lanes] = shares[core][24 * side : 24 * side + 24]
    for member in range(4):
        rows = slice(48 + 8 * (member // 2), 56 + 8 * (member // 2))
        lanes = slice(64 * (member % 2), 64 * (member % 2) + 64)
        p_out[:, 128 * member : 128 * member + 128] = jnp.concatenate(
            [share[rows, lanes] for share in shares], 1
        )
    n_out[...] = (mine[64:] + theirs[64:]).T[:2]


def upper_rows(row):
    return (lax.broadcasted_iota(jnp.int32, (4, 8, C), 1) < 4) != (row == 1)


def merge_kernel(
    spot, inputs, upstream, mine_high, mine_low, other_high, other_low, output, grad_inputs
):
    upper = upper_rows(spot[4])
    for array, (source, out) in enumerate(((inputs, output), (upstream, grad_inputs))):
        for start, other, mine in ((4, other_high, mine_high), (0, other_low, mine_low)):
            rows = source[start : start + 4].astype(F32)
            from_other = other[array].astype(F32)
            from_mine = mine[array].astype(F32)
            first = rows[:, :8] + jnp.where(upper, from_other, from_mine)
            second = rows[:, 8:] + jnp.where(upper, from_mine, from_other)
            out[start : start + 4] = jnp.concatenate([first, second], 1).astype(BF16)


def token_kernel(
    spot, r0, r1, r2, r3, own0, own1, w_qkv, w_proj, norm, out
):
    x = spot[0]
    projected = jnp.zeros((SLAB, C), F32)
    d_normed = jnp.zeros((SLAB, C), F32)
    for across, r_ref in enumerate((r0, r1, r2, r3)):
        rows = r_ref[...]
        member = x ^ across
        start = pl.multiple_of(OWN * member, OWN)
        projected += dot(rows[:, 3 * OWN :], w_proj[pl.ds(start, OWN), :])
        for third in range(3):
            lanes = slice(third * OWN, (third + 1) * OWN)
            columns = w_qkv[:, pl.ds(pl.multiple_of(start + C * third, OWN), OWN)]
            d_normed += dot_nt(rows[:, lanes], columns)
    out[0] = projected.astype(BF16)
    unit, inv_scale = unit_of(jnp.concatenate([own0[0], own1[0]], 0))
    d_unit = d_normed * norm[0:1, :]
    first_mean = jnp.mean(d_unit, -1, keepdims=True)
    second_mean = jnp.mean(d_unit * unit, -1, keepdims=True)
    out[1] = (inv_scale * (d_unit - first_mean - unit * second_mean)).astype(BF16)


def call(kernel, scalars, arrays, outs, scratch=(), flops=0, moved=0):
    smem = pl.BlockSpec(memory_space=pltpu.SMEM)
    vmem = pl.BlockSpec(memory_space=pltpu.VMEM)
    return pl.pallas_call(
        kernel,
        out_shape=[jax.ShapeDtypeStruct(shape, dtype) for shape, dtype in outs],
        in_specs=[smem] + [vmem] * len(arrays),
        out_specs=[vmem] * len(outs),
        scratch_shapes=list(scratch),
        compiler_params=pltpu.CompilerParams(vmem_limit_bytes=8 * 2**20),
        cost_estimate=pl.CostEstimate(flops=flops, bytes_accessed=moved, transcendentals=0),
        name=kernel.__name__,
    )(scalars, *arrays)


def on_device(inputs, norm_params, w_qkv, w_proj, upstream):
    place = lax.axis_index("wide")
    column = lax.axis_index("narrow")
    x, y, z = place % 4, place // 4 % 4, place // 16
    core = column % 2
    row = 1 - y % 2
    window = (place - 4) % 64 // 8
    spot = jnp.stack([x, y, core, z, row]).astype(jnp.int32)
    flags = jnp.stack([4 * (window == 7), 2 * (column == 3), row, x]).astype(jnp.int32)

    own_inputs, own_upstream = inputs[0, 0], upstream[0, 0]
    upper_y = (jnp.arange(8)[:, None] < 4) != (row == 1)
    both = jnp.stack([own_inputs, own_upstream]).reshape(2, 8, 2, 8, C)
    mine = jnp.where(upper_y, both[:, :, 1], both[:, :, 0])
    other = jnp.where(upper_y, both[:, :, 0], both[:, :, 1])
    lower_in = move(mine[:, :4], lambda p, n: (p, n - 1))
    other_in = move(other[:, 4:], lambda p, n: (partner_of(p), n))
    cross_in = move(other[:, :4], lambda p, n: (partner_of(p), n - 1))

    part0 = jnp.stack([mine[:, 4:], lower_in], 1).reshape(2, SLAB // 2, C)
    parts0 = [part0] + [move(part0, across_x(mask)) for mask in (1, 2, 3)]
    part1 = jnp.stack([other_in, cross_in], 1).reshape(2, SLAB // 2, C)
    parts1 = [part1] + [move(part1, across_x(mask)) for mask in (1, 2, 3)]
    half = TOKENS // 2
    normed0, qkv0, up0 = call(
        first_kernel,
        flags,
        (*parts0, norm_params, w_qkv, w_proj),
        [((half, C), BF16), ((half, 3 * OWN), BF16), ((half, OWN), BF16)],
        flops=10_000_000_000,
        moved=3_000_000,
    )
    r0, r1, r2, r3, d_t, a_t, normed1 = call(
        attention_kernel,
        flags,
        (*parts1, normed0, qkv0, up0, norm_params, w_qkv, w_proj),
        [((SLAB, C), BF16)] * 4
        + [((3 * OWN, TOKENS), F32), ((OWN, TOKENS), BF16), ((half, C), BF16)],
        flops=1_200_000_000,
        moved=6_000_000,
    )

    returned = [r0] + [move(rows, across_x(mask)) for mask, rows in ((1, r1), (2, r2), (3, r3))]
    keep, send = call(
        gradient_kernel,
        spot,
        (*parts0, *parts1, r0, r1, r2, r3, d_t, a_t, normed0, normed1, w_qkv),
        [((16, 72, 128), F32)] * 2,
        scratch=[
            pltpu.VMEM((3 * OWN, C), F32),
            pltpu.VMEM((C, OWN), F32),
            pltpu.VMEM((C, 128), F32),
        ],
        flops=20_000_000_000,
        moved=6_000_000,
    )
    received = move(send, across_narrow(1))
    blocks = [slice(4 * mask, 4 * mask + 4) for mask in range(4)]
    halves = [keep[block] + received[block] for block in blocks]
    from_y = [halves[0]] + [move(halves[mask], across_y(mask)) for mask in (1, 2, 3)]
    (back,) = call(
        token_kernel,
        spot,
        (*returned, part0, part1, w_qkv, w_proj, norm_params),
        [((2, SLAB, C), BF16)],
        flops=500_000_000,
        moved=4_000_000,
    )
    from_y[1], from_y[2], from_y[3], back = lax.optimization_barrier(
        (from_y[1], from_y[2], from_y[3], back)
    )
    back = back.reshape(2, 4, 4, 8, C)
    lower = move(back[:, 1], lambda p, n: (p, n + 1))
    other_upper = move(back[:, 2], lambda p, n: (partner_of(p), n))
    other_lower = move(back[:, 3], lambda p, n: (partner_of(p), n + 1))

    share = ((72, 128), F32)
    x_parts = call(x_parts_kernel, spot, from_y, [share] * 4)
    from_x = [x_parts[0]] + [move(x_parts[mask], across_x(mask)) for mask in (1, 2, 3)]
    z_parts = call(z_parts_kernel, spot, from_x, [share] * 4)
    output, grad_inputs = call(
        merge_kernel,
        spot,
        (own_inputs, own_upstream, back[:, 0], lower, other_upper, other_lower),
        [((8, 16, C), BF16)] * 2,
    )
    line = [z_parts[0]] + [move(z_parts[mask], across_z(mask)) for mask in (1, 2, 3)]
    line[1], line[2], line[3], output, grad_inputs = lax.optimization_barrier(
        (line[1], line[2], line[3], output, grad_inputs)
    )
    line = (line[0] + line[1]) + (line[2] + line[3])
    grad_qkv, grad_proj, grad_norm = call(
        last_kernel,
        spot,
        (line, *[move(line, across_narrow(mask)) for mask in (1, 2, 3)]),
        [((24, C), F32), ((8, C), F32), ((2, 8), F32)],
    )
    return (
        output[None, None], grad_inputs[None, None], grad_qkv.T, grad_proj.T, grad_norm
    )


def solution(mesh):
    in_specs = (
        P(None, "wide", "narrow", None, None),
        P(),
        P(),
        P(),
        P(None, "wide", "narrow", None, None),
    )
    out_specs = (
        P(None, "wide", "narrow", None, None),
        P(None, "wide", "narrow", None, None),
        P(None, "wide"),
        P(None, "wide"),
        P(None, "wide"),
    )
    return jax.shard_map(
        on_device, mesh=mesh, in_specs=in_specs, out_specs=out_specs, check_vma=False
    )
```

```python
import jax
import jax.numpy as jnp
from jax import lax
from jax.experimental import pallas as pl
from jax.experimental.pallas import tpu as pltpu
from jax.sharding import PartitionSpec as P

HEADS = 16
HEAD_DIM = 32
C = 512
WIN = 8
RING = 4
OWN = C // RING
SLAB = 128
TOKENS = RING * SLAB
BLOCK = 256
CHUNK = 64
SCALE = HEAD_DIM**-0.5
LOG2E = 1.4426950408889634
F32 = jnp.float32
BF16 = jnp.bfloat16


def move(value, target):
    pairs = []
    for place in range(64):
        for column in range(4):
            to_place, to_column = target(place, column)
            pairs.append((place * 4 + column, (to_place % 64) * 4 + to_column % 4))
    return lax.ppermute(value, ("wide", "narrow"), pairs)


def partner_of(place):
    return place + 4 if (place // 4) % 2 else place - 4


def across_x(mask):
    return lambda p, n: (p ^ mask, n)


def across_y(mask):
    return lambda p, n: (p ^ (4 * mask), n)


def across_z(mask):
    return lambda p, n: (p ^ (16 * mask), n)


def across_narrow(mask):
    return lambda p, n: (p, n ^ mask)


def dot(a, b):
    return lax.dot_general(a, b, (((1,), (0,)), ((), ())), preferred_element_type=F32)


def dot_nt(a, b):
    return lax.dot_general(a, b, (((1,), (1,)), ((), ())), preferred_element_type=F32)


def unit_of(rows):
    floats = rows.astype(F32)
    average = jnp.mean(floats, -1, keepdims=True)
    centered = floats - average
    variance = jnp.mean(centered * centered, -1, keepdims=True)
    inv_scale = lax.rsqrt(variance + 1e-05)
    return centered * inv_scale, inv_scale


def two_terms(value):
    high = value.astype(BF16)
    low = (value - high.astype(F32)).astype(BF16)
    return high, low


def own_columns(w_qkv, x):
    start = pl.multiple_of(OWN * x, OWN)
    return jnp.concatenate(
        [w_qkv[:, pl.ds(pl.multiple_of(start + C * third, OWN), OWN)] for third in range(3)], 1
    )


def project(parts, norm, w_qkv, w_proj, member):
    unit, _ = unit_of(jnp.concatenate([part[0] for part in parts], 0))
    normed = (unit * norm[0:1, :] + norm[1:2, :]).astype(BF16)
    qkv = dot(normed, own_columns(w_qkv, member)).astype(BF16)
    rows = w_proj[pl.ds(pl.multiple_of(OWN * member, OWN), OWN), :]
    cotangent = dot_nt(jnp.concatenate([part[1] for part in parts], 0), rows).astype(BF16)
    return normed, qkv, cotangent


def first_kernel(flags, p0, p1, p2, p3, norm, w_qkv, w_proj, normed_ref, qkv_ref, up_ref):
    normed_ref[...], qkv_ref[...], up_ref[...] = project(
        (p0, p1, p2, p3), norm, w_qkv, w_proj, flags[3]
    )


def keeper_kernel(flags, own, norm, w_qkv, w_proj, *outs):
    for across, out in enumerate(outs):
        _, out[:, : 3 * OWN], out[:, 3 * OWN :] = project(
            (own,), norm, w_qkv, w_proj, flags[3] ^ across
        )


def attention_kernel(
    flags, s0, s1, s2, s3, qkv0, up0, r0, r1, r2, r3, dt_ref, at_ref
):
    shares = jnp.concatenate([s0[...], s1[...], s2[...], s3[...]], 0)
    qkv = jnp.concatenate([qkv0[...], shares[:, : 3 * OWN]], 0)
    cotangent = jnp.concatenate([up0[...], shares[:, 3 * OWN :]], 0)
    queries = qkv[:, :OWN]
    keys = qkv[:, OWN : 2 * OWN]
    values = qkv[:, 2 * OWN :]
    queries_t = queries.T
    cotangent_t = cotangent.T
    keys_t = keys.T
    values_t = values.T
    head_of_lane = lax.broadcasted_iota(jnp.int32, (TOKENS, OWN), 1) // HEAD_DIM

    def label(shape, dim):
        token = lax.broadcasted_iota(jnp.int32, shape, dim)
        row = token // 256
        half = (token // 32) % 2
        low_y = (token // 4) % 2
        return row * flags[0] + half * flags[1] + low_y * flags[2]

    key_label = label((TOKENS, 1), 0)
    query_label = label((1, TOKENS), 1)
    d_key = jnp.zeros((TOKENS, OWN), F32)
    d_value = jnp.zeros((TOKENS, OWN), F32)
    for block in range(TOKENS // BLOCK):
        span = slice(block * BLOCK, (block + 1) * BLOCK)
        allowed = key_label == query_label[:, span]
        for head in range(RING):
            chosen = head_of_lane == head
            rows = slice(head * HEAD_DIM, (head + 1) * HEAD_DIM)
            key_head = jnp.where(chosen, keys, jnp.zeros_like(keys))
            value_head = jnp.where(chosen, values, jnp.zeros_like(values))
            scores = jnp.where(allowed, dot(key_head, queries_t[:, span]), -1e30)
            highest = jnp.max(scores, 0, keepdims=True)
            d_probs = dot(value_head, cotangent_t[:, span])
            weights = []
            total = jnp.zeros((8, BLOCK), F32)
            inner = jnp.zeros((8, BLOCK), F32)
            for start in range(0, TOKENS, CHUNK):
                part = slice(start, start + CHUNK)
                weight = jnp.exp2((scores[part] - highest) * (SCALE * LOG2E))
                total += jnp.sum(weight.reshape(CHUNK // 8, 8, BLOCK), 0)
                inner += jnp.sum((weight * d_probs[part]).reshape(CHUNK // 8, 8, BLOCK), 0)
                weights.append(weight)
            over = 1.0 / jnp.sum(total, 0, keepdims=True)
            inner = jnp.sum(inner, 0, keepdims=True) * over
            over_scaled = over * SCALE
            probs_low, d_scores = [], []
            for index, weight in enumerate(weights):
                part = slice(index * CHUNK, (index + 1) * CHUNK)
                probs_low.append((weight * over).astype(BF16))
                d_scores.append(((weight * over_scaled) * (d_probs[part] - inner)).astype(BF16))
            probs_low = jnp.concatenate(probs_low, 0)
            d_scores = jnp.concatenate(d_scores, 0)
            at_ref[rows, span] = dot(values_t[rows], probs_low).astype(BF16)
            dt_ref[rows, span] = dot(keys_t[rows], d_scores)
            query_head = jnp.where(chosen[span], queries[span], jnp.zeros_like(queries[span]))
            cotangent_head = jnp.where(
                chosen[span], cotangent[span], jnp.zeros_like(cotangent[span])
            )
            d_key += dot(d_scores, query_head)
            d_value += dot(probs_low, cotangent_head)
    dt_ref[OWN : 2 * OWN, :] = d_key.T
    dt_ref[2 * OWN :, :] = d_value.T
    d_query = dt_ref[:OWN, :].T.astype(BF16)
    attended = at_ref[...].T
    for member, r_ref in enumerate((r0, r1, r2, r3)):
        for part in range(2):
            rows = slice(256 * part + 64 * member, 256 * part + 64 * member + 64)
            to = slice(64 * part, 64 * part + 64)
            r_ref[to, :OWN] = d_query[rows]
            r_ref[to, OWN : 2 * OWN] = d_key[rows].astype(BF16)
            r_ref[to, 2 * OWN : 3 * OWN] = d_value[rows].astype(BF16)
            r_ref[to, 3 * OWN :] = attended[rows]


def gradient_kernel(
    spot, p0, p1, p2, p3, p4, p5, p6, p7, r0, r1, r2, r3, dt_ref, at_ref, normed0, norm, w_qkv,
    keep, send, g_ref, p_ref, n_ref,
):
    x, y, core = spot[0], spot[1], spot[2]
    parts = (p0, p1, p2, p3, p4, p5, p6, p7)
    d_high, d_low = two_terms(dt_ref[...])
    units = [unit_of(part[0])[0] for part in parts]
    normed1 = [(unit * norm[0:1, :] + norm[1:2, :]).astype(BF16) for unit in units[4:]]
    normed = jnp.concatenate([normed0[...]] + normed1, 0)
    g_ref[...] = dot(d_high, normed) + dot(d_low, normed)
    p_ref[...] = dot(at_ref[...], jnp.concatenate([part[1] for part in parts], 0)).T
    columns = own_columns(w_qkv, x)
    gain_row = jnp.zeros((1, C), F32)
    offset_row = jnp.zeros((1, C), F32)
    for member, r_ref in enumerate((r0, r1, r2, r3)):
        unit = jnp.concatenate([units[member], units[4 + member]], 0)
        d_normed = dot_nt(r_ref[:, : 3 * OWN], columns)
        gain_row += jnp.sum(d_normed * unit, 0, keepdims=True)
        offset_row += jnp.sum(d_normed, 0, keepdims=True)
    row = lax.broadcasted_iota(jnp.int32, (128, C), 0)
    n_ref[...] = jnp.where(row == 0, gain_row, jnp.where(row == 1, offset_row, 0.0)).T
    for ahead, out in ((0, keep), (1, send)):
        to_core = core if ahead == 0 else 1 - core
        for across in range(4):
            to_y = y ^ across
            for to_x in range(4):
                block = 4 * across + to_x
                for side in range(2):
                    lanes = pl.ds(pl.multiple_of(256 * to_core + 128 * side, 128), 128)
                    for slot in range(3):
                        residue = 12 * to_y + 3 * to_x + slot
                        third_of = lax.rem(residue // 16 - x + 6, 3)
                        start = pl.multiple_of(128 * third_of + 8 * lax.rem(residue, 16), 8)
                        top = 24 * side + 8 * slot
                        out[block, top : top + 8, :] = g_ref[pl.ds(start, 8), lanes]
                for z in range(4):
                    rows = pl.ds(pl.multiple_of(128 * z + 32 * to_y + 8 * to_x, 8), 8)
                    piece = p_ref[rows, :]
                    top = 48 + 8 * (z // 2)
                    out[block, top : top + 8, 64 * (z % 2) : 64 * (z % 2) + 64] = jnp.where(
                        to_core == 0, piece[:, :64], piece[:, 64:]
                    )
                    if ahead == 0:
                        out[block, 64:, 32 * z : 32 * z + 32] = n_ref[rows, :32]
                if ahead == 1:
                    out[block, 64:, :] = jnp.zeros((8, 128), F32)


def x_parts_kernel(spot, s0, s1, s2, s3, *outs):
    x = spot[0]
    for across, out in enumerate(outs):
        to_x = x ^ across
        out[...] = (s0[to_x] + s1[to_x]) + (s2[to_x] + s3[to_x])


def z_parts_kernel(spot, m0, m1, m2, m3, *outs):
    x, y, z = spot[0], spot[1], spot[3]
    pieces = (m0, m1, m2, m3)

    def from_member(member, rows):
        across = member ^ x
        picked = pieces[0][rows, :]
        for index in range(1, 4):
            picked = jnp.where(across == index, pieces[index][rows, :], picked)
        return picked

    total = (m0[64:, :] + m1[64:, :]) + (m2[64:, :] + m3[64:, :])
    proj = [from_member(member, slice(48, 64)) for member in range(4)]
    for to_z in range(4):
        block = []
        for side in range(2):
            for slot in range(3):
                owner = lax.rem(48 * to_z + 12 * y + 3 * x + slot, 64) // 16
                top = 24 * side + 8 * slot
                block.append(from_member(owner, slice(top, top + 8)))
        rows = slice(8 * (to_z // 2), 8 * (to_z // 2) + 8)
        lanes = slice(64 * (to_z % 2), 64 * (to_z % 2) + 64)
        for pair in range(2):
            block.append(
                jnp.concatenate([proj[2 * pair][rows, lanes], proj[2 * pair + 1][rows, lanes]], 1)
            )
        lanes = slice(32 * to_z, 32 * to_z + 32)
        block.append(jnp.concatenate([total[:, lanes], jnp.zeros((8, 96), F32)], 1))
        block = jnp.concatenate(block, 0)
        for across in range(4):
            ahead = (to_z ^ z) == across
            outs[across][...] = jnp.where(ahead, block, outs[across][...]) if to_z else block


def last_kernel(spot, near, core_in, z_in, both_in, g_out, p_out, n_out):
    mine = near[...] + z_in[...]
    theirs = core_in[...] + both_in[...]
    swap = spot[2] == 1
    shares = (jnp.where(swap, theirs, mine), jnp.where(swap, mine, theirs))
    for core in range(2):
        for side in range(2):
            lanes = slice(256 * core + 128 * side, 256 * core + 128 * side + 128)
            g_out[:, lanes] = shares[core][24 * side : 24 * side + 24]
    for member in range(4):
        rows = slice(48 + 8 * (member // 2), 56 + 8 * (member // 2))
        lanes = slice(64 * (member % 2), 64 * (member % 2) + 64)
        p_out[:, 128 * member : 128 * member + 128] = jnp.concatenate(
            [share[rows, lanes] for share in shares], 1
        )
    n_out[...] = (mine[64:] + theirs[64:]).T[:2]


def upper_rows(row):
    return (lax.broadcasted_iota(jnp.int32, (4, 8, C), 1) < 4) != (row == 1)


def merge_kernel(
    spot, inputs, upstream, mine_high, mine_low, other_high, other_low, output, grad_inputs
):
    upper = upper_rows(spot[4])
    for array, (source, out) in enumerate(((inputs, output), (upstream, grad_inputs))):
        for start, other, mine in ((4, other_high, mine_high), (0, other_low, mine_low)):
            rows = source[start : start + 4].astype(F32)
            from_other = other[array].astype(F32)
            from_mine = mine[array].astype(F32)
            first = rows[:, :8] + jnp.where(upper, from_other, from_mine)
            second = rows[:, 8:] + jnp.where(upper, from_mine, from_other)
            out[start : start + 4] = jnp.concatenate([first, second], 1).astype(BF16)


def token_kernel(
    spot, r0, r1, r2, r3, own0, own1, w_qkv, w_proj, norm, out
):
    x = spot[0]
    projected = jnp.zeros((SLAB, C), F32)
    d_normed = jnp.zeros((SLAB, C), F32)
    for across, r_ref in enumerate((r0, r1, r2, r3)):
        rows = r_ref[...]
        member = x ^ across
        start = pl.multiple_of(OWN * member, OWN)
        projected += dot(rows[:, 3 * OWN :], w_proj[pl.ds(start, OWN), :])
        for third in range(3):
            lanes = slice(third * OWN, (third + 1) * OWN)
            columns = w_qkv[:, pl.ds(pl.multiple_of(start + C * third, OWN), OWN)]
            d_normed += dot_nt(rows[:, lanes], columns)
    out[0] = projected.astype(BF16)
    unit, inv_scale = unit_of(jnp.concatenate([own0[0], own1[0]], 0))
    d_unit = d_normed * norm[0:1, :]
    first_mean = jnp.mean(d_unit, -1, keepdims=True)
    second_mean = jnp.mean(d_unit * unit, -1, keepdims=True)
    out[1] = (inv_scale * (d_unit - first_mean - unit * second_mean)).astype(BF16)


def call(kernel, scalars, arrays, outs, scratch=(), flops=0, moved=0):
    smem = pl.BlockSpec(memory_space=pltpu.SMEM)
    vmem = pl.BlockSpec(memory_space=pltpu.VMEM)
    return pl.pallas_call(
        kernel,
        out_shape=[jax.ShapeDtypeStruct(shape, dtype) for shape, dtype in outs],
        in_specs=[smem] + [vmem] * len(arrays),
        out_specs=[vmem] * len(outs),
        scratch_shapes=list(scratch),
        compiler_params=pltpu.CompilerParams(vmem_limit_bytes=8 * 2**20),
        cost_estimate=pl.CostEstimate(flops=flops, bytes_accessed=moved, transcendentals=0),
        name=kernel.__name__,
    )(scalars, *arrays)


def on_device(inputs, norm_params, w_qkv, w_proj, upstream):
    place = lax.axis_index("wide")
    column = lax.axis_index("narrow")
    x, y, z = place % 4, place // 4 % 4, place // 16
    core = column % 2
    row = 1 - y % 2
    window = (place - 4) % 64 // 8
    spot = jnp.stack([x, y, core, z, row]).astype(jnp.int32)
    flags = jnp.stack([4 * (window == 7), 2 * (column == 3), row, x]).astype(jnp.int32)

    own_inputs, own_upstream = inputs[0, 0], upstream[0, 0]
    upper_y = (jnp.arange(8)[:, None] < 4) != (row == 1)
    both = jnp.stack([own_inputs, own_upstream]).reshape(2, 8, 2, 8, C)
    mine = jnp.where(upper_y, both[:, :, 1], both[:, :, 0])
    other = jnp.where(upper_y, both[:, :, 0], both[:, :, 1])
    lower_in = move(mine[:, :4], lambda p, n: (p, n - 1))
    other_in = move(other[:, 4:], lambda p, n: (partner_of(p), n))
    cross_in = move(other[:, :4], lambda p, n: (partner_of(p), n - 1))

    part0 = jnp.stack([mine[:, 4:], lower_in], 1).reshape(2, SLAB // 2, C)
    parts0 = [part0] + [move(part0, across_x(mask)) for mask in (1, 2, 3)]
    part1 = jnp.stack([other_in, cross_in], 1).reshape(2, SLAB // 2, C)
    half = TOKENS // 2
    normed0, qkv0, up0 = call(
        first_kernel,
        flags,
        (*parts0, norm_params, w_qkv, w_proj),
        [((half, C), BF16), ((half, 3 * OWN), BF16), ((half, OWN), BF16)],
        flops=10_000_000_000,
        moved=3_000_000,
    )
    shares = call(
        keeper_kernel,
        flags,
        (part1, norm_params, w_qkv, w_proj),
        [((SLAB // 2, C), BF16)] * 4,
        flops=300_000_000,
        moved=3_000_000,
    )
    shares = [shares[0]] + [move(shares[mask], across_x(mask)) for mask in (1, 2, 3)]
    part1, normed0 = lax.optimization_barrier((part1, normed0))
    parts1 = [part1] + [move(part1, across_x(mask)) for mask in (1, 2, 3)]
    r0, r1, r2, r3, d_t, a_t = call(
        attention_kernel,
        flags,
        (*shares, qkv0, up0),
        [((SLAB, C), BF16)] * 4 + [((3 * OWN, TOKENS), F32), ((OWN, TOKENS), BF16)],
        flops=1_200_000_000,
        moved=6_000_000,
    )

    returned = [r0] + [move(rows, across_x(mask)) for mask, rows in ((1, r1), (2, r2), (3, r3))]
    keep, send = call(
        gradient_kernel,
        spot,
        (*parts0, *parts1, r0, r1, r2, r3, d_t, a_t, normed0, norm_params, w_qkv),
        [((16, 72, 128), F32)] * 2,
        scratch=[
            pltpu.VMEM((3 * OWN, C), F32),
            pltpu.VMEM((C, OWN), F32),
            pltpu.VMEM((C, 128), F32),
        ],
        flops=20_000_000_000,
        moved=6_000_000,
    )
    received = move(send, across_narrow(1))
    blocks = [slice(4 * mask, 4 * mask + 4) for mask in range(4)]
    halves = [keep[block] + received[block] for block in blocks]
    from_y = [halves[0]] + [move(halves[mask], across_y(mask)) for mask in (1, 2, 3)]
    (back,) = call(
        token_kernel,
        spot,
        (*returned, part0, part1, w_qkv, w_proj, norm_params),
        [((2, SLAB, C), BF16)],
        flops=500_000_000,
        moved=4_000_000,
    )
    from_y[1], from_y[2], from_y[3], back = lax.optimization_barrier(
        (from_y[1], from_y[2], from_y[3], back)
    )
    back = back.reshape(2, 4, 4, 8, C)
    crossed = move(back[:, 2:], lambda p, n: (partner_of(p), n))

    share = ((72, 128), F32)
    x_parts = call(x_parts_kernel, spot, from_y, [share] * 4)
    from_x = [x_parts[0]] + [move(x_parts[mask], across_x(mask)) for mask in (1, 2, 3)]
    z_parts = call(z_parts_kernel, spot, from_x, [share] * 4)
    line = [z_parts[0]] + [move(z_parts[mask], across_z(mask)) for mask in (1, 2, 3)]
    line[1], line[2], line[3], crossed = lax.optimization_barrier(
        (line[1], line[2], line[3], crossed)
    )
    low = move(jnp.stack([back[:, 1], crossed[:, 1]], 1), lambda p, n: (p, n + 1))
    line = (line[0] + line[1]) + (line[2] + line[3])
    last = [line] + [move(line, across_narrow(mask)) for mask in (1, 2, 3)]
    output, grad_inputs = call(
        merge_kernel,
        spot,
        (own_inputs, own_upstream, back[:, 0], low[:, 0], crossed[:, 0], low[:, 1]),
        [((8, 16, C), BF16)] * 2,
    )
    last[1], last[2], last[3], output, grad_inputs = lax.optimization_barrier(
        (last[1], last[2], last[3], output, grad_inputs)
    )
    grad_qkv, grad_proj, grad_norm = call(
        last_kernel, spot, last, [((24, C), F32), ((8, C), F32), ((2, 8), F32)]
    )
    return (
        output[None, None], grad_inputs[None, None], grad_qkv.T, grad_proj.T, grad_norm
    )


def solution(mesh):
    in_specs = (
        P(None, "wide", "narrow", None, None),
        P(),
        P(),
        P(),
        P(None, "wide", "narrow", None, None),
    )
    out_specs = (
        P(None, "wide", "narrow", None, None),
        P(None, "wide", "narrow", None, None),
        P(None, "wide"),
        P(None, "wide"),
        P(None, "wide"),
    )
    return jax.shard_map(
        on_device, mesh=mesh, in_specs=in_specs, out_specs=out_specs, check_vma=False
    )
```

```python
import jax
import jax.numpy as jnp
from jax import lax
from jax.experimental import pallas as pl
from jax.experimental.pallas import tpu as pltpu
from jax.sharding import PartitionSpec as P

HEADS = 16
HEAD_DIM = 32
C = 512
WIN = 8
RING = 4
OWN = C // RING
SLAB = 128
TOKENS = RING * SLAB
BLOCK = 256
CHUNK = 64
SCALE = HEAD_DIM**-0.5
LOG2E = 1.4426950408889634
F32 = jnp.float32
BF16 = jnp.bfloat16


def move(value, target):
    pairs = []
    for place in range(64):
        for column in range(4):
            to_place, to_column = target(place, column)
            pairs.append((place * 4 + column, (to_place % 64) * 4 + to_column % 4))
    return lax.ppermute(value, ("wide", "narrow"), pairs)


def partner_of(place):
    return place + 4 if (place // 4) % 2 else place - 4


def across_x(mask):
    return lambda p, n: (p ^ mask, n)


def across_y(mask):
    return lambda p, n: (p ^ (4 * mask), n)


def across_z(mask):
    return lambda p, n: (p ^ (16 * mask), n)


def across_narrow(mask):
    return lambda p, n: (p, n ^ mask)


def dot(a, b):
    return lax.dot_general(a, b, (((1,), (0,)), ((), ())), preferred_element_type=F32)


def dot_nt(a, b):
    return lax.dot_general(a, b, (((1,), (1,)), ((), ())), preferred_element_type=F32)


def unit_of(rows):
    floats = rows.astype(F32)
    average = jnp.mean(floats, -1, keepdims=True)
    centered = floats - average
    variance = jnp.mean(centered * centered, -1, keepdims=True)
    inv_scale = lax.rsqrt(variance + 1e-05)
    return centered * inv_scale, inv_scale


def two_terms(value):
    high = value.astype(BF16)
    low = (value - high.astype(F32)).astype(BF16)
    return high, low


def own_columns(w_qkv, x):
    start = pl.multiple_of(OWN * x, OWN)
    return jnp.concatenate(
        [w_qkv[:, pl.ds(pl.multiple_of(start + C * third, OWN), OWN)] for third in range(3)], 1
    )


def project(parts, norm, w_qkv, w_proj, member):
    unit, _ = unit_of(jnp.concatenate([part[0] for part in parts], 0))
    normed = (unit * norm[0:1, :] + norm[1:2, :]).astype(BF16)
    qkv = dot(normed, own_columns(w_qkv, member)).astype(BF16)
    rows = w_proj[pl.ds(pl.multiple_of(OWN * member, OWN), OWN), :]
    cotangent = dot_nt(jnp.concatenate([part[1] for part in parts], 0), rows).astype(BF16)
    return normed, qkv, cotangent


def first_kernel(flags, p0, p1, p2, p3, norm, w_qkv, w_proj, normed_ref, qkv_ref, up_ref):
    normed_ref[...], qkv_ref[...], up_ref[...] = project(
        (p0, p1, p2, p3), norm, w_qkv, w_proj, flags[3]
    )


def attention_kernel(
    flags, p0, p1, p2, p3, normed0, qkv0, up0, norm, w_qkv, w_proj,
    r0, r1, r2, r3, dt_ref, at_ref, normed1,
):
    normed1[...], qkv1, up1 = project((p0, p1, p2, p3), norm, w_qkv, w_proj, flags[3])
    qkv = jnp.concatenate([qkv0[...], qkv1], 0)
    cotangent = jnp.concatenate([up0[...], up1], 0)
    queries = qkv[:, :OWN]
    keys = qkv[:, OWN : 2 * OWN]
    values = qkv[:, 2 * OWN :]
    queries_t = queries.T
    cotangent_t = cotangent.T
    keys_t = keys.T
    values_t = values.T
    head_of_lane = lax.broadcasted_iota(jnp.int32, (TOKENS, OWN), 1) // HEAD_DIM

    def label(shape, dim):
        token = lax.broadcasted_iota(jnp.int32, shape, dim)
        row = token // 256
        half = (token // 32) % 2
        low_y = (token // 4) % 2
        return row * flags[0] + half * flags[1] + low_y * flags[2]

    key_label = label((TOKENS, 1), 0)
    query_label = label((1, TOKENS), 1)
    d_key = jnp.zeros((TOKENS, OWN), F32)
    d_value = jnp.zeros((TOKENS, OWN), F32)
    for block in range(TOKENS // BLOCK):
        span = slice(block * BLOCK, (block + 1) * BLOCK)
        allowed = key_label == query_label[:, span]
        for head in range(RING):
            chosen = head_of_lane == head
            rows = slice(head * HEAD_DIM, (head + 1) * HEAD_DIM)
            key_head = jnp.where(chosen, keys, jnp.zeros_like(keys))
            value_head = jnp.where(chosen, values, jnp.zeros_like(values))
            scores = jnp.where(allowed, dot(key_head, queries_t[:, span]), -1e30)
            highest = jnp.max(scores, 0, keepdims=True)
            d_probs = dot(value_head, cotangent_t[:, span])
            weights = []
            total = jnp.zeros((8, BLOCK), F32)
            inner = jnp.zeros((8, BLOCK), F32)
            for start in range(0, TOKENS, CHUNK):
                part = slice(start, start + CHUNK)
                weight = jnp.exp2((scores[part] - highest) * (SCALE * LOG2E))
                total += jnp.sum(weight.reshape(CHUNK // 8, 8, BLOCK), 0)
                inner += jnp.sum((weight * d_probs[part]).reshape(CHUNK // 8, 8, BLOCK), 0)
                weights.append(weight)
            over = 1.0 / jnp.sum(total, 0, keepdims=True)
            inner = jnp.sum(inner, 0, keepdims=True) * over
            over_scaled = over * SCALE
            probs_low, d_scores = [], []
            for index, weight in enumerate(weights):
                part = slice(index * CHUNK, (index + 1) * CHUNK)
                probs_low.append((weight * over).astype(BF16))
                d_scores.append(((weight * over_scaled) * (d_probs[part] - inner)).astype(BF16))
            probs_low = jnp.concatenate(probs_low, 0)
            d_scores = jnp.concatenate(d_scores, 0)
            at_ref[rows, span] = dot(values_t[rows], probs_low).astype(BF16)
            dt_ref[rows, span] = dot(keys_t[rows], d_scores)
            query_head = jnp.where(chosen[span], queries[span], jnp.zeros_like(queries[span]))
            cotangent_head = jnp.where(
                chosen[span], cotangent[span], jnp.zeros_like(cotangent[span])
            )
            d_key += dot(d_scores, query_head)
            d_value += dot(probs_low, cotangent_head)
    dt_ref[OWN : 2 * OWN, :] = d_key.T
    dt_ref[2 * OWN :, :] = d_value.T
    d_query = dt_ref[:OWN, :].T.astype(BF16)
    attended = at_ref[...].T
    for member, r_ref in enumerate((r0, r1, r2, r3)):
        for part in range(2):
            rows = slice(256 * part + 64 * member, 256 * part + 64 * member + 64)
            to = slice(64 * part, 64 * part + 64)
            r_ref[to, :OWN] = d_query[rows]
            r_ref[to, OWN : 2 * OWN] = d_key[rows].astype(BF16)
            r_ref[to, 2 * OWN : 3 * OWN] = d_value[rows].astype(BF16)
            r_ref[to, 3 * OWN :] = attended[rows]


def gradient_kernel(
    spot, p0, p1, p2, p3, p4, p5, p6, p7, r0, r1, r2, r3, dt_ref, at_ref, normed0, normed1, w_qkv,
    keep, send, g_ref, p_ref, n_ref,
):
    x, y, core = spot[0], spot[1], spot[2]
    parts = (p0, p1, p2, p3, p4, p5, p6, p7)
    d_high, d_low = two_terms(dt_ref[...])
    normed = jnp.concatenate([normed0[...], normed1[...]], 0)
    g_ref[...] = dot(d_high, normed) + dot(d_low, normed)
    p_ref[...] = dot(at_ref[...], jnp.concatenate([part[1] for part in parts], 0)).T
    columns = own_columns(w_qkv, x)
    gain_row = jnp.zeros((1, C), F32)
    offset_row = jnp.zeros((1, C), F32)
    for member, r_ref in enumerate((r0, r1, r2, r3)):
        rows = jnp.concatenate([parts[member][0], parts[4 + member][0]], 0)
        d_normed = dot_nt(r_ref[:, : 3 * OWN], columns)
        gain_row += jnp.sum(d_normed * unit_of(rows)[0], 0, keepdims=True)
        offset_row += jnp.sum(d_normed, 0, keepdims=True)
    row = lax.broadcasted_iota(jnp.int32, (128, C), 0)
    n_ref[...] = jnp.where(row == 0, gain_row, jnp.where(row == 1, offset_row, 0.0)).T
    for ahead, out in ((0, keep), (1, send)):
        to_core = core if ahead == 0 else 1 - core
        for across in range(4):
            to_y = y ^ across
            for to_x in range(4):
                block = 4 * across + to_x
                for side in range(2):
                    lanes = pl.ds(pl.multiple_of(256 * to_core + 128 * side, 128), 128)
                    for slot in range(3):
                        residue = 12 * to_y + 3 * to_x + slot
                        third_of = lax.rem(residue // 16 - x + 6, 3)
                        start = pl.multiple_of(128 * third_of + 8 * lax.rem(residue, 16), 8)
                        top = 24 * side + 8 * slot
                        out[block, top : top + 8, :] = g_ref[pl.ds(start, 8), lanes]
                for z in range(4):
                    rows = pl.ds(pl.multiple_of(128 * z + 32 * to_y + 8 * to_x, 8), 8)
                    piece = p_ref[rows, :]
                    top = 48 + 8 * (z // 2)
                    out[block, top : top + 8, 64 * (z % 2) : 64 * (z % 2) + 64] = jnp.where(
                        to_core == 0, piece[:, :64], piece[:, 64:]
                    )
                    if ahead == 0:
                        out[block, 64:, 32 * z : 32 * z + 32] = n_ref[rows, :32]
                if ahead == 1:
                    out[block, 64:, :] = jnp.zeros((8, 128), F32)


def x_parts_kernel(spot, s0, s1, s2, s3, *outs):
    x = spot[0]
    for across, out in enumerate(outs):
        to_x = x ^ across
        out[...] = (s0[to_x] + s1[to_x]) + (s2[to_x] + s3[to_x])


def z_parts_kernel(spot, m0, m1, m2, m3, *outs):
    x, y, z = spot[0], spot[1], spot[3]
    pieces = (m0, m1, m2, m3)

    def from_member(member, rows):
        across = member ^ x
        picked = pieces[0][rows, :]
        for index in range(1, 4):
            picked = jnp.where(across == index, pieces[index][rows, :], picked)
        return picked

    total = (m0[64:, :] + m1[64:, :]) + (m2[64:, :] + m3[64:, :])
    proj = [from_member(member, slice(48, 64)) for member in range(4)]
    for to_z in range(4):
        block = []
        for side in range(2):
            for slot in range(3):
                owner = lax.rem(48 * to_z + 12 * y + 3 * x + slot, 64) // 16
                top = 24 * side + 8 * slot
                block.append(from_member(owner, slice(top, top + 8)))
        rows = slice(8 * (to_z // 2), 8 * (to_z // 2) + 8)
        lanes = slice(64 * (to_z % 2), 64 * (to_z % 2) + 64)
        for pair in range(2):
            block.append(
                jnp.concatenate([proj[2 * pair][rows, lanes], proj[2 * pair + 1][rows, lanes]], 1)
            )
        lanes = slice(32 * to_z, 32 * to_z + 32)
        block.append(jnp.concatenate([total[:, lanes], jnp.zeros((8, 96), F32)], 1))
        block = jnp.concatenate(block, 0)
        for across in range(4):
            ahead = (to_z ^ z) == across
            outs[across][...] = jnp.where(ahead, block, outs[across][...]) if to_z else block


def last_kernel(spot, near, core_in, z_in, both_in, g_out, p_out, n_out):
    mine = near[...] + z_in[...]
    theirs = core_in[...] + both_in[...]
    swap = spot[2] == 1
    shares = (jnp.where(swap, theirs, mine), jnp.where(swap, mine, theirs))
    for core in range(2):
        for side in range(2):
            lanes = slice(256 * core + 128 * side, 256 * core + 128 * side + 128)
            g_out[:, lanes] = shares[core][24 * side : 24 * side + 24]
    for member in range(4):
        rows = slice(48 + 8 * (member // 2), 56 + 8 * (member // 2))
        lanes = slice(64 * (member % 2), 64 * (member % 2) + 64)
        p_out[:, 128 * member : 128 * member + 128] = jnp.concatenate(
            [share[rows, lanes] for share in shares], 1
        )
    n_out[...] = (mine[64:] + theirs[64:]).T[:2]


def upper_rows(row):
    return (lax.broadcasted_iota(jnp.int32, (4, 8, C), 1) < 4) != (row == 1)


def merge_kernel(
    spot, inputs, upstream, mine_high, mine_low, other_high, other_low, output, grad_inputs
):
    upper = upper_rows(spot[4])
    for array, (source, out) in enumerate(((inputs, output), (upstream, grad_inputs))):
        for start, other, mine in ((4, other_high, mine_high), (0, other_low, mine_low)):
            rows = source[start : start + 4].astype(F32)
            from_other = other[array].astype(F32)
            from_mine = mine[array].astype(F32)
            first = rows[:, :8] + jnp.where(upper, from_other, from_mine)
            second = rows[:, 8:] + jnp.where(upper, from_mine, from_other)
            out[start : start + 4] = jnp.concatenate([first, second], 1).astype(BF16)


def token_kernel(
    spot, r0, r1, r2, r3, own0, own1, w_qkv, w_proj, norm, out
):
    x = spot[0]
    projected = jnp.zeros((SLAB, C), F32)
    d_normed = jnp.zeros((SLAB, C), F32)
    for across, r_ref in enumerate((r0, r1, r2, r3)):
        rows = r_ref[...]
        member = x ^ across
        start = pl.multiple_of(OWN * member, OWN)
        projected += dot(rows[:, 3 * OWN :], w_proj[pl.ds(start, OWN), :])
        for third in range(3):
            lanes = slice(third * OWN, (third + 1) * OWN)
            columns = w_qkv[:, pl.ds(pl.multiple_of(start + C * third, OWN), OWN)]
            d_normed += dot_nt(rows[:, lanes], columns)
    out[0] = projected.astype(BF16)
    unit, inv_scale = unit_of(jnp.concatenate([own0[0], own1[0]], 0))
    d_unit = d_normed * norm[0:1, :]
    first_mean = jnp.mean(d_unit, -1, keepdims=True)
    second_mean = jnp.mean(d_unit * unit, -1, keepdims=True)
    out[1] = (inv_scale * (d_unit - first_mean - unit * second_mean)).astype(BF16)


def call(kernel, scalars, arrays, outs, scratch=(), flops=0, moved=0):
    smem = pl.BlockSpec(memory_space=pltpu.SMEM)
    vmem = pl.BlockSpec(memory_space=pltpu.VMEM)
    return pl.pallas_call(
        kernel,
        out_shape=[jax.ShapeDtypeStruct(shape, dtype) for shape, dtype in outs],
        in_specs=[smem] + [vmem] * len(arrays),
        out_specs=[vmem] * len(outs),
        scratch_shapes=list(scratch),
        compiler_params=pltpu.CompilerParams(vmem_limit_bytes=8 * 2**20),
        cost_estimate=pl.CostEstimate(flops=flops, bytes_accessed=moved, transcendentals=0),
        name=kernel.__name__,
    )(scalars, *arrays)


def on_device(inputs, norm_params, w_qkv, w_proj, upstream):
    place = lax.axis_index("wide")
    column = lax.axis_index("narrow")
    x, y, z = place % 4, place // 4 % 4, place // 16
    core = column % 2
    row = 1 - y % 2
    window = (place - 4) % 64 // 8
    spot = jnp.stack([x, y, core, z, row]).astype(jnp.int32)
    flags = jnp.stack([4 * (window == 7), 2 * (column == 3), row, x]).astype(jnp.int32)

    own_inputs, own_upstream = inputs[0, 0], upstream[0, 0]
    upper_y = (jnp.arange(8)[:, None] < 4) != (row == 1)
    both = jnp.stack([own_inputs, own_upstream]).reshape(2, 8, 2, 8, C)
    mine = jnp.where(upper_y, both[:, :, 1], both[:, :, 0])
    other = jnp.where(upper_y, both[:, :, 0], both[:, :, 1])
    lower_in = move(mine[:, :4], lambda p, n: (p, n - 1))
    other_in = move(other[:, 4:], lambda p, n: (partner_of(p), n))
    cross_in = move(other[:, :4], lambda p, n: (partner_of(p), n - 1))

    part0 = jnp.stack([mine[:, 4:], lower_in], 1).reshape(2, SLAB // 2, C)
    parts0 = [part0] + [move(part0, across_x(mask)) for mask in (1, 2, 3)]
    part1 = jnp.stack([other_in, cross_in], 1).reshape(2, SLAB // 2, C)
    parts1 = [part1] + [move(part1, across_x(mask)) for mask in (1, 2, 3)]
    half = TOKENS // 2
    normed0, qkv0, up0 = call(
        first_kernel,
        flags,
        (*parts0, norm_params, w_qkv, w_proj),
        [((half, C), BF16), ((half, 3 * OWN), BF16), ((half, OWN), BF16)],
        flops=10_000_000_000,
        moved=3_000_000,
    )
    r0, r1, r2, r3, d_t, a_t, normed1 = call(
        attention_kernel,
        flags,
        (*parts1, normed0, qkv0, up0, norm_params, w_qkv, w_proj),
        [((SLAB, C), BF16)] * 4
        + [((3 * OWN, TOKENS), F32), ((OWN, TOKENS), BF16), ((half, C), BF16)],
        flops=1_200_000_000,
        moved=6_000_000,
    )

    keep, send = call(
        gradient_kernel,
        spot,
        (*parts0, *parts1, r0, r1, r2, r3, d_t, a_t, normed0, normed1, w_qkv),
        [((16, 72, 128), F32)] * 2,
        scratch=[
            pltpu.VMEM((3 * OWN, C), F32),
            pltpu.VMEM((C, OWN), F32),
            pltpu.VMEM((C, 128), F32),
        ],
        flops=20_000_000_000,
        moved=6_000_000,
    )
    received = move(send, across_narrow(1))
    blocks = [slice(4 * mask, 4 * mask + 4) for mask in range(4)]
    halves = [keep[block] + received[block] for block in blocks]
    *halves, late2, late3 = lax.optimization_barrier((*halves, r2, r3))
    from_y = [halves[0]] + [move(halves[mask], across_y(mask)) for mask in (1, 2, 3)]
    returned = [r0] + [
        move(rows, across_x(mask)) for mask, rows in ((1, r1), (2, late2), (3, late3))
    ]
    (back,) = call(
        token_kernel,
        spot,
        (*returned, part0, part1, w_qkv, w_proj, norm_params),
        [((2, SLAB, C), BF16)],
        flops=500_000_000,
        moved=4_000_000,
    )
    share = ((72, 128), F32)
    x_parts = call(x_parts_kernel, spot, from_y, [share] * 4)
    from_x = [x_parts[0]] + [move(x_parts[mask], across_x(mask)) for mask in (1, 2, 3)]
    from_x[1], from_x[2], from_x[3], back = lax.optimization_barrier(
        (from_x[1], from_x[2], from_x[3], back)
    )
    back = back.reshape(2, 2, 2, 4, 8, C)
    low = move(back[:, :, 1], lambda p, n: (p, n + 1))
    z_parts = call(z_parts_kernel, spot, from_x, [share] * 4)
    *z_parts, low = lax.optimization_barrier((*z_parts, low))
    crossed = move(jnp.stack([back[:, 1, 0], low[:, 1]], 1), lambda p, n: (partner_of(p), n))
    line = [z_parts[0]] + [move(z_parts[mask], across_z(mask)) for mask in (1, 2, 3)]
    line[1], line[2], line[3], crossed = lax.optimization_barrier(
        (line[1], line[2], line[3], crossed)
    )
    line = (line[0] + line[1]) + (line[2] + line[3])
    last = [line] + [move(line, across_narrow(mask)) for mask in (1, 2, 3)]
    output, grad_inputs = call(
        merge_kernel,
        spot,
        (own_inputs, own_upstream, back[:, 0, 0], low[:, 0], crossed[:, 0], crossed[:, 1]),
        [((8, 16, C), BF16)] * 2,
    )
    last[1], last[2], last[3], output, grad_inputs = lax.optimization_barrier(
        (last[1], last[2], last[3], output, grad_inputs)
    )
    grad_qkv, grad_proj, grad_norm = call(
        last_kernel, spot, last, [((24, C), F32), ((8, C), F32), ((2, 8), F32)]
    )
    return (
        output[None, None], grad_inputs[None, None], grad_qkv.T, grad_proj.T, grad_norm
    )


def solution(mesh):
    in_specs = (
        P(None, "wide", "narrow", None, None),
        P(),
        P(),
        P(),
        P(None, "wide", "narrow", None, None),
    )
    out_specs = (
        P(None, "wide", "narrow", None, None),
        P(None, "wide", "narrow", None, None),
        P(None, "wide"),
        P(None, "wide"),
        P(None, "wide"),
    )
    return jax.shard_map(
        on_device, mesh=mesh, in_specs=in_specs, out_specs=out_specs, check_vma=False
    )
```

```python
import jax
import jax.numpy as jnp
from jax import lax
from jax.experimental import pallas as pl
from jax.experimental.pallas import tpu as pltpu
from jax.sharding import PartitionSpec as P

HEADS = 16
HEAD_DIM = 32
C = 512
WIN = 8
RING = 4
OWN = C // RING
SLAB = 128
TOKENS = RING * SLAB
BLOCK = 256
CHUNK = 64
SCALE = HEAD_DIM**-0.5
LOG2E = 1.4426950408889634
F32 = jnp.float32
BF16 = jnp.bfloat16


def move(value, target):
    pairs = []
    for place in range(64):
        for column in range(4):
            to_place, to_column = target(place, column)
            pairs.append((place * 4 + column, (to_place % 64) * 4 + to_column % 4))
    return lax.ppermute(value, ("wide", "narrow"), pairs)


def partner_of(place):
    return place + 4 if (place // 4) % 2 else place - 4


def across_x(mask):
    return lambda p, n: (p ^ mask, n)


def across_y(mask):
    return lambda p, n: (p ^ (4 * mask), n)


def across_z(mask):
    return lambda p, n: (p ^ (16 * mask), n)


def across_narrow(mask):
    return lambda p, n: (p, n ^ mask)


def index_of(z, y, x, column):
    return (16 * z + 4 * y + x) * 4 + column


X_GROUPS = [
    [index_of(z, y, x, n) for x in range(4)] for z in range(4) for y in range(4) for n in range(4)
]
Z_GROUPS = [
    [index_of(z, y, x, n) for z in range(4)] for y in range(4) for x in range(4) for n in range(4)
]


def exchange(value, groups):
    return lax.all_to_all(value, ("wide", "narrow"), 0, 0, axis_index_groups=groups)


def dot(a, b):
    return lax.dot_general(a, b, (((1,), (0,)), ((), ())), preferred_element_type=F32)


def dot_nt(a, b):
    return lax.dot_general(a, b, (((1,), (1,)), ((), ())), preferred_element_type=F32)


def unit_of(rows):
    floats = rows.astype(F32)
    average = jnp.mean(floats, -1, keepdims=True)
    centered = floats - average
    variance = jnp.mean(centered * centered, -1, keepdims=True)
    inv_scale = lax.rsqrt(variance + 1e-05)
    return centered * inv_scale, inv_scale


def two_terms(value):
    high = value.astype(BF16)
    low = (value - high.astype(F32)).astype(BF16)
    return high, low


def own_columns(w_qkv, x):
    start = pl.multiple_of(OWN * x, OWN)
    return jnp.concatenate(
        [w_qkv[:, pl.ds(pl.multiple_of(start + C * third, OWN), OWN)] for third in range(3)], 1
    )


def project(parts, norm, w_qkv, w_proj, member):
    unit, _ = unit_of(jnp.concatenate([part[0] for part in parts], 0))
    normed = (unit * norm[0:1, :] + norm[1:2, :]).astype(BF16)
    qkv = dot(normed, own_columns(w_qkv, member)).astype(BF16)
    rows = w_proj[pl.ds(pl.multiple_of(OWN * member, OWN), OWN), :]
    cotangent = dot_nt(jnp.concatenate([part[1] for part in parts], 0), rows).astype(BF16)
    return normed, qkv, cotangent


def first_kernel(flags, p0, p1, p2, p3, norm, w_qkv, w_proj, normed_ref, qkv_ref, up_ref):
    normed_ref[...], qkv_ref[...], up_ref[...] = project(
        (p0, p1, p2, p3), norm, w_qkv, w_proj, flags[3]
    )


def attention_kernel(
    flags, p0, p1, p2, p3, normed0, qkv0, up0, norm, w_qkv, w_proj,
    r0, r1, r2, r3, dt_ref, at_ref, normed1,
):
    normed1[...], qkv1, up1 = project((p0, p1, p2, p3), norm, w_qkv, w_proj, flags[3])
    qkv = jnp.concatenate([qkv0[...], qkv1], 0)
    cotangent = jnp.concatenate([up0[...], up1], 0)
    queries = qkv[:, :OWN]
    keys = qkv[:, OWN : 2 * OWN]
    values = qkv[:, 2 * OWN :]
    queries_t = queries.T
    cotangent_t = cotangent.T
    keys_t = keys.T
    values_t = values.T
    head_of_lane = lax.broadcasted_iota(jnp.int32, (TOKENS, OWN), 1) // HEAD_DIM

    def label(shape, dim):
        token = lax.broadcasted_iota(jnp.int32, shape, dim)
        row = token // 256
        half = (token // 32) % 2
        low_y = (token // 4) % 2
        return row * flags[0] + half * flags[1] + low_y * flags[2]

    key_label = label((TOKENS, 1), 0)
    query_label = label((1, TOKENS), 1)
    d_key = jnp.zeros((TOKENS, OWN), F32)
    d_value = jnp.zeros((TOKENS, OWN), F32)
    for block in range(TOKENS // BLOCK):
        span = slice(block * BLOCK, (block + 1) * BLOCK)
        allowed = key_label == query_label[:, span]
        for head in range(RING):
            chosen = head_of_lane == head
            rows = slice(head * HEAD_DIM, (head + 1) * HEAD_DIM)
            key_head = jnp.where(chosen, keys, jnp.zeros_like(keys))
            value_head = jnp.where(chosen, values, jnp.zeros_like(values))
            scores = jnp.where(allowed, dot(key_head, queries_t[:, span]), -1e30)
            highest = jnp.max(scores, 0, keepdims=True)
            d_probs = dot(value_head, cotangent_t[:, span])
            weights = []
            total = jnp.zeros((8, BLOCK), F32)
            inner = jnp.zeros((8, BLOCK), F32)
            for start in range(0, TOKENS, CHUNK):
                part = slice(start, start + CHUNK)
                weight = jnp.exp2((scores[part] - highest) * (SCALE * LOG2E))
                total += jnp.sum(weight.reshape(CHUNK // 8, 8, BLOCK), 0)
                inner += jnp.sum((weight * d_probs[part]).reshape(CHUNK // 8, 8, BLOCK), 0)
                weights.append(weight)
            over = 1.0 / jnp.sum(total, 0, keepdims=True)
            inner = jnp.sum(inner, 0, keepdims=True) * over
            over_scaled = over * SCALE
            probs_low, d_scores = [], []
            for index, weight in enumerate(weights):
                part = slice(index * CHUNK, (index + 1) * CHUNK)
                probs_low.append((weight * over).astype(BF16))
                d_scores.append(((weight * over_scaled) * (d_probs[part] - inner)).astype(BF16))
            probs_low = jnp.concatenate(probs_low, 0)
            d_scores = jnp.concatenate(d_scores, 0)
            at_ref[rows, span] = dot(values_t[rows], probs_low).astype(BF16)
            dt_ref[rows, span] = dot(keys_t[rows], d_scores)
            query_head = jnp.where(chosen[span], queries[span], jnp.zeros_like(queries[span]))
            cotangent_head = jnp.where(
                chosen[span], cotangent[span], jnp.zeros_like(cotangent[span])
            )
            d_key += dot(d_scores, query_head)
            d_value += dot(probs_low, cotangent_head)
    dt_ref[OWN : 2 * OWN, :] = d_key.T
    dt_ref[2 * OWN :, :] = d_value.T
    d_query = dt_ref[:OWN, :].T.astype(BF16)
    attended = at_ref[...].T
    for member, r_ref in enumerate((r0, r1, r2, r3)):
        for part in range(2):
            rows = slice(256 * part + 64 * member, 256 * part + 64 * member + 64)
            to = slice(64 * part, 64 * part + 64)
            r_ref[to, :OWN] = d_query[rows]
            r_ref[to, OWN : 2 * OWN] = d_key[rows].astype(BF16)
            r_ref[to, 2 * OWN : 3 * OWN] = d_value[rows].astype(BF16)
            r_ref[to, 3 * OWN :] = attended[rows]


def gradient_kernel(
    spot, p0, p1, p2, p3, p4, p5, p6, p7, r0, r1, r2, r3, dt_ref, at_ref, normed0, normed1, w_qkv,
    keep, send, g_ref, p_ref, n_ref,
):
    x, y, core = spot[0], spot[1], spot[2]
    parts = (p0, p1, p2, p3, p4, p5, p6, p7)
    d_high, d_low = two_terms(dt_ref[...])
    normed = jnp.concatenate([normed0[...], normed1[...]], 0)
    g_ref[...] = dot(d_high, normed) + dot(d_low, normed)
    p_ref[...] = dot(at_ref[...], jnp.concatenate([part[1] for part in parts], 0)).T
    columns = own_columns(w_qkv, x)
    gain_row = jnp.zeros((1, C), F32)
    offset_row = jnp.zeros((1, C), F32)
    for member, r_ref in enumerate((r0, r1, r2, r3)):
        rows = jnp.concatenate([parts[member][0], parts[4 + member][0]], 0)
        d_normed = dot_nt(r_ref[:, : 3 * OWN], columns)
        gain_row += jnp.sum(d_normed * unit_of(rows)[0], 0, keepdims=True)
        offset_row += jnp.sum(d_normed, 0, keepdims=True)
    row = lax.broadcasted_iota(jnp.int32, (128, C), 0)
    n_ref[...] = jnp.where(row == 0, gain_row, jnp.where(row == 1, offset_row, 0.0)).T
    for ahead, out in ((0, keep), (1, send)):
        to_core = core if ahead == 0 else 1 - core
        for across in range(4):
            to_y = y ^ across
            for to_x in range(4):
                block = 4 * across + to_x
                for side in range(2):
                    lanes = pl.ds(pl.multiple_of(256 * to_core + 128 * side, 128), 128)
                    for slot in range(3):
                        residue = 12 * to_y + 3 * to_x + slot
                        third_of = lax.rem(residue // 16 - x + 6, 3)
                        start = pl.multiple_of(128 * third_of + 8 * lax.rem(residue, 16), 8)
                        top = 24 * side + 8 * slot
                        out[block, top : top + 8, :] = g_ref[pl.ds(start, 8), lanes]
                for z in range(4):
                    rows = pl.ds(pl.multiple_of(128 * z + 32 * to_y + 8 * to_x, 8), 8)
                    piece = p_ref[rows, :]
                    top = 48 + 8 * (z // 2)
                    out[block, top : top + 8, 64 * (z % 2) : 64 * (z % 2) + 64] = jnp.where(
                        to_core == 0, piece[:, :64], piece[:, 64:]
                    )
                    if ahead == 0:
                        out[block, 64:, 32 * z : 32 * z + 32] = n_ref[rows, :32]
                if ahead == 1:
                    out[block, 64:, :] = jnp.zeros((8, 128), F32)


def x_parts_kernel(spot, s0, s1, s2, s3, out):
    out[...] = (s0[...] + s1[...]) + (s2[...] + s3[...])


def z_parts_kernel(spot, pieces, out):
    x, y = spot[0], spot[1]
    total = (pieces[0, 64:] + pieces[1, 64:]) + (pieces[2, 64:] + pieces[3, 64:])
    for to_z in range(4):
        for side in range(2):
            for slot in range(3):
                owner = lax.rem(48 * to_z + 12 * y + 3 * x + slot, 64) // 16
                rows = slice(24 * side + 8 * slot, 24 * side + 8 * slot + 8)
                out[to_z, rows, :] = pieces[owner, rows, :]
        rows = slice(48 + 8 * (to_z // 2), 56 + 8 * (to_z // 2))
        lanes = slice(64 * (to_z % 2), 64 * (to_z % 2) + 64)
        for pair in range(2):
            out[to_z, 48 + 8 * pair : 56 + 8 * pair, :] = jnp.concatenate(
                [pieces[2 * pair, rows, lanes], pieces[2 * pair + 1, rows, lanes]], 1
            )
        lanes = slice(32 * to_z, 32 * to_z + 32)
        out[to_z, 64:, :] = jnp.concatenate([total[:, lanes], jnp.zeros((8, 96), F32)], 1)


def last_kernel(spot, near, core_in, z_in, both_in, g_out, p_out, n_out):
    mine = near[...] + z_in[...]
    theirs = core_in[...] + both_in[...]
    swap = spot[2] == 1
    shares = (jnp.where(swap, theirs, mine), jnp.where(swap, mine, theirs))
    for core in range(2):
        for side in range(2):
            lanes = slice(256 * core + 128 * side, 256 * core + 128 * side + 128)
            g_out[:, lanes] = shares[core][24 * side : 24 * side + 24]
    for member in range(4):
        rows = slice(48 + 8 * (member // 2), 56 + 8 * (member // 2))
        lanes = slice(64 * (member % 2), 64 * (member % 2) + 64)
        p_out[:, 128 * member : 128 * member + 128] = jnp.concatenate(
            [share[rows, lanes] for share in shares], 1
        )
    n_out[...] = (mine[64:] + theirs[64:]).T[:2]


def upper_rows(row):
    return (lax.broadcasted_iota(jnp.int32, (4, 8, C), 1) < 4) != (row == 1)


def merge_kernel(
    spot, inputs, upstream, mine_high, mine_low, other_high, other_low, output, grad_inputs
):
    upper = upper_rows(spot[4])
    for array, (source, out) in enumerate(((inputs, output), (upstream, grad_inputs))):
        for start, other, mine in ((4, other_high, mine_high), (0, other_low, mine_low)):
            rows = source[start : start + 4].astype(F32)
            from_other = other[array].astype(F32)
            from_mine = mine[array].astype(F32)
            first = rows[:, :8] + jnp.where(upper, from_other, from_mine)
            second = rows[:, 8:] + jnp.where(upper, from_mine, from_other)
            out[start : start + 4] = jnp.concatenate([first, second], 1).astype(BF16)


def token_kernel(
    spot, r0, r1, r2, r3, own0, own1, w_qkv, w_proj, norm, out
):
    x = spot[0]
    projected = jnp.zeros((SLAB, C), F32)
    d_normed = jnp.zeros((SLAB, C), F32)
    for across, r_ref in enumerate((r0, r1, r2, r3)):
        rows = r_ref[...]
        member = x ^ across
        start = pl.multiple_of(OWN * member, OWN)
        projected += dot(rows[:, 3 * OWN :], w_proj[pl.ds(start, OWN), :])
        for third in range(3):
            lanes = slice(third * OWN, (third + 1) * OWN)
            columns = w_qkv[:, pl.ds(pl.multiple_of(start + C * third, OWN), OWN)]
            d_normed += dot_nt(rows[:, lanes], columns)
    out[0] = projected.astype(BF16)
    unit, inv_scale = unit_of(jnp.concatenate([own0[0], own1[0]], 0))
    d_unit = d_normed * norm[0:1, :]
    first_mean = jnp.mean(d_unit, -1, keepdims=True)
    second_mean = jnp.mean(d_unit * unit, -1, keepdims=True)
    out[1] = (inv_scale * (d_unit - first_mean - unit * second_mean)).astype(BF16)


def call(kernel, scalars, arrays, outs, scratch=(), flops=0, moved=0):
    smem = pl.BlockSpec(memory_space=pltpu.SMEM)
    vmem = pl.BlockSpec(memory_space=pltpu.VMEM)
    return pl.pallas_call(
        kernel,
        out_shape=[jax.ShapeDtypeStruct(shape, dtype) for shape, dtype in outs],
        in_specs=[smem] + [vmem] * len(arrays),
        out_specs=[vmem] * len(outs),
        scratch_shapes=list(scratch),
        compiler_params=pltpu.CompilerParams(vmem_limit_bytes=8 * 2**20),
        cost_estimate=pl.CostEstimate(flops=flops, bytes_accessed=moved, transcendentals=0),
        name=kernel.__name__,
    )(scalars, *arrays)


def on_device(inputs, norm_params, w_qkv, w_proj, upstream):
    place = lax.axis_index("wide")
    column = lax.axis_index("narrow")
    x, y, z = place % 4, place // 4 % 4, place // 16
    core = column % 2
    row = 1 - y % 2
    window = (place - 4) % 64 // 8
    spot = jnp.stack([x, y, core, z, row]).astype(jnp.int32)
    flags = jnp.stack([4 * (window == 7), 2 * (column == 3), row, x]).astype(jnp.int32)

    own_inputs, own_upstream = inputs[0, 0], upstream[0, 0]
    upper_y = (jnp.arange(8)[:, None] < 4) != (row == 1)
    both = jnp.stack([own_inputs, own_upstream]).reshape(2, 8, 2, 8, C)
    mine = jnp.where(upper_y, both[:, :, 1], both[:, :, 0])
    other = jnp.where(upper_y, both[:, :, 0], both[:, :, 1])
    lower_in = move(mine[:, :4], lambda p, n: (p, n - 1))
    other_in = move(other[:, 4:], lambda p, n: (partner_of(p), n))
    cross_in = move(other[:, :4], lambda p, n: (partner_of(p), n - 1))

    part0 = jnp.stack([mine[:, 4:], lower_in], 1).reshape(2, SLAB // 2, C)
    parts0 = [part0] + [move(part0, across_x(mask)) for mask in (1, 2, 3)]
    part1 = jnp.stack([other_in, cross_in], 1).reshape(2, SLAB // 2, C)
    parts1 = [part1] + [move(part1, across_x(mask)) for mask in (1, 2, 3)]
    half = TOKENS // 2
    normed0, qkv0, up0 = call(
        first_kernel,
        flags,
        (*parts0, norm_params, w_qkv, w_proj),
        [((half, C), BF16), ((half, 3 * OWN), BF16), ((half, OWN), BF16)],
        flops=10_000_000_000,
        moved=3_000_000,
    )
    r0, r1, r2, r3, d_t, a_t, normed1 = call(
        attention_kernel,
        flags,
        (*parts1, normed0, qkv0, up0, norm_params, w_qkv, w_proj),
        [((SLAB, C), BF16)] * 4
        + [((3 * OWN, TOKENS), F32), ((OWN, TOKENS), BF16), ((half, C), BF16)],
        flops=1_200_000_000,
        moved=6_000_000,
    )

    returned = [r0] + [move(rows, across_x(mask)) for mask, rows in ((1, r1), (2, r2), (3, r3))]
    keep, send = call(
        gradient_kernel,
        spot,
        (*parts0, *parts1, r0, r1, r2, r3, d_t, a_t, normed0, normed1, w_qkv),
        [((16, 72, 128), F32)] * 2,
        scratch=[
            pltpu.VMEM((3 * OWN, C), F32),
            pltpu.VMEM((C, OWN), F32),
            pltpu.VMEM((C, 128), F32),
        ],
        flops=20_000_000_000,
        moved=6_000_000,
    )
    received = move(send, across_narrow(1))
    blocks = [slice(4 * mask, 4 * mask + 4) for mask in range(4)]
    halves = [keep[block] + received[block] for block in blocks]
    from_y = [halves[0]] + [move(halves[mask], across_y(mask)) for mask in (1, 2, 3)]
    (back,) = call(
        token_kernel,
        spot,
        (*returned, part0, part1, w_qkv, w_proj, norm_params),
        [((2, SLAB, C), BF16)],
        flops=500_000_000,
        moved=4_000_000,
    )
    from_y[1], from_y[2], from_y[3], back = lax.optimization_barrier(
        (from_y[1], from_y[2], from_y[3], back)
    )
    back = back.reshape(2, 4, 4, 8, C)
    lower = move(back[:, 1], lambda p, n: (p, n + 1))
    other_upper = move(back[:, 2], lambda p, n: (partner_of(p), n))
    other_lower = move(back[:, 3], lambda p, n: (partner_of(p), n + 1))

    shares = ((4, 72, 128), F32)
    (x_parts,) = call(x_parts_kernel, spot, from_y, [shares])
    (z_parts,) = call(z_parts_kernel, spot, (exchange(x_parts, X_GROUPS),), [shares])
    output, grad_inputs = call(
        merge_kernel,
        spot,
        (own_inputs, own_upstream, back[:, 0], lower, other_upper, other_lower),
        [((8, 16, C), BF16)] * 2,
    )
    line, output, grad_inputs = lax.optimization_barrier(
        (exchange(z_parts, Z_GROUPS), output, grad_inputs)
    )
    line = jnp.sum(line, 0)
    grad_qkv, grad_proj, grad_norm = call(
        last_kernel,
        spot,
        (line, *[move(line, across_narrow(mask)) for mask in (1, 2, 3)]),
        [((24, C), F32), ((8, C), F32), ((2, 8), F32)],
    )
    return (
        output[None, None], grad_inputs[None, None], grad_qkv.T, grad_proj.T, grad_norm
    )


def solution(mesh):
    in_specs = (
        P(None, "wide", "narrow", None, None),
        P(),
        P(),
        P(),
        P(None, "wide", "narrow", None, None),
    )
    out_specs = (
        P(None, "wide", "narrow", None, None),
        P(None, "wide", "narrow", None, None),
        P(None, "wide"),
        P(None, "wide"),
        P(None, "wide"),
    )
    return jax.shard_map(
        on_device, mesh=mesh, in_specs=in_specs, out_specs=out_specs, check_vma=False
    )
```

```python
import jax
import jax.numpy as jnp
from jax import lax
from jax.experimental import pallas as pl
from jax.experimental.pallas import tpu as pltpu
from jax.sharding import PartitionSpec as P

HEADS = 16
HEAD_DIM = 32
C = 512
WIN = 8
RING = 4
OWN = C // RING
SLAB = 128
TOKENS = RING * SLAB
BLOCK = 256
CHUNK = 64
SCALE = HEAD_DIM**-0.5
LOG2E = 1.4426950408889634
F32 = jnp.float32
BF16 = jnp.bfloat16


def move(value, target):
    pairs = []
    for place in range(64):
        for column in range(4):
            to_place, to_column = target(place, column)
            pairs.append((place * 4 + column, (to_place % 64) * 4 + to_column % 4))
    return lax.ppermute(value, ("wide", "narrow"), pairs)


def partner_of(place):
    return place + 4 if (place // 4) % 2 else place - 4


def over_x(mask):
    return lambda p, n: (p ^ mask, n)


def over_y(mask):
    return lambda p, n: (p ^ (4 * mask), n)


def over_z(mask):
    return lambda p, n: (p ^ (16 * mask), n)


def over_narrow(mask):
    return lambda p, n: (p, n ^ mask)


def dot(a, b):
    return lax.dot_general(a, b, (((1,), (0,)), ((), ())), preferred_element_type=F32)


def dot_nt(a, b):
    return lax.dot_general(a, b, (((1,), (1,)), ((), ())), preferred_element_type=F32)


def unit_of(rows):
    floats = rows.astype(F32)
    average = jnp.mean(floats, -1, keepdims=True)
    centered = floats - average
    variance = jnp.mean(centered * centered, -1, keepdims=True)
    inv_scale = lax.rsqrt(variance + 1e-05)
    return centered * inv_scale, inv_scale


def two_terms(value):
    high = value.astype(BF16)
    low = (value - high.astype(F32)).astype(BF16)
    return high, low


def own_columns(w_qkv, x):
    start = pl.multiple_of(OWN * x, OWN)
    return jnp.concatenate(
        [w_qkv[:, pl.ds(pl.multiple_of(start + C * third, OWN), OWN)] for third in range(3)], 1
    )


def project(parts, norm, w_qkv, w_proj, member):
    unit, _ = unit_of(jnp.concatenate([part[0] for part in parts], 0))
    normed = (unit * norm[0:1, :] + norm[1:2, :]).astype(BF16)
    qkv = dot(normed, own_columns(w_qkv, member)).astype(BF16)
    rows = w_proj[pl.ds(pl.multiple_of(OWN * member, OWN), OWN), :]
    cotangent = dot_nt(jnp.concatenate([part[1] for part in parts], 0), rows).astype(BF16)
    return normed, qkv, cotangent


def first_kernel(flags, p0, p1, p2, p3, norm, w_qkv, w_proj, normed_ref, qkv_ref, up_ref):
    normed_ref[...], qkv_ref[...], up_ref[...] = project(
        (p0, p1, p2, p3), norm, w_qkv, w_proj, flags[3]
    )


def attention_kernel(
    flags, p0, p1, p2, p3, normed0, qkv0, up0, norm, w_qkv, w_proj,
    r0, r1, r2, r3, dt_ref, at_ref, normed1,
):
    normed1[...], qkv1, up1 = project((p0, p1, p2, p3), norm, w_qkv, w_proj, flags[3])
    qkv = jnp.concatenate([qkv0[...], qkv1], 0)
    cotangent = jnp.concatenate([up0[...], up1], 0)
    queries = qkv[:, :OWN]
    keys = qkv[:, OWN : 2 * OWN]
    values = qkv[:, 2 * OWN :]
    queries_t = queries.T
    cotangent_t = cotangent.T
    keys_t = keys.T
    values_t = values.T
    head_of_lane = lax.broadcasted_iota(jnp.int32, (TOKENS, OWN), 1) // HEAD_DIM

    def label(shape, dim):
        token = lax.broadcasted_iota(jnp.int32, shape, dim)
        row = token // 256
        half = (token // 32) % 2
        low_y = (token // 4) % 2
        return row * flags[0] + half * flags[1] + low_y * flags[2]

    key_label = label((TOKENS, 1), 0)
    query_label = label((1, TOKENS), 1)
    d_key = jnp.zeros((TOKENS, OWN), F32)
    d_value = jnp.zeros((TOKENS, OWN), F32)
    for block in range(TOKENS // BLOCK):
        span = slice(block * BLOCK, (block + 1) * BLOCK)
        allowed = key_label == query_label[:, span]
        for head in range(RING):
            chosen = head_of_lane == head
            rows = slice(head * HEAD_DIM, (head + 1) * HEAD_DIM)
            key_head = jnp.where(chosen, keys, jnp.zeros_like(keys))
            value_head = jnp.where(chosen, values, jnp.zeros_like(values))
            scores = jnp.where(allowed, dot(key_head, queries_t[:, span]), -1e30)
            highest = jnp.max(scores, 0, keepdims=True)
            d_probs = dot(value_head, cotangent_t[:, span])
            weights = []
            total = jnp.zeros((8, BLOCK), F32)
            inner = jnp.zeros((8, BLOCK), F32)
            for start in range(0, TOKENS, CHUNK):
                part = slice(start, start + CHUNK)
                weight = jnp.exp2((scores[part] - highest) * (SCALE * LOG2E))
                total += jnp.sum(weight.reshape(CHUNK // 8, 8, BLOCK), 0)
                inner += jnp.sum((weight * d_probs[part]).reshape(CHUNK // 8, 8, BLOCK), 0)
                weights.append(weight)
            over = 1.0 / jnp.sum(total, 0, keepdims=True)
            inner = jnp.sum(inner, 0, keepdims=True) * over
            over_scaled = over * SCALE
            probs_low, d_scores = [], []
            for index, weight in enumerate(weights):
                part = slice(index * CHUNK, (index + 1) * CHUNK)
                probs_low.append((weight * over).astype(BF16))
                d_scores.append(((weight * over_scaled) * (d_probs[part] - inner)).astype(BF16))
            probs_low = jnp.concatenate(probs_low, 0)
            d_scores = jnp.concatenate(d_scores, 0)
            at_ref[rows, span] = dot(values_t[rows], probs_low).astype(BF16)
            dt_ref[rows, span] = dot(keys_t[rows], d_scores)
            query_head = jnp.where(chosen[span], queries[span], jnp.zeros_like(queries[span]))
            cotangent_head = jnp.where(
                chosen[span], cotangent[span], jnp.zeros_like(cotangent[span])
            )
            d_key += dot(d_scores, query_head)
            d_value += dot(probs_low, cotangent_head)
    dt_ref[OWN : 2 * OWN, :] = d_key.T
    dt_ref[2 * OWN :, :] = d_value.T
    d_query = dt_ref[:OWN, :].T.astype(BF16)
    attended = at_ref[...].T
    for member, r_ref in enumerate((r0, r1, r2, r3)):
        for part in range(2):
            rows = slice(256 * part + 64 * member, 256 * part + 64 * member + 64)
            to = slice(64 * part, 64 * part + 64)
            r_ref[to, :OWN] = d_query[rows]
            r_ref[to, OWN : 2 * OWN] = d_key[rows].astype(BF16)
            r_ref[to, 2 * OWN : 3 * OWN] = d_value[rows].astype(BF16)
            r_ref[to, 3 * OWN :] = attended[rows]


def gradient_kernel(
    spot, p0, p1, p2, p3, p4, p5, p6, p7, r0, r1, r2, r3, dt_ref, at_ref, normed0, normed1, w_qkv,
    keep, send, g_ref, p_ref, n_ref,
):
    x, y, core = spot[0], spot[1], spot[2]
    parts = (p0, p1, p2, p3, p4, p5, p6, p7)
    d_high, d_low = two_terms(dt_ref[...])
    normed = jnp.concatenate([normed0[...], normed1[...]], 0)
    g_ref[...] = dot(d_high, normed) + dot(d_low, normed)
    p_ref[...] = dot(at_ref[...], jnp.concatenate([part[1] for part in parts], 0)).T
    columns = own_columns(w_qkv, x)
    gain_row = jnp.zeros((1, C), F32)
    offset_row = jnp.zeros((1, C), F32)
    for member, r_ref in enumerate((r0, r1, r2, r3)):
        rows = jnp.concatenate([parts[member][0], parts[4 + member][0]], 0)
        d_normed = dot_nt(r_ref[:, : 3 * OWN], columns)
        gain_row += jnp.sum(d_normed * unit_of(rows)[0], 0, keepdims=True)
        offset_row += jnp.sum(d_normed, 0, keepdims=True)
    row = lax.broadcasted_iota(jnp.int32, (128, C), 0)
    n_ref[...] = jnp.where(row == 0, gain_row, jnp.where(row == 1, offset_row, 0.0)).T
    for ahead, out in ((0, keep), (1, send)):
        to_core = core if ahead == 0 else 1 - core
        for across in range(4):
            to_y = y ^ across
            for across_x in range(4):
                to_x = x ^ across_x
                block = 4 * across + across_x
                for side in range(2):
                    lanes = pl.ds(pl.multiple_of(256 * to_core + 128 * side, 128), 128)
                    for slot in range(3):
                        residue = 12 * to_y + 3 * to_x + slot
                        third_of = lax.rem(residue // 16 - x + 6, 3)
                        start = pl.multiple_of(128 * third_of + 8 * lax.rem(residue, 16), 8)
                        top = 24 * side + 8 * slot
                        out[block, top : top + 8, :] = g_ref[pl.ds(start, 8), lanes]
                for z in range(4):
                    rows = pl.ds(pl.multiple_of(128 * z + 32 * to_y + 8 * to_x, 8), 8)
                    piece = p_ref[rows, :]
                    top = 48 + 8 * (z // 2)
                    out[block, top : top + 8, 64 * (z % 2) : 64 * (z % 2) + 64] = jnp.where(
                        to_core == 0, piece[:, :64], piece[:, 64:]
                    )
                    if ahead == 0:
                        out[block, 64:, 32 * z : 32 * z + 32] = n_ref[rows, :32]
                if ahead == 1:
                    out[block, 64:, :] = jnp.zeros((8, 128), F32)


def z_parts_kernel(spot, m0, m1, m2, m3, *outs):
    x, y, z = spot[0], spot[1], spot[3]
    pieces = (m0, m1, m2, m3)

    def from_member(member, rows):
        across = member ^ x
        picked = pieces[0][rows, :]
        for index in range(1, 4):
            picked = jnp.where(across == index, pieces[index][rows, :], picked)
        return picked

    total = (m0[64:, :] + m1[64:, :]) + (m2[64:, :] + m3[64:, :])
    proj = [from_member(member, slice(48, 64)) for member in range(4)]
    for to_z in range(4):
        block = []
        for side in range(2):
            for slot in range(3):
                owner = lax.rem(48 * to_z + 12 * y + 3 * x + slot, 64) // 16
                top = 24 * side + 8 * slot
                block.append(from_member(owner, slice(top, top + 8)))
        rows = slice(8 * (to_z // 2), 8 * (to_z // 2) + 8)
        lanes = slice(64 * (to_z % 2), 64 * (to_z % 2) + 64)
        for pair in range(2):
            block.append(
                jnp.concatenate([proj[2 * pair][rows, lanes], proj[2 * pair + 1][rows, lanes]], 1)
            )
        lanes = slice(32 * to_z, 32 * to_z + 32)
        block.append(jnp.concatenate([total[:, lanes], jnp.zeros((8, 96), F32)], 1))
        block = jnp.concatenate(block, 0)
        for across in range(4):
            ahead = (to_z ^ z) == across
            outs[across][...] = jnp.where(ahead, block, outs[across][...]) if to_z else block


def last_kernel(spot, near, core_in, z_in, both_in, g_out, p_out, n_out):
    mine = near[...] + z_in[...]
    theirs = core_in[...] + both_in[...]
    swap = spot[2] == 1
    shares = (jnp.where(swap, theirs, mine), jnp.where(swap, mine, theirs))
    for core in range(2):
        for side in range(2):
            lanes = slice(256 * core + 128 * side, 256 * core + 128 * side + 128)
            g_out[:, lanes] = shares[core][24 * side : 24 * side + 24]
    for member in range(4):
        rows = slice(48 + 8 * (member // 2), 56 + 8 * (member // 2))
        lanes = slice(64 * (member % 2), 64 * (member % 2) + 64)
        p_out[:, 128 * member : 128 * member + 128] = jnp.concatenate(
            [share[rows, lanes] for share in shares], 1
        )
    n_out[...] = (mine[64:] + theirs[64:]).T[:2]


def upper_rows(row):
    return (lax.broadcasted_iota(jnp.int32, (4, 8, C), 1) < 4) != (row == 1)


def merge_kernel(
    spot, inputs, upstream, mine_high, mine_low, other_high, other_low, output, grad_inputs
):
    upper = upper_rows(spot[4])
    for array, (source, out) in enumerate(((inputs, output), (upstream, grad_inputs))):
        for start, other, mine in ((4, other_high, mine_high), (0, other_low, mine_low)):
            rows = source[start : start + 4].astype(F32)
            from_other = other[array].astype(F32)
            from_mine = mine[array].astype(F32)
            first = rows[:, :8] + jnp.where(upper, from_other, from_mine)
            second = rows[:, 8:] + jnp.where(upper, from_mine, from_other)
            out[start : start + 4] = jnp.concatenate([first, second], 1).astype(BF16)


def token_kernel(
    spot, r0, r1, r2, r3, own0, own1, w_qkv, w_proj, norm, out
):
    x = spot[0]
    projected = jnp.zeros((SLAB, C), F32)
    d_normed = jnp.zeros((SLAB, C), F32)
    for across, r_ref in enumerate((r0, r1, r2, r3)):
        rows = r_ref[...]
        member = x ^ across
        start = pl.multiple_of(OWN * member, OWN)
        projected += dot(rows[:, 3 * OWN :], w_proj[pl.ds(start, OWN), :])
        for third in range(3):
            lanes = slice(third * OWN, (third + 1) * OWN)
            columns = w_qkv[:, pl.ds(pl.multiple_of(start + C * third, OWN), OWN)]
            d_normed += dot_nt(rows[:, lanes], columns)
    out[0] = projected.astype(BF16)
    unit, inv_scale = unit_of(jnp.concatenate([own0[0], own1[0]], 0))
    d_unit = d_normed * norm[0:1, :]
    first_mean = jnp.mean(d_unit, -1, keepdims=True)
    second_mean = jnp.mean(d_unit * unit, -1, keepdims=True)
    out[1] = (inv_scale * (d_unit - first_mean - unit * second_mean)).astype(BF16)


def call(kernel, scalars, arrays, outs, scratch=(), flops=0, moved=0):
    smem = pl.BlockSpec(memory_space=pltpu.SMEM)
    vmem = pl.BlockSpec(memory_space=pltpu.VMEM)
    return pl.pallas_call(
        kernel,
        out_shape=[jax.ShapeDtypeStruct(shape, dtype) for shape, dtype in outs],
        in_specs=[smem] + [vmem] * len(arrays),
        out_specs=[vmem] * len(outs),
        scratch_shapes=list(scratch),
        compiler_params=pltpu.CompilerParams(vmem_limit_bytes=8 * 2**20),
        cost_estimate=pl.CostEstimate(flops=flops, bytes_accessed=moved, transcendentals=0),
        name=kernel.__name__,
    )(scalars, *arrays)


def on_device(inputs, norm_params, w_qkv, w_proj, upstream):
    place = lax.axis_index("wide")
    column = lax.axis_index("narrow")
    x, y, z = place % 4, place // 4 % 4, place // 16
    core = column % 2
    row = 1 - y % 2
    window = (place - 4) % 64 // 8
    spot = jnp.stack([x, y, core, z, row]).astype(jnp.int32)
    flags = jnp.stack([4 * (window == 7), 2 * (column == 3), row, x]).astype(jnp.int32)

    own_inputs, own_upstream = inputs[0, 0], upstream[0, 0]
    upper_y = (jnp.arange(8)[:, None] < 4) != (row == 1)
    both = jnp.stack([own_inputs, own_upstream]).reshape(2, 8, 2, 8, C)
    mine = jnp.where(upper_y, both[:, :, 1], both[:, :, 0])
    other = jnp.where(upper_y, both[:, :, 0], both[:, :, 1])
    lower_in = move(mine[:, :4], lambda p, n: (p, n - 1))
    other_in = move(other[:, 4:], lambda p, n: (partner_of(p), n))
    cross_in = move(other[:, :4], lambda p, n: (partner_of(p), n - 1))

    part0 = jnp.stack([mine[:, 4:], lower_in], 1).reshape(2, SLAB // 2, C)
    parts0 = [part0] + [move(part0, over_x(mask)) for mask in (1, 2, 3)]
    part1 = jnp.stack([other_in, cross_in], 1).reshape(2, SLAB // 2, C)
    parts1 = [part1] + [move(part1, over_x(mask)) for mask in (1, 2, 3)]
    half = TOKENS // 2
    normed0, qkv0, up0 = call(
        first_kernel,
        flags,
        (*parts0, norm_params, w_qkv, w_proj),
        [((half, C), BF16), ((half, 3 * OWN), BF16), ((half, OWN), BF16)],
        flops=10_000_000_000,
        moved=3_000_000,
    )
    r0, r1, r2, r3, d_t, a_t, normed1 = call(
        attention_kernel,
        flags,
        (*parts1, normed0, qkv0, up0, norm_params, w_qkv, w_proj),
        [((SLAB, C), BF16)] * 4
        + [((3 * OWN, TOKENS), F32), ((OWN, TOKENS), BF16), ((half, C), BF16)],
        flops=1_200_000_000,
        moved=6_000_000,
    )

    keep, send = call(
        gradient_kernel,
        spot,
        (*parts0, *parts1, r0, r1, r2, r3, d_t, a_t, normed0, normed1, w_qkv),
        [((16, 72, 128), F32)] * 2,
        scratch=[
            pltpu.VMEM((3 * OWN, C), F32),
            pltpu.VMEM((C, OWN), F32),
            pltpu.VMEM((C, 128), F32),
        ],
        flops=20_000_000_000,
        moved=6_000_000,
    )
    received = move(send, over_narrow(1))
    blocks = [slice(4 * mask, 4 * mask + 4) for mask in range(4)]
    halves = [keep[block] + received[block] for block in blocks]
    halves[1:] = [half.astype(BF16) for half in halves[1:]]
    from_y = [halves[0]] + [move(halves[mask], over_y(mask)) for mask in (1, 2, 3)]
    returned = [r0] + [
        move(rows, over_x(mask)) for mask, rows in ((1, r1), (2, r2), (3, r3))
    ]
    *from_y, returned[1], returned[2] = lax.optimization_barrier(
        (*from_y, returned[1], returned[2])
    )
    (back,) = call(
        token_kernel,
        spot,
        (*returned, part0, part1, w_qkv, w_proj, norm_params),
        [((2, SLAB, C), BF16)],
        flops=500_000_000,
        moved=4_000_000,
    )
    share = ((72, 128), F32)
    sums = [piece.astype(F32) for piece in from_y]
    x_parts = [(sums[0][k] + sums[1][k]) + (sums[2][k] + sums[3][k]) for k in range(4)]
    from_x = [x_parts[0]] + [move(x_parts[mask], over_x(mask)) for mask in (1, 2, 3)]
    from_x[1], from_x[2], from_x[3], back = lax.optimization_barrier(
        (from_x[1], from_x[2], from_x[3], back)
    )
    back = back.reshape(2, 4, 4, 8, C)
    lower = move(back[:, 1], lambda p, n: (p, n + 1))
    other_upper = move(back[:, 2], lambda p, n: (partner_of(p), n))
    other_lower = move(back[:, 3], lambda p, n: (partner_of(p), n + 1))
    z_parts = call(z_parts_kernel, spot, from_x, [share] * 4)
    output, grad_inputs = call(
        merge_kernel,
        spot,
        (own_inputs, own_upstream, back[:, 0], lower, other_upper, other_lower),
        [((8, 16, C), BF16)] * 2,
    )
    line = [z_parts[0]] + [move(z_parts[mask], over_z(mask)) for mask in (1, 2, 3)]
    line[1], line[2], line[3], output, grad_inputs = lax.optimization_barrier(
        (line[1], line[2], line[3], output, grad_inputs)
    )
    line = (line[0] + line[1]) + (line[2] + line[3])
    last = [line] + [move(line, over_narrow(mask)) for mask in (1, 2, 3)]
    grad_qkv, grad_proj, grad_norm = call(
        last_kernel, spot, last, [((24, C), F32), ((8, C), F32), ((2, 8), F32)]
    )
    return (
        output[None, None], grad_inputs[None, None], grad_qkv.T, grad_proj.T, grad_norm
    )


def solution(mesh):
    in_specs = (
        P(None, "wide", "narrow", None, None),
        P(),
        P(),
        P(),
        P(None, "wide", "narrow", None, None),
    )
    out_specs = (
        P(None, "wide", "narrow", None, None),
        P(None, "wide", "narrow", None, None),
        P(None, "wide"),
        P(None, "wide"),
        P(None, "wide"),
    )
    return jax.shard_map(
        on_device, mesh=mesh, in_specs=in_specs, out_specs=out_specs, check_vma=False
    )
```

```python
import jax
import jax.numpy as jnp
from jax import lax
from jax.experimental import pallas as pl
from jax.experimental.pallas import tpu as pltpu
from jax.sharding import PartitionSpec as P

HEADS = 16
HEAD_DIM = 32
C = 512
WIN = 8
RING = 4
OWN = C // RING
SLAB = 128
TOKENS = RING * SLAB
BLOCK = 256
CHUNK = 64
SCALE = HEAD_DIM**-0.5
LOG2E = 1.4426950408889634
F32 = jnp.float32
BF16 = jnp.bfloat16


def move(value, target):
    pairs = []
    for place in range(64):
        for column in range(4):
            to_place, to_column = target(place, column)
            pairs.append((place * 4 + column, (to_place % 64) * 4 + to_column % 4))
    return lax.ppermute(value, ("wide", "narrow"), pairs)


def partner_of(place):
    return place + 4 if (place // 4) % 2 else place - 4


def over_x(mask):
    return lambda p, n: (p ^ mask, n)


def over_y(mask):
    return lambda p, n: (p ^ (4 * mask), n)


def over_z(mask):
    return lambda p, n: (p ^ (16 * mask), n)


def over_narrow(mask):
    return lambda p, n: (p, n ^ mask)


def dot(a, b):
    return lax.dot_general(a, b, (((1,), (0,)), ((), ())), preferred_element_type=F32)


def dot_nt(a, b):
    return lax.dot_general(a, b, (((1,), (1,)), ((), ())), preferred_element_type=F32)


def unit_of(rows):
    floats = rows.astype(F32)
    average = jnp.mean(floats, -1, keepdims=True)
    centered = floats - average
    variance = jnp.mean(centered * centered, -1, keepdims=True)
    inv_scale = lax.rsqrt(variance + 1e-05)
    return centered * inv_scale, inv_scale


def two_terms(value):
    high = value.astype(BF16)
    low = (value - high.astype(F32)).astype(BF16)
    return high, low


def own_columns(w_qkv, x):
    start = pl.multiple_of(OWN * x, OWN)
    return jnp.concatenate(
        [w_qkv[:, pl.ds(pl.multiple_of(start + C * third, OWN), OWN)] for third in range(3)], 1
    )


def project(parts, norm, w_qkv, w_proj, member):
    unit, _ = unit_of(jnp.concatenate([part[0] for part in parts], 0))
    normed = (unit * norm[0:1, :] + norm[1:2, :]).astype(BF16)
    qkv = dot(normed, own_columns(w_qkv, member)).astype(BF16)
    rows = w_proj[pl.ds(pl.multiple_of(OWN * member, OWN), OWN), :]
    cotangent = dot_nt(jnp.concatenate([part[1] for part in parts], 0), rows).astype(BF16)
    return normed, qkv, cotangent


def first_kernel(flags, p0, p1, p2, p3, norm, w_qkv, w_proj, normed_ref, qkv_ref, up_ref):
    normed_ref[...], qkv_ref[...], up_ref[...] = project(
        (p0, p1, p2, p3), norm, w_qkv, w_proj, flags[3]
    )


def attention_kernel(
    flags, p0, p1, p2, p3, normed0, qkv0, up0, norm, w_qkv, w_proj,
    r0, r1, r2, r3, dt_ref, at_ref, normed1,
):
    normed1[...], qkv1, up1 = project((p0, p1, p2, p3), norm, w_qkv, w_proj, flags[3])
    qkv = jnp.concatenate([qkv0[...], qkv1], 0)
    cotangent = jnp.concatenate([up0[...], up1], 0)
    queries = qkv[:, :OWN]
    keys = qkv[:, OWN : 2 * OWN]
    values = qkv[:, 2 * OWN :]
    queries_t = queries.T
    cotangent_t = cotangent.T
    keys_t = keys.T
    values_t = values.T
    head_of_lane = lax.broadcasted_iota(jnp.int32, (TOKENS, OWN), 1) // HEAD_DIM

    def label(shape, dim):
        token = lax.broadcasted_iota(jnp.int32, shape, dim)
        row = token // 256
        half = (token // 32) % 2
        low_y = (token // 4) % 2
        return row * flags[0] + half * flags[1] + low_y * flags[2]

    key_label = label((TOKENS, 1), 0)
    query_label = label((1, TOKENS), 1)
    d_key = jnp.zeros((TOKENS, OWN), F32)
    d_value = jnp.zeros((TOKENS, OWN), F32)
    for block in range(TOKENS // BLOCK):
        span = slice(block * BLOCK, (block + 1) * BLOCK)
        allowed = key_label == query_label[:, span]
        for head in range(RING):
            chosen = head_of_lane == head
            rows = slice(head * HEAD_DIM, (head + 1) * HEAD_DIM)
            key_head = jnp.where(chosen, keys, jnp.zeros_like(keys))
            value_head = jnp.where(chosen, values, jnp.zeros_like(values))
            scores = jnp.where(allowed, dot(key_head, queries_t[:, span]), -1e30)
            highest = jnp.max(scores, 0, keepdims=True)
            d_probs = dot(value_head, cotangent_t[:, span])
            weights = []
            total = jnp.zeros((8, BLOCK), F32)
            inner = jnp.zeros((8, BLOCK), F32)
            for start in range(0, TOKENS, CHUNK):
                part = slice(start, start + CHUNK)
                weight = jnp.exp2((scores[part] - highest) * (SCALE * LOG2E))
                total += jnp.sum(weight.reshape(CHUNK // 8, 8, BLOCK), 0)
                inner += jnp.sum((weight * d_probs[part]).reshape(CHUNK // 8, 8, BLOCK), 0)
                weights.append(weight)
            over = 1.0 / jnp.sum(total, 0, keepdims=True)
            inner = jnp.sum(inner, 0, keepdims=True) * over
            over_scaled = over * SCALE
            probs_low, d_scores = [], []
            for index, weight in enumerate(weights):
                part = slice(index * CHUNK, (index + 1) * CHUNK)
                probs_low.append((weight * over).astype(BF16))
                d_scores.append(((weight * over_scaled) * (d_probs[part] - inner)).astype(BF16))
            probs_low = jnp.concatenate(probs_low, 0)
            d_scores = jnp.concatenate(d_scores, 0)
            at_ref[rows, span] = dot(values_t[rows], probs_low).astype(BF16)
            dt_ref[rows, span] = dot(keys_t[rows], d_scores)
            query_head = jnp.where(chosen[span], queries[span], jnp.zeros_like(queries[span]))
            cotangent_head = jnp.where(
                chosen[span], cotangent[span], jnp.zeros_like(cotangent[span])
            )
            d_key += dot(d_scores, query_head)
            d_value += dot(probs_low, cotangent_head)
    dt_ref[OWN : 2 * OWN, :] = d_key.T
    dt_ref[2 * OWN :, :] = d_value.T
    d_query = dt_ref[:OWN, :].T.astype(BF16)
    attended = at_ref[...].T
    for member, r_ref in enumerate((r0, r1, r2, r3)):
        for part in range(2):
            rows = slice(256 * part + 64 * member, 256 * part + 64 * member + 64)
            to = slice(64 * part, 64 * part + 64)
            r_ref[to, :OWN] = d_query[rows]
            r_ref[to, OWN : 2 * OWN] = d_key[rows].astype(BF16)
            r_ref[to, 2 * OWN : 3 * OWN] = d_value[rows].astype(BF16)
            r_ref[to, 3 * OWN :] = attended[rows]


def gradient_kernel(
    spot, p0, p1, p2, p3, p4, p5, p6, p7, r0, r1, r2, r3, dt_ref, at_ref, normed0, normed1, w_qkv,
    keep, send, g_ref, p_ref, n_ref,
):
    x, y, core = spot[0], spot[1], spot[2]
    parts = (p0, p1, p2, p3, p4, p5, p6, p7)
    d_high, d_low = two_terms(dt_ref[...])
    normed = jnp.concatenate([normed0[...], normed1[...]], 0)
    g_ref[...] = dot(d_high, normed) + dot(d_low, normed)
    p_ref[...] = dot(at_ref[...], jnp.concatenate([part[1] for part in parts], 0)).T
    columns = own_columns(w_qkv, x)
    gain_row = jnp.zeros((1, C), F32)
    offset_row = jnp.zeros((1, C), F32)
    for member, r_ref in enumerate((r0, r1, r2, r3)):
        rows = jnp.concatenate([parts[member][0], parts[4 + member][0]], 0)
        d_normed = dot_nt(r_ref[:, : 3 * OWN], columns)
        gain_row += jnp.sum(d_normed * unit_of(rows)[0], 0, keepdims=True)
        offset_row += jnp.sum(d_normed, 0, keepdims=True)
    row = lax.broadcasted_iota(jnp.int32, (128, C), 0)
    n_ref[...] = jnp.where(row == 0, gain_row, jnp.where(row == 1, offset_row, 0.0)).T
    for ahead, out in ((0, keep), (1, send)):
        to_core = core if ahead == 0 else 1 - core
        for across in range(4):
            to_y = y ^ across
            for across_x in range(4):
                to_x = x ^ across_x
                block = 4 * across + across_x
                for side in range(2):
                    lanes = pl.ds(pl.multiple_of(256 * to_core + 128 * side, 128), 128)
                    for slot in range(3):
                        residue = 12 * to_y + 3 * to_x + slot
                        third_of = lax.rem(residue // 16 - x + 6, 3)
                        start = pl.multiple_of(128 * third_of + 8 * lax.rem(residue, 16), 8)
                        top = 24 * side + 8 * slot
                        out[block, top : top + 8, :] = g_ref[pl.ds(start, 8), lanes]
                for z in range(4):
                    rows = pl.ds(pl.multiple_of(128 * z + 32 * to_y + 8 * to_x, 8), 8)
                    piece = p_ref[rows, :]
                    top = 48 + 8 * (z // 2)
                    out[block, top : top + 8, 64 * (z % 2) : 64 * (z % 2) + 64] = jnp.where(
                        to_core == 0, piece[:, :64], piece[:, 64:]
                    )
                    if ahead == 0:
                        out[block, 64:, 32 * z : 32 * z + 32] = n_ref[rows, :32]
                if ahead == 1:
                    out[block, 64:, :] = jnp.zeros((8, 128), F32)


def z_parts_kernel(spot, m0, m1, m2, m3, mark, *outs):
    x, y, z = spot[0], spot[1], spot[3]
    pieces = (m0, m1, m2, m3)

    def from_member(member, rows):
        across = member ^ x
        picked = pieces[0][rows, :]
        for index in range(1, 4):
            picked = jnp.where(across == index, pieces[index][rows, :], picked)
        return picked

    total = (m0[64:, :] + m1[64:, :]) + (m2[64:, :] + m3[64:, :])
    proj = [from_member(member, slice(48, 64)) for member in range(4)]
    for to_z in range(4):
        block = []
        for side in range(2):
            for slot in range(3):
                owner = lax.rem(48 * to_z + 12 * y + 3 * x + slot, 64) // 16
                top = 24 * side + 8 * slot
                block.append(from_member(owner, slice(top, top + 8)))
        rows = slice(8 * (to_z // 2), 8 * (to_z // 2) + 8)
        lanes = slice(64 * (to_z % 2), 64 * (to_z % 2) + 64)
        for pair in range(2):
            block.append(
                jnp.concatenate([proj[2 * pair][rows, lanes], proj[2 * pair + 1][rows, lanes]], 1)
            )
        lanes = slice(32 * to_z, 32 * to_z + 32)
        block.append(jnp.concatenate([total[:, lanes], jnp.zeros((8, 96), F32)], 1))
        block = jnp.concatenate(block, 0)
        for across in range(4):
            ahead = (to_z ^ z) == across
            outs[across][...] = jnp.where(ahead, block, outs[across][...]) if to_z else block


def last_kernel(spot, near, core_in, z_in, both_in, g_out, p_out, n_out):
    mine = near[...] + z_in[...]
    theirs = core_in[...] + both_in[...]
    swap = spot[2] == 1
    shares = (jnp.where(swap, theirs, mine), jnp.where(swap, mine, theirs))
    for core in range(2):
        for side in range(2):
            lanes = slice(256 * core + 128 * side, 256 * core + 128 * side + 128)
            g_out[:, lanes] = shares[core][24 * side : 24 * side + 24]
    for member in range(4):
        rows = slice(48 + 8 * (member // 2), 56 + 8 * (member // 2))
        lanes = slice(64 * (member % 2), 64 * (member % 2) + 64)
        p_out[:, 128 * member : 128 * member + 128] = jnp.concatenate(
            [share[rows, lanes] for share in shares], 1
        )
    n_out[...] = (mine[64:] + theirs[64:]).T[:2]


def upper_rows(row):
    return (lax.broadcasted_iota(jnp.int32, (4, 8, C), 1) < 4) != (row == 1)


def merge_kernel(
    spot, inputs, upstream, mine_high, mine_low, other_high, other_low, output, grad_inputs
):
    upper = upper_rows(spot[4])
    for array, (source, out) in enumerate(((inputs, output), (upstream, grad_inputs))):
        for start, other, mine in ((4, other_high, mine_high), (0, other_low, mine_low)):
            rows = source[start : start + 4].astype(F32)
            from_other = other[array].astype(F32)
            from_mine = mine[array].astype(F32)
            first = rows[:, :8] + jnp.where(upper, from_other, from_mine)
            second = rows[:, 8:] + jnp.where(upper, from_mine, from_other)
            out[start : start + 4] = jnp.concatenate([first, second], 1).astype(BF16)


def token_kernel(
    spot, r0, r1, r2, r3, own0, own1, w_qkv, w_proj, norm, out, mark
):
    x = spot[0]
    projected = jnp.zeros((SLAB, C), F32)
    d_normed = jnp.zeros((SLAB, C), F32)
    for across, r_ref in enumerate((r0, r1, r2, r3)):
        rows = r_ref[...]
        member = x ^ across
        start = pl.multiple_of(OWN * member, OWN)
        projected += dot(rows[:, 3 * OWN :], w_proj[pl.ds(start, OWN), :])
        for third in range(3):
            lanes = slice(third * OWN, (third + 1) * OWN)
            columns = w_qkv[:, pl.ds(pl.multiple_of(start + C * third, OWN), OWN)]
            d_normed += dot_nt(rows[:, lanes], columns)
    mark[...] = projected[:8, :128]
    out[0] = projected.astype(BF16)
    unit, inv_scale = unit_of(jnp.concatenate([own0[0], own1[0]], 0))
    d_unit = d_normed * norm[0:1, :]
    first_mean = jnp.mean(d_unit, -1, keepdims=True)
    second_mean = jnp.mean(d_unit * unit, -1, keepdims=True)
    out[1] = (inv_scale * (d_unit - first_mean - unit * second_mean)).astype(BF16)


def call(kernel, scalars, arrays, outs, scratch=(), flops=0, moved=0):
    smem = pl.BlockSpec(memory_space=pltpu.SMEM)
    vmem = pl.BlockSpec(memory_space=pltpu.VMEM)
    return pl.pallas_call(
        kernel,
        out_shape=[jax.ShapeDtypeStruct(shape, dtype) for shape, dtype in outs],
        in_specs=[smem] + [vmem] * len(arrays),
        out_specs=[vmem] * len(outs),
        scratch_shapes=list(scratch),
        compiler_params=pltpu.CompilerParams(vmem_limit_bytes=8 * 2**20),
        cost_estimate=pl.CostEstimate(flops=flops, bytes_accessed=moved, transcendentals=0),
        name=kernel.__name__,
    )(scalars, *arrays)


def on_device(inputs, norm_params, w_qkv, w_proj, upstream):
    place = lax.axis_index("wide")
    column = lax.axis_index("narrow")
    x, y, z = place % 4, place // 4 % 4, place // 16
    core = column % 2
    row = 1 - y % 2
    window = (place - 4) % 64 // 8
    spot = jnp.stack([x, y, core, z, row]).astype(jnp.int32)
    flags = jnp.stack([4 * (window == 7), 2 * (column == 3), row, x]).astype(jnp.int32)

    own_inputs, own_upstream = inputs[0, 0], upstream[0, 0]
    upper_y = (jnp.arange(8)[:, None] < 4) != (row == 1)
    both = jnp.stack([own_inputs, own_upstream]).reshape(2, 8, 2, 8, C)
    mine = jnp.where(upper_y, both[:, :, 1], both[:, :, 0])
    other = jnp.where(upper_y, both[:, :, 0], both[:, :, 1])
    lower_in = move(mine[:, :4], lambda p, n: (p, n - 1))
    other_in = move(other[:, 4:], lambda p, n: (partner_of(p), n))
    cross_in = move(other[:, :4], lambda p, n: (partner_of(p), n - 1))

    part0 = jnp.stack([mine[:, 4:], lower_in], 1).reshape(2, SLAB // 2, C)
    parts0 = [part0] + [move(part0, over_x(mask)) for mask in (1, 2, 3)]
    part1 = jnp.stack([other_in, cross_in], 1).reshape(2, SLAB // 2, C)
    parts1 = [part1] + [move(part1, over_x(mask)) for mask in (1, 2, 3)]
    half = TOKENS // 2
    normed0, qkv0, up0 = call(
        first_kernel,
        flags,
        (*parts0, norm_params, w_qkv, w_proj),
        [((half, C), BF16), ((half, 3 * OWN), BF16), ((half, OWN), BF16)],
        flops=10_000_000_000,
        moved=3_000_000,
    )
    r0, r1, r2, r3, d_t, a_t, normed1 = call(
        attention_kernel,
        flags,
        (*parts1, normed0, qkv0, up0, norm_params, w_qkv, w_proj),
        [((SLAB, C), BF16)] * 4
        + [((3 * OWN, TOKENS), F32), ((OWN, TOKENS), BF16), ((half, C), BF16)],
        flops=1_200_000_000,
        moved=6_000_000,
    )

    keep, send = call(
        gradient_kernel,
        spot,
        (*parts0, *parts1, r0, r1, r2, r3, d_t, a_t, normed0, normed1, w_qkv),
        [((16, 72, 128), F32)] * 2,
        scratch=[
            pltpu.VMEM((3 * OWN, C), F32),
            pltpu.VMEM((C, OWN), F32),
            pltpu.VMEM((C, 128), F32),
        ],
        flops=20_000_000_000,
        moved=6_000_000,
    )
    received = move(send, over_narrow(1))
    blocks = [slice(4 * mask, 4 * mask + 4) for mask in range(4)]
    halves = [keep[block] + received[block] for block in blocks]
    halves[1:] = [half.astype(BF16) for half in halves[1:]]
    from_y = [halves[0]] + [move(halves[mask], over_y(mask)) for mask in (1, 2, 3)]
    returned = [r0] + [
        move(rows, over_x(mask)) for mask, rows in ((1, r1), (2, r2), (3, r3))
    ]
    *from_y, returned[1], returned[2] = lax.optimization_barrier(
        (*from_y, returned[1], returned[2])
    )
    back, mark = call(
        token_kernel,
        spot,
        (*returned, part0, part1, w_qkv, w_proj, norm_params),
        [((2, SLAB, C), BF16), ((8, 128), F32)],
        flops=500_000_000,
        moved=4_000_000,
    )
    share = ((72, 128), F32)
    sums = [piece.astype(F32) for piece in from_y]
    x_parts = [(sums[0][k] + sums[1][k]) + (sums[2][k] + sums[3][k]) for k in range(4)]
    from_x = [x_parts[0]] + [move(x_parts[mask], over_x(mask)) for mask in (1, 2, 3)]
    from_x[1], from_x[2], from_x[3], mark = lax.optimization_barrier(
        (from_x[1], from_x[2], from_x[3], mark)
    )
    back = back.reshape(2, 4, 4, 8, C)
    crossed = move(back[:, 2:], lambda p, n: (partner_of(p), n))
    z_parts = call(z_parts_kernel, spot, (*from_x, mark), [share] * 4)
    line = [z_parts[0]] + [move(z_parts[mask], over_z(mask)) for mask in (1, 2, 3)]
    line[1], line[2], line[3], crossed = lax.optimization_barrier(
        (line[1], line[2], line[3], crossed)
    )
    line = (line[0] + line[1]) + (line[2] + line[3])
    last = [line] + [move(line, over_narrow(mask)) for mask in (1, 2, 3)]
    lower = move(jnp.stack([back[:, 1], crossed[:, 1]], 1), lambda p, n: (p, n + 1))
    output, grad_inputs = call(
        merge_kernel,
        spot,
        (own_inputs, own_upstream, back[:, 0], lower[:, 0], crossed[:, 0], lower[:, 1]),
        [((8, 16, C), BF16)] * 2,
    )
    last[1], last[2], last[3], output, grad_inputs = lax.optimization_barrier(
        (last[1], last[2], last[3], output, grad_inputs)
    )
    grad_qkv, grad_proj, grad_norm = call(
        last_kernel, spot, last, [((24, C), F32), ((8, C), F32), ((2, 8), F32)]
    )
    return (
        output[None, None], grad_inputs[None, None], grad_qkv.T, grad_proj.T, grad_norm
    )


def solution(mesh):
    in_specs = (
        P(None, "wide", "narrow", None, None),
        P(),
        P(),
        P(),
        P(None, "wide", "narrow", None, None),
    )
    out_specs = (
        P(None, "wide", "narrow", None, None),
        P(None, "wide", "narrow", None, None),
        P(None, "wide"),
        P(None, "wide"),
        P(None, "wide"),
    )
    return jax.shard_map(
        on_device, mesh=mesh, in_specs=in_specs, out_specs=out_specs, check_vma=False
    )
```

```python
import jax
import jax.numpy as jnp
from jax import lax
from jax.experimental import pallas as pl
from jax.experimental.pallas import tpu as pltpu
from jax.sharding import PartitionSpec as P

HEADS = 16
HEAD_DIM = 32
C = 512
WIN = 8
RING = 4
OWN = C // RING
SLAB = 128
TOKENS = RING * SLAB
BLOCK = 256
CHUNK = 64
SCALE = HEAD_DIM**-0.5
LOG2E = 1.4426950408889634
F32 = jnp.float32
BF16 = jnp.bfloat16


def move(value, target):
    pairs = []
    for place in range(64):
        for column in range(4):
            to_place, to_column = target(place, column)
            pairs.append((place * 4 + column, (to_place % 64) * 4 + to_column % 4))
    return lax.ppermute(value, ("wide", "narrow"), pairs)


def partner_of(place):
    return place + 4 if (place // 4) % 2 else place - 4


def over_x(mask):
    return lambda p, n: (p ^ mask, n)


def over_y(mask):
    return lambda p, n: (p ^ (4 * mask), n)


def over_z(mask):
    return lambda p, n: (p ^ (16 * mask), n)


def over_narrow(mask):
    return lambda p, n: (p, n ^ mask)


def dot(a, b):
    return lax.dot_general(a, b, (((1,), (0,)), ((), ())), preferred_element_type=F32)


def dot_nt(a, b):
    return lax.dot_general(a, b, (((1,), (1,)), ((), ())), preferred_element_type=F32)


def unit_of(rows):
    floats = rows.astype(F32)
    average = jnp.mean(floats, -1, keepdims=True)
    centered = floats - average
    variance = jnp.mean(centered * centered, -1, keepdims=True)
    inv_scale = lax.rsqrt(variance + 1e-05)
    return centered * inv_scale, inv_scale


def two_terms(value):
    high = value.astype(BF16)
    low = (value - high.astype(F32)).astype(BF16)
    return high, low


def own_columns(w_qkv, x):
    start = pl.multiple_of(OWN * x, OWN)
    return jnp.concatenate(
        [w_qkv[:, pl.ds(pl.multiple_of(start + C * third, OWN), OWN)] for third in range(3)], 1
    )


def project(parts, norm, w_qkv, w_proj, member):
    unit, _ = unit_of(jnp.concatenate([part[0] for part in parts], 0))
    normed = (unit * norm[0:1, :] + norm[1:2, :]).astype(BF16)
    qkv = dot(normed, own_columns(w_qkv, member)).astype(BF16)
    rows = w_proj[pl.ds(pl.multiple_of(OWN * member, OWN), OWN), :]
    cotangent = dot_nt(jnp.concatenate([part[1] for part in parts], 0), rows).astype(BF16)
    return normed, qkv, cotangent


def first_kernel(flags, p0, p1, p2, p3, norm, w_qkv, w_proj, normed_ref, qkv_ref, up_ref):
    normed_ref[...], qkv_ref[...], up_ref[...] = project(
        (p0, p1, p2, p3), norm, w_qkv, w_proj, flags[3]
    )


def attention_kernel(
    flags, p0, p1, p2, p3, normed0, qkv0, up0, norm, w_qkv, w_proj,
    r0, r1, r2, r3, dt_ref, at_ref, normed1,
):
    normed1[...], qkv1, up1 = project((p0, p1, p2, p3), norm, w_qkv, w_proj, flags[3])
    qkv = jnp.concatenate([qkv0[...], qkv1], 0)
    cotangent = jnp.concatenate([up0[...], up1], 0)
    queries = qkv[:, :OWN]
    keys = qkv[:, OWN : 2 * OWN]
    values = qkv[:, 2 * OWN :]
    queries_t = queries.T
    cotangent_t = cotangent.T
    keys_t = keys.T
    values_t = values.T
    head_of_lane = lax.broadcasted_iota(jnp.int32, (TOKENS, OWN), 1) // HEAD_DIM

    def label(shape, dim):
        token = lax.broadcasted_iota(jnp.int32, shape, dim)
        row = token // 256
        half = (token // 32) % 2
        low_y = (token // 4) % 2
        return row * flags[0] + half * flags[1] + low_y * flags[2]

    key_label = label((TOKENS, 1), 0)
    query_label = label((1, TOKENS), 1)
    d_key = jnp.zeros((TOKENS, OWN), F32)
    d_value = jnp.zeros((TOKENS, OWN), F32)
    for block in range(TOKENS // BLOCK):
        span = slice(block * BLOCK, (block + 1) * BLOCK)
        barred = jnp.where(key_label == query_label[:, span], 0.0, -1e30)
        for head in range(RING):
            chosen = head_of_lane == head
            rows = slice(head * HEAD_DIM, (head + 1) * HEAD_DIM)
            key_head = jnp.where(chosen, keys, jnp.zeros_like(keys))
            value_head = jnp.where(chosen, values, jnp.zeros_like(values))
            scores = dot(key_head, queries_t[:, span]) + barred
            highest = jnp.max(scores, 0, keepdims=True)
            d_probs = dot(value_head, cotangent_t[:, span])
            weights = []
            total = jnp.zeros((8, BLOCK), F32)
            inner = jnp.zeros((8, BLOCK), F32)
            for start in range(0, TOKENS, CHUNK):
                part = slice(start, start + CHUNK)
                weight = jnp.exp2((scores[part] - highest) * (SCALE * LOG2E))
                total += jnp.sum(weight.reshape(CHUNK // 8, 8, BLOCK), 0)
                inner += jnp.sum((weight * d_probs[part]).reshape(CHUNK // 8, 8, BLOCK), 0)
                weights.append(weight)
            over = 1.0 / jnp.sum(total, 0, keepdims=True)
            inner = jnp.sum(inner, 0, keepdims=True) * over
            over_scaled = over * SCALE
            probs_low, d_scores = [], []
            for index, weight in enumerate(weights):
                part = slice(index * CHUNK, (index + 1) * CHUNK)
                probs_low.append((weight * over).astype(BF16))
                d_scores.append(((weight * over_scaled) * (d_probs[part] - inner)).astype(BF16))
            probs_low = jnp.concatenate(probs_low, 0)
            d_scores = jnp.concatenate(d_scores, 0)
            at_ref[rows, span] = dot(values_t[rows], probs_low).astype(BF16)
            dt_ref[rows, span] = dot(keys_t[rows], d_scores)
            query_head = jnp.where(chosen[span], queries[span], jnp.zeros_like(queries[span]))
            cotangent_head = jnp.where(
                chosen[span], cotangent[span], jnp.zeros_like(cotangent[span])
            )
            d_key += dot(d_scores, query_head)
            d_value += dot(probs_low, cotangent_head)
    dt_ref[OWN : 2 * OWN, :] = d_key.T
    dt_ref[2 * OWN :, :] = d_value.T
    d_query = dt_ref[:OWN, :].T.astype(BF16)
    attended = at_ref[...].T
    for member, r_ref in enumerate((r0, r1, r2, r3)):
        for part in range(2):
            rows = slice(256 * part + 64 * member, 256 * part + 64 * member + 64)
            to = slice(64 * part, 64 * part + 64)
            r_ref[to, :OWN] = d_query[rows]
            r_ref[to, OWN : 2 * OWN] = d_key[rows].astype(BF16)
            r_ref[to, 2 * OWN : 3 * OWN] = d_value[rows].astype(BF16)
            r_ref[to, 3 * OWN :] = attended[rows]


def gradient_kernel(
    spot, p0, p1, p2, p3, p4, p5, p6, p7, r0, r1, r2, r3, dt_ref, at_ref, normed0, normed1, w_qkv,
    keep, send, g_ref, p_ref, n_ref,
):
    x, y, core = spot[0], spot[1], spot[2]
    parts = (p0, p1, p2, p3, p4, p5, p6, p7)
    d_high, d_low = two_terms(dt_ref[...])
    normed = jnp.concatenate([normed0[...], normed1[...]], 0)
    g_ref[...] = dot(d_high, normed) + dot(d_low, normed)
    p_ref[...] = dot(at_ref[...], jnp.concatenate([part[1] for part in parts], 0)).T
    columns = own_columns(w_qkv, x)
    gain_row = jnp.zeros((1, C), F32)
    offset_row = jnp.zeros((1, C), F32)
    for member, r_ref in enumerate((r0, r1, r2, r3)):
        rows = jnp.concatenate([parts[member][0], parts[4 + member][0]], 0)
        d_normed = dot_nt(r_ref[:, : 3 * OWN], columns)
        gain_row += jnp.sum(d_normed * unit_of(rows)[0], 0, keepdims=True)
        offset_row += jnp.sum(d_normed, 0, keepdims=True)
    row = lax.broadcasted_iota(jnp.int32, (128, C), 0)
    n_ref[...] = jnp.where(row == 0, gain_row, jnp.where(row == 1, offset_row, 0.0)).T
    for ahead, out in ((0, keep), (1, send)):
        to_core = core if ahead == 0 else 1 - core
        for across in range(4):
            to_y = y ^ across
            for across_x in range(4):
                to_x = x ^ across_x
                block = 4 * across + across_x
                for side in range(2):
                    lanes = pl.ds(pl.multiple_of(256 * to_core + 128 * side, 128), 128)
                    for slot in range(3):
                        residue = 12 * to_y + 3 * to_x + slot
                        third_of = lax.rem(residue // 16 - x + 6, 3)
                        start = pl.multiple_of(128 * third_of + 8 * lax.rem(residue, 16), 8)
                        top = 24 * side + 8 * slot
                        out[block, top : top + 8, :] = g_ref[pl.ds(start, 8), lanes]
                for z in range(4):
                    rows = pl.ds(pl.multiple_of(128 * z + 32 * to_y + 8 * to_x, 8), 8)
                    piece = p_ref[rows, :]
                    top = 48 + 8 * (z // 2)
                    out[block, top : top + 8, 64 * (z % 2) : 64 * (z % 2) + 64] = jnp.where(
                        to_core == 0, piece[:, :64], piece[:, 64:]
                    )
                    if ahead == 0:
                        out[block, 64:, 32 * z : 32 * z + 32] = n_ref[rows, :32]
                if ahead == 1:
                    out[block, 64:, :] = jnp.zeros((8, 128), F32)


def z_parts_kernel(spot, m0, m1, m2, m3, mark, *outs):
    x, y, z = spot[0], spot[1], spot[3]
    pieces = (m0, m1, m2, m3)

    def from_member(member, rows):
        across = member ^ x
        picked = pieces[0][rows, :]
        for index in range(1, 4):
            picked = jnp.where(across == index, pieces[index][rows, :], picked)
        return picked

    total = (m0[64:, :] + m1[64:, :]) + (m2[64:, :] + m3[64:, :])
    proj = [from_member(member, slice(48, 64)) for member in range(4)]
    for to_z in range(4):
        block = []
        for side in range(2):
            for slot in range(3):
                owner = lax.rem(48 * to_z + 12 * y + 3 * x + slot, 64) // 16
                top = 24 * side + 8 * slot
                block.append(from_member(owner, slice(top, top + 8)))
        rows = slice(8 * (to_z // 2), 8 * (to_z // 2) + 8)
        lanes = slice(64 * (to_z % 2), 64 * (to_z % 2) + 64)
        for pair in range(2):
            block.append(
                jnp.concatenate([proj[2 * pair][rows, lanes], proj[2 * pair + 1][rows, lanes]], 1)
            )
        lanes = slice(32 * to_z, 32 * to_z + 32)
        block.append(jnp.concatenate([total[:, lanes], jnp.zeros((8, 96), F32)], 1))
        block = jnp.concatenate(block, 0)
        for across in range(4):
            ahead = (to_z ^ z) == across
            outs[across][...] = jnp.where(ahead, block, outs[across][...]) if to_z else block


def last_kernel(spot, near, core_in, g_out, p_out, n_out):
    mine = near[...]
    theirs = core_in[...]
    swap = spot[2] == 1
    shares = (jnp.where(swap, theirs, mine), jnp.where(swap, mine, theirs))
    for core in range(2):
        for side in range(2):
            lanes = slice(256 * core + 128 * side, 256 * core + 128 * side + 128)
            g_out[:, lanes] = shares[core][24 * side : 24 * side + 24]
    for member in range(4):
        rows = slice(48 + 8 * (member // 2), 56 + 8 * (member // 2))
        lanes = slice(64 * (member % 2), 64 * (member % 2) + 64)
        p_out[:, 128 * member : 128 * member + 128] = jnp.concatenate(
            [share[rows, lanes] for share in shares], 1
        )
    n_out[...] = (mine[64:] + theirs[64:]).T[:2]


def upper_rows(row):
    return (lax.broadcasted_iota(jnp.int32, (4, 8, C), 1) < 4) != (row == 1)


def merge_kernel(
    spot, inputs, upstream, mine_high, mine_low, other_high, other_low, output, grad_inputs
):
    upper = upper_rows(spot[4])
    for array, (source, out) in enumerate(((inputs, output), (upstream, grad_inputs))):
        for start, other, mine in ((4, other_high, mine_high), (0, other_low, mine_low)):
            rows = source[start : start + 4].astype(F32)
            from_other = other[array].astype(F32)
            from_mine = mine[array].astype(F32)
            first = rows[:, :8] + jnp.where(upper, from_other, from_mine)
            second = rows[:, 8:] + jnp.where(upper, from_mine, from_other)
            out[start : start + 4] = jnp.concatenate([first, second], 1).astype(BF16)


def token_kernel(
    spot, r0, r1, r2, r3, own0, own1, w_qkv, w_proj, norm, out, mark
):
    x = spot[0]
    projected = jnp.zeros((SLAB, C), F32)
    d_normed = jnp.zeros((SLAB, C), F32)
    for across, r_ref in enumerate((r0, r1, r2, r3)):
        rows = r_ref[...]
        member = x ^ across
        start = pl.multiple_of(OWN * member, OWN)
        projected += dot(rows[:, 3 * OWN :], w_proj[pl.ds(start, OWN), :])
        for third in range(3):
            lanes = slice(third * OWN, (third + 1) * OWN)
            columns = w_qkv[:, pl.ds(pl.multiple_of(start + C * third, OWN), OWN)]
            d_normed += dot_nt(rows[:, lanes], columns)
    mark[...] = projected[:8, :128]
    out[0] = projected.astype(BF16)
    unit, inv_scale = unit_of(jnp.concatenate([own0[0], own1[0]], 0))
    d_unit = d_normed * norm[0:1, :]
    first_mean = jnp.mean(d_unit, -1, keepdims=True)
    second_mean = jnp.mean(d_unit * unit, -1, keepdims=True)
    out[1] = (inv_scale * (d_unit - first_mean - unit * second_mean)).astype(BF16)


def call(kernel, scalars, arrays, outs, scratch=(), flops=0, moved=0):
    smem = pl.BlockSpec(memory_space=pltpu.SMEM)
    vmem = pl.BlockSpec(memory_space=pltpu.VMEM)
    return pl.pallas_call(
        kernel,
        out_shape=[jax.ShapeDtypeStruct(shape, dtype) for shape, dtype in outs],
        in_specs=[smem] + [vmem] * len(arrays),
        out_specs=[vmem] * len(outs),
        scratch_shapes=list(scratch),
        compiler_params=pltpu.CompilerParams(vmem_limit_bytes=8 * 2**20),
        cost_estimate=pl.CostEstimate(flops=flops, bytes_accessed=moved, transcendentals=0),
        name=kernel.__name__,
    )(scalars, *arrays)


def on_device(inputs, norm_params, w_qkv, w_proj, upstream):
    place = lax.axis_index("wide")
    column = lax.axis_index("narrow")
    x, y, z = place % 4, place // 4 % 4, place // 16
    core = column % 2
    row = 1 - y % 2
    window = (place - 4) % 64 // 8
    spot = jnp.stack([x, y, core, z, row]).astype(jnp.int32)
    flags = jnp.stack([4 * (window == 7), 2 * (column == 3), row, x]).astype(jnp.int32)

    own_inputs, own_upstream = inputs[0, 0], upstream[0, 0]
    upper_y = (jnp.arange(8)[:, None] < 4) != (row == 1)
    both = jnp.stack([own_inputs, own_upstream]).reshape(2, 8, 2, 8, C)
    mine = jnp.where(upper_y, both[:, :, 1], both[:, :, 0])
    other = jnp.where(upper_y, both[:, :, 0], both[:, :, 1])
    lower_in = move(mine[:, :4], lambda p, n: (p, n - 1))
    other_in = move(other[:, 4:], lambda p, n: (partner_of(p), n))
    cross_in = move(other[:, :4], lambda p, n: (partner_of(p), n - 1))

    part0 = jnp.stack([mine[:, 4:], lower_in], 1).reshape(2, SLAB // 2, C)
    parts0 = [part0] + [move(part0, over_x(mask)) for mask in (1, 2, 3)]
    part1 = jnp.stack([other_in, cross_in], 1).reshape(2, SLAB // 2, C)
    parts1 = [part1] + [move(part1, over_x(mask)) for mask in (1, 2, 3)]
    half = TOKENS // 2
    normed0, qkv0, up0 = call(
        first_kernel,
        flags,
        (*parts0, norm_params, w_qkv, w_proj),
        [((half, C), BF16), ((half, 3 * OWN), BF16), ((half, OWN), BF16)],
        flops=10_000_000_000,
        moved=3_000_000,
    )
    r0, r1, r2, r3, d_t, a_t, normed1 = call(
        attention_kernel,
        flags,
        (*parts1, normed0, qkv0, up0, norm_params, w_qkv, w_proj),
        [((SLAB, C), BF16)] * 4
        + [((3 * OWN, TOKENS), F32), ((OWN, TOKENS), BF16), ((half, C), BF16)],
        flops=1_200_000_000,
        moved=6_000_000,
    )

    keep, send = call(
        gradient_kernel,
        spot,
        (*parts0, *parts1, r0, r1, r2, r3, d_t, a_t, normed0, normed1, w_qkv),
        [((16, 72, 128), F32)] * 2,
        scratch=[
            pltpu.VMEM((3 * OWN, C), F32),
            pltpu.VMEM((C, OWN), F32),
            pltpu.VMEM((C, 128), F32),
        ],
        flops=20_000_000_000,
        moved=6_000_000,
    )
    received = move(send, over_narrow(1))
    blocks = [slice(4 * mask, 4 * mask + 4) for mask in range(4)]
    halves = [keep[block] + received[block] for block in blocks]
    halves[1:] = [half.astype(BF16) for half in halves[1:]]
    from_y = [halves[0]] + [move(halves[mask], over_y(mask)) for mask in (1, 2, 3)]
    returned = [r0] + [
        move(rows, over_x(mask)) for mask, rows in ((1, r1), (2, r2), (3, r3))
    ]
    *from_y, returned[1], returned[2] = lax.optimization_barrier(
        (*from_y, returned[1], returned[2])
    )
    back, mark = call(
        token_kernel,
        spot,
        (*returned, part0, part1, w_qkv, w_proj, norm_params),
        [((2, SLAB, C), BF16), ((8, 128), F32)],
        flops=500_000_000,
        moved=4_000_000,
    )
    share = ((72, 128), F32)
    sums = [piece.astype(F32) for piece in from_y]
    x_parts = [(sums[0][k] + sums[1][k]) + (sums[2][k] + sums[3][k]) for k in range(4)]
    from_x = [x_parts[0]] + [move(x_parts[mask], over_x(mask)) for mask in (1, 2, 3)]
    from_x[1], from_x[2], from_x[3], mark = lax.optimization_barrier(
        (from_x[1], from_x[2], from_x[3], mark)
    )
    back = back.reshape(2, 4, 4, 8, C)
    crossed = move(back[:, 2:], lambda p, n: (partner_of(p), n))
    z_parts = call(z_parts_kernel, spot, (*from_x, mark), [share] * 4)
    line = [z_parts[0]] + [move(z_parts[mask], over_z(mask)) for mask in (1, 2, 3)]
    line[1], line[2], line[3], crossed = lax.optimization_barrier(
        (line[1], line[2], line[3], crossed)
    )
    line = (line[0] + line[1]) + (line[2] + line[3])
    across = move(line, over_narrow(2))
    lower = move(jnp.stack([back[:, 1], crossed[:, 1]], 1), lambda p, n: (p, n + 1))
    output, grad_inputs = call(
        merge_kernel,
        spot,
        (own_inputs, own_upstream, back[:, 0], lower[:, 0], crossed[:, 0], lower[:, 1]),
        [((8, 16, C), BF16)] * 2,
    )
    across, output, grad_inputs = lax.optimization_barrier((across, output, grad_inputs))
    line = line + across
    grad_qkv, grad_proj, grad_norm = call(
        last_kernel,
        spot,
        (line, move(line, over_narrow(1))),
        [((24, C), F32), ((8, C), F32), ((2, 8), F32)],
    )
    return (
        output[None, None], grad_inputs[None, None], grad_qkv.T, grad_proj.T, grad_norm
    )


def solution(mesh):
    in_specs = (
        P(None, "wide", "narrow", None, None),
        P(),
        P(),
        P(),
        P(None, "wide", "narrow", None, None),
    )
    out_specs = (
        P(None, "wide", "narrow", None, None),
        P(None, "wide", "narrow", None, None),
        P(None, "wide"),
        P(None, "wide"),
        P(None, "wide"),
    )
    return jax.shard_map(
        on_device, mesh=mesh, in_specs=in_specs, out_specs=out_specs, check_vma=False
    )
```

```python
import jax
import jax.numpy as jnp
from jax import lax
from jax.experimental import pallas as pl
from jax.experimental.pallas import tpu as pltpu
from jax.sharding import PartitionSpec as P

HEADS = 16
HEAD_DIM = 32
C = 512
WIN = 8
RING = 4
OWN = C // RING
SLAB = 128
TOKENS = RING * SLAB
BLOCK = 256
CHUNK = 64
SCALE = HEAD_DIM**-0.5
LOG2E = 1.4426950408889634
F32 = jnp.float32
BF16 = jnp.bfloat16


def move(value, target):
    pairs = []
    for place in range(64):
        for column in range(4):
            to_place, to_column = target(place, column)
            pairs.append((place * 4 + column, (to_place % 64) * 4 + to_column % 4))
    return lax.ppermute(value, ("wide", "narrow"), pairs)


def partner_of(place):
    return place + 4 if (place // 4) % 2 else place - 4


def over_x(mask):
    return lambda p, n: (p ^ mask, n)


def over_y(mask):
    return lambda p, n: (p ^ (4 * mask), n)


def over_z(mask):
    return lambda p, n: (p ^ (16 * mask), n)


def over_narrow(mask):
    return lambda p, n: (p, n ^ mask)


def dot(a, b):
    return lax.dot_general(a, b, (((1,), (0,)), ((), ())), preferred_element_type=F32)


def dot_nt(a, b):
    return lax.dot_general(a, b, (((1,), (1,)), ((), ())), preferred_element_type=F32)


def unit_of(rows):
    floats = rows.astype(F32)
    average = jnp.mean(floats, -1, keepdims=True)
    centered = floats - average
    variance = jnp.mean(centered * centered, -1, keepdims=True)
    inv_scale = lax.rsqrt(variance + 1e-05)
    return centered * inv_scale, inv_scale


def two_terms(value):
    high = value.astype(BF16)
    low = (value - high.astype(F32)).astype(BF16)
    return high, low


def own_columns(w_qkv, x):
    start = pl.multiple_of(OWN * x, OWN)
    return jnp.concatenate(
        [w_qkv[:, pl.ds(pl.multiple_of(start + C * third, OWN), OWN)] for third in range(3)], 1
    )


def project(parts, norm, w_qkv, w_proj, member):
    unit, _ = unit_of(jnp.concatenate([part[0] for part in parts], 0))
    normed = (unit * norm[0:1, :] + norm[1:2, :]).astype(BF16)
    qkv = dot(normed, own_columns(w_qkv, member)).astype(BF16)
    rows = w_proj[pl.ds(pl.multiple_of(OWN * member, OWN), OWN), :]
    cotangent = dot_nt(jnp.concatenate([part[1] for part in parts], 0), rows).astype(BF16)
    return normed, qkv, cotangent


def first_kernel(flags, p0, p1, p2, p3, norm, w_qkv, w_proj, normed_ref, qkv_ref, up_ref):
    normed_ref[...], qkv_ref[...], up_ref[...] = project(
        (p0, p1, p2, p3), norm, w_qkv, w_proj, flags[3]
    )


def attention_kernel(
    flags, p0, p1, p2, p3, normed0, qkv0, up0, norm, w_qkv, w_proj,
    r0, r1, r2, r3, dt_ref, at_ref, normed1,
):
    normed1[...], qkv1, up1 = project((p0, p1, p2, p3), norm, w_qkv, w_proj, flags[3])
    qkv = jnp.concatenate([qkv0[...], qkv1], 0)
    cotangent = jnp.concatenate([up0[...], up1], 0)
    queries = qkv[:, :OWN]
    keys = qkv[:, OWN : 2 * OWN]
    values = qkv[:, 2 * OWN :]
    queries_t = queries.T
    cotangent_t = cotangent.T
    keys_t = keys.T
    values_t = values.T

    def label(shape, dim):
        token = lax.broadcasted_iota(jnp.int32, shape, dim)
        row = token // 256
        half = (token // 32) % 2
        low_y = (token // 4) % 2
        return row * flags[0] + half * flags[1] + low_y * flags[2]

    key_label = label((TOKENS, 1), 0)
    query_label = label((1, TOKENS), 1)
    def heads_of(rows):
        lane_head = lax.broadcasted_iota(jnp.int32, rows.shape, 1) // HEAD_DIM
        return [jnp.where(lane_head == head, rows, jnp.zeros_like(rows)) for head in range(RING)]

    key_heads, value_heads = heads_of(keys), heads_of(values)
    d_key = jnp.zeros((TOKENS, OWN), F32)
    d_value = jnp.zeros((TOKENS, OWN), F32)
    for block in range(TOKENS // BLOCK):
        span = slice(block * BLOCK, (block + 1) * BLOCK)
        allowed = key_label == query_label[:, span]
        block_scores, block_probs = [], []
        for head in range(RING):
            rows = slice(head * HEAD_DIM, (head + 1) * HEAD_DIM)
            key_head, value_head = key_heads[head], value_heads[head]
            scores = jnp.where(allowed, dot(key_head, queries_t[:, span]), -1e30)
            highest = jnp.max(scores, 0, keepdims=True)
            d_probs = dot(value_head, cotangent_t[:, span])
            weights = []
            total = jnp.zeros((8, BLOCK), F32)
            inner = jnp.zeros((8, BLOCK), F32)
            for start in range(0, TOKENS, CHUNK):
                part = slice(start, start + CHUNK)
                weight = jnp.exp2((scores[part] - highest) * (SCALE * LOG2E))
                total += jnp.sum(weight.reshape(CHUNK // 8, 8, BLOCK), 0)
                inner += jnp.sum((weight * d_probs[part]).reshape(CHUNK // 8, 8, BLOCK), 0)
                weights.append(weight)
            over = 1.0 / jnp.sum(total, 0, keepdims=True)
            inner = jnp.sum(inner, 0, keepdims=True) * over
            over_scaled = over * SCALE
            probs_low, d_scores = [], []
            for index, weight in enumerate(weights):
                part = slice(index * CHUNK, (index + 1) * CHUNK)
                probs_low.append((weight * over).astype(BF16))
                d_scores.append(((weight * over_scaled) * (d_probs[part] - inner)).astype(BF16))
            probs_low = jnp.concatenate(probs_low, 0)
            d_scores = jnp.concatenate(d_scores, 0)
            at_ref[rows, span] = dot(values_t[rows], probs_low).astype(BF16)
            dt_ref[rows, span] = dot(keys_t[rows], d_scores)
            block_scores.append(d_scores)
            block_probs.append(probs_low)
        query_heads = jnp.concatenate(heads_of(queries[span]), 0)
        cotangent_heads = jnp.concatenate(heads_of(cotangent[span]), 0)
        d_key += dot(jnp.concatenate(block_scores, 1), query_heads)
        d_value += dot(jnp.concatenate(block_probs, 1), cotangent_heads)
    dt_ref[OWN : 2 * OWN, :] = d_key.T
    dt_ref[2 * OWN :, :] = d_value.T
    d_query = dt_ref[:OWN, :].T.astype(BF16)
    attended = at_ref[...].T
    for member, r_ref in enumerate((r0, r1, r2, r3)):
        for part in range(2):
            rows = slice(256 * part + 64 * member, 256 * part + 64 * member + 64)
            to = slice(64 * part, 64 * part + 64)
            r_ref[to, :OWN] = d_query[rows]
            r_ref[to, OWN : 2 * OWN] = d_key[rows].astype(BF16)
            r_ref[to, 2 * OWN : 3 * OWN] = d_value[rows].astype(BF16)
            r_ref[to, 3 * OWN :] = attended[rows]


def gradient_kernel(
    spot, p0, p1, p2, p3, p4, p5, p6, p7, r0, r1, r2, r3, dt_ref, at_ref, normed0, normed1, w_qkv,
    keep, send, g_ref, p_ref, n_ref,
):
    x, y, core = spot[0], spot[1], spot[2]
    parts = (p0, p1, p2, p3, p4, p5, p6, p7)
    d_high, d_low = two_terms(dt_ref[...])
    normed = jnp.concatenate([normed0[...], normed1[...]], 0)
    g_ref[...] = dot(d_high, normed) + dot(d_low, normed)
    p_ref[...] = dot(at_ref[...], jnp.concatenate([part[1] for part in parts], 0)).T
    columns = own_columns(w_qkv, x)
    gain_row = jnp.zeros((1, C), F32)
    offset_row = jnp.zeros((1, C), F32)
    for member, r_ref in enumerate((r0, r1, r2, r3)):
        rows = jnp.concatenate([parts[member][0], parts[4 + member][0]], 0)
        d_normed = dot_nt(r_ref[:, : 3 * OWN], columns)
        gain_row += jnp.sum(d_normed * unit_of(rows)[0], 0, keepdims=True)
        offset_row += jnp.sum(d_normed, 0, keepdims=True)
    row = lax.broadcasted_iota(jnp.int32, (128, C), 0)
    n_ref[...] = jnp.where(row == 0, gain_row, jnp.where(row == 1, offset_row, 0.0)).T
    for ahead, out in ((0, keep), (1, send)):
        to_core = core if ahead == 0 else 1 - core
        for across in range(4):
            to_y = y ^ across
            for across_x in range(4):
                to_x = x ^ across_x
                block = 4 * across + across_x
                for side in range(2):
                    lanes = pl.ds(pl.multiple_of(256 * to_core + 128 * side, 128), 128)
                    for slot in range(3):
                        residue = 12 * to_y + 3 * to_x + slot
                        third_of = lax.rem(residue // 16 - x + 6, 3)
                        start = pl.multiple_of(128 * third_of + 8 * lax.rem(residue, 16), 8)
                        top = 24 * side + 8 * slot
                        out[block, top : top + 8, :] = g_ref[pl.ds(start, 8), lanes]
                for z in range(4):
                    rows = pl.ds(pl.multiple_of(128 * z + 32 * to_y + 8 * to_x, 8), 8)
                    piece = p_ref[rows, :]
                    top = 48 + 8 * (z // 2)
                    out[block, top : top + 8, 64 * (z % 2) : 64 * (z % 2) + 64] = jnp.where(
                        to_core == 0, piece[:, :64], piece[:, 64:]
                    )
                    if ahead == 0:
                        out[block, 64:, 32 * z : 32 * z + 32] = n_ref[rows, :32]
                if ahead == 1:
                    out[block, 64:, :] = jnp.zeros((8, 128), F32)


def z_parts_kernel(spot, m0, m1, m2, m3, mark, *outs):
    x, y, z = spot[0], spot[1], spot[3]
    pieces = (m0, m1, m2, m3)

    def from_member(member, rows):
        across = member ^ x
        picked = pieces[0][rows, :]
        for index in range(1, 4):
            picked = jnp.where(across == index, pieces[index][rows, :], picked)
        return picked

    total = (m0[64:, :] + m1[64:, :]) + (m2[64:, :] + m3[64:, :])
    proj = [from_member(member, slice(48, 64)) for member in range(4)]
    for to_z in range(4):
        block = []
        for side in range(2):
            for slot in range(3):
                owner = lax.rem(48 * to_z + 12 * y + 3 * x + slot, 64) // 16
                top = 24 * side + 8 * slot
                block.append(from_member(owner, slice(top, top + 8)))
        rows = slice(8 * (to_z // 2), 8 * (to_z // 2) + 8)
        lanes = slice(64 * (to_z % 2), 64 * (to_z % 2) + 64)
        for pair in range(2):
            block.append(
                jnp.concatenate([proj[2 * pair][rows, lanes], proj[2 * pair + 1][rows, lanes]], 1)
            )
        lanes = slice(32 * to_z, 32 * to_z + 32)
        block.append(jnp.concatenate([total[:, lanes], jnp.zeros((8, 96), F32)], 1))
        block = jnp.concatenate(block, 0)
        for across in range(4):
            ahead = (to_z ^ z) == across
            outs[across][...] = jnp.where(ahead, block, outs[across][...]) if to_z else block


def last_kernel(spot, near, core_in, z_in, both_in, g_out, p_out, n_out):
    mine = near[...] + z_in[...]
    theirs = core_in[...] + both_in[...]
    swap = spot[2] == 1
    shares = (jnp.where(swap, theirs, mine), jnp.where(swap, mine, theirs))
    for core in range(2):
        for side in range(2):
            lanes = slice(256 * core + 128 * side, 256 * core + 128 * side + 128)
            g_out[:, lanes] = shares[core][24 * side : 24 * side + 24]
    for member in range(4):
        rows = slice(48 + 8 * (member // 2), 56 + 8 * (member // 2))
        lanes = slice(64 * (member % 2), 64 * (member % 2) + 64)
        p_out[:, 128 * member : 128 * member + 128] = jnp.concatenate(
            [share[rows, lanes] for share in shares], 1
        )
    n_out[...] = (mine[64:] + theirs[64:]).T[:2]


def upper_rows(row):
    return (lax.broadcasted_iota(jnp.int32, (4, 8, C), 1) < 4) != (row == 1)


def merge_kernel(
    spot, inputs, upstream, mine_high, mine_low, other_high, other_low, output, grad_inputs
):
    upper = upper_rows(spot[4])
    for array, (source, out) in enumerate(((inputs, output), (upstream, grad_inputs))):
        for start, other, mine in ((4, other_high, mine_high), (0, other_low, mine_low)):
            rows = source[start : start + 4].astype(F32)
            from_other = other[array].astype(F32)
            from_mine = mine[array].astype(F32)
            first = rows[:, :8] + jnp.where(upper, from_other, from_mine)
            second = rows[:, 8:] + jnp.where(upper, from_mine, from_other)
            out[start : start + 4] = jnp.concatenate([first, second], 1).astype(BF16)


def token_kernel(
    spot, r0, r1, r2, r3, own0, own1, w_qkv, w_proj, norm, out, mark
):
    x = spot[0]
    projected = jnp.zeros((SLAB, C), F32)
    d_normed = jnp.zeros((SLAB, C), F32)
    for across, r_ref in enumerate((r0, r1, r2, r3)):
        rows = r_ref[...]
        member = x ^ across
        start = pl.multiple_of(OWN * member, OWN)
        projected += dot(rows[:, 3 * OWN :], w_proj[pl.ds(start, OWN), :])
        for third in range(3):
            lanes = slice(third * OWN, (third + 1) * OWN)
            columns = w_qkv[:, pl.ds(pl.multiple_of(start + C * third, OWN), OWN)]
            d_normed += dot_nt(rows[:, lanes], columns)
    mark[...] = projected[:8, :128]
    out[0] = projected.astype(BF16)
    unit, inv_scale = unit_of(jnp.concatenate([own0[0], own1[0]], 0))
    d_unit = d_normed * norm[0:1, :]
    first_mean = jnp.mean(d_unit, -1, keepdims=True)
    second_mean = jnp.mean(d_unit * unit, -1, keepdims=True)
    out[1] = (inv_scale * (d_unit - first_mean - unit * second_mean)).astype(BF16)


def call(kernel, scalars, arrays, outs, scratch=(), flops=0, moved=0):
    smem = pl.BlockSpec(memory_space=pltpu.SMEM)
    vmem = pl.BlockSpec(memory_space=pltpu.VMEM)
    return pl.pallas_call(
        kernel,
        out_shape=[jax.ShapeDtypeStruct(shape, dtype) for shape, dtype in outs],
        in_specs=[smem] + [vmem] * len(arrays),
        out_specs=[vmem] * len(outs),
        scratch_shapes=list(scratch),
        compiler_params=pltpu.CompilerParams(vmem_limit_bytes=8 * 2**20),
        cost_estimate=pl.CostEstimate(flops=flops, bytes_accessed=moved, transcendentals=0),
        name=kernel.__name__,
    )(scalars, *arrays)


def on_device(inputs, norm_params, w_qkv, w_proj, upstream):
    place = lax.axis_index("wide")
    column = lax.axis_index("narrow")
    x, y, z = place % 4, place // 4 % 4, place // 16
    core = column % 2
    row = 1 - y % 2
    window = (place - 4) % 64 // 8
    spot = jnp.stack([x, y, core, z, row]).astype(jnp.int32)
    flags = jnp.stack([4 * (window == 7), 2 * (column == 3), row, x]).astype(jnp.int32)

    own_inputs, own_upstream = inputs[0, 0], upstream[0, 0]
    upper_y = (jnp.arange(8)[:, None] < 4) != (row == 1)
    both = jnp.stack([own_inputs, own_upstream]).reshape(2, 8, 2, 8, C)
    mine = jnp.where(upper_y, both[:, :, 1], both[:, :, 0])
    other = jnp.where(upper_y, both[:, :, 0], both[:, :, 1])
    lower_in = move(mine[:, :4], lambda p, n: (p, n - 1))
    other_in = move(other[:, 4:], lambda p, n: (partner_of(p), n))
    cross_in = move(other[:, :4], lambda p, n: (partner_of(p), n - 1))

    part0 = jnp.stack([mine[:, 4:], lower_in], 1).reshape(2, SLAB // 2, C)
    parts0 = [part0] + [move(part0, over_x(mask)) for mask in (1, 2, 3)]
    part1 = jnp.stack([other_in, cross_in], 1).reshape(2, SLAB // 2, C)
    parts1 = [part1] + [move(part1, over_x(mask)) for mask in (1, 2, 3)]
    half = TOKENS // 2
    normed0, qkv0, up0 = call(
        first_kernel,
        flags,
        (*parts0, norm_params, w_qkv, w_proj),
        [((half, C), BF16), ((half, 3 * OWN), BF16), ((half, OWN), BF16)],
        flops=10_000_000_000,
        moved=3_000_000,
    )
    r0, r1, r2, r3, d_t, a_t, normed1 = call(
        attention_kernel,
        flags,
        (*parts1, normed0, qkv0, up0, norm_params, w_qkv, w_proj),
        [((SLAB, C), BF16)] * 4
        + [((3 * OWN, TOKENS), F32), ((OWN, TOKENS), BF16), ((half, C), BF16)],
        flops=1_200_000_000,
        moved=6_000_000,
    )

    keep, send = call(
        gradient_kernel,
        spot,
        (*parts0, *parts1, r0, r1, r2, r3, d_t, a_t, normed0, normed1, w_qkv),
        [((16, 72, 128), F32)] * 2,
        scratch=[
            pltpu.VMEM((3 * OWN, C), F32),
            pltpu.VMEM((C, OWN), F32),
            pltpu.VMEM((C, 128), F32),
        ],
        flops=20_000_000_000,
        moved=6_000_000,
    )
    received = move(send, over_narrow(1))
    blocks = [slice(4 * mask, 4 * mask + 4) for mask in range(4)]
    halves = [keep[block] + received[block] for block in blocks]
    halves[1:] = [half.astype(BF16) for half in halves[1:]]
    from_y = [halves[0]] + [move(halves[mask], over_y(mask)) for mask in (1, 2, 3)]
    returned = [r0] + [
        move(rows, over_x(mask)) for mask, rows in ((1, r1), (2, r2), (3, r3))
    ]
    *from_y, returned[1], returned[2] = lax.optimization_barrier(
        (*from_y, returned[1], returned[2])
    )
    back, mark = call(
        token_kernel,
        spot,
        (*returned, part0, part1, w_qkv, w_proj, norm_params),
        [((2, SLAB, C), BF16), ((8, 128), F32)],
        flops=500_000_000,
        moved=4_000_000,
    )
    share = ((72, 128), F32)
    sums = [piece.astype(F32) for piece in from_y]
    x_parts = [(sums[0][k] + sums[1][k]) + (sums[2][k] + sums[3][k]) for k in range(4)]
    from_x = [x_parts[0]] + [move(x_parts[mask], over_x(mask)) for mask in (1, 2, 3)]
    from_x[1], from_x[2], from_x[3], mark = lax.optimization_barrier(
        (from_x[1], from_x[2], from_x[3], mark)
    )
    back = back.reshape(2, 4, 4, 8, C)
    crossed = move(back[:, 2:], lambda p, n: (partner_of(p), n))
    z_parts = call(z_parts_kernel, spot, (*from_x, mark), [share] * 4)
    line = [z_parts[0]] + [move(z_parts[mask], over_z(mask)) for mask in (1, 2, 3)]
    line[1], line[2], line[3], crossed = lax.optimization_barrier(
        (line[1], line[2], line[3], crossed)
    )
    line = (line[0] + line[1]) + (line[2] + line[3])
    last = [line] + [move(line, over_narrow(mask)) for mask in (1, 2, 3)]
    lower = move(jnp.stack([back[:, 1], crossed[:, 1]], 1), lambda p, n: (p, n + 1))
    output, grad_inputs = call(
        merge_kernel,
        spot,
        (own_inputs, own_upstream, back[:, 0], lower[:, 0], crossed[:, 0], lower[:, 1]),
        [((8, 16, C), BF16)] * 2,
    )
    last[1], last[2], last[3], output, grad_inputs = lax.optimization_barrier(
        (last[1], last[2], last[3], output, grad_inputs)
    )
    grad_qkv, grad_proj, grad_norm = call(
        last_kernel, spot, last, [((24, C), F32), ((8, C), F32), ((2, 8), F32)]
    )
    return (
        output[None, None], grad_inputs[None, None], grad_qkv.T, grad_proj.T, grad_norm
    )


def solution(mesh):
    in_specs = (
        P(None, "wide", "narrow", None, None),
        P(),
        P(),
        P(),
        P(None, "wide", "narrow", None, None),
    )
    out_specs = (
        P(None, "wide", "narrow", None, None),
        P(None, "wide", "narrow", None, None),
        P(None, "wide"),
        P(None, "wide"),
        P(None, "wide"),
    )
    return jax.shard_map(
        on_device, mesh=mesh, in_specs=in_specs, out_specs=out_specs, check_vma=False
    )
```

```python
import jax
import jax.numpy as jnp
from jax import lax
from jax.experimental import pallas as pl
from jax.experimental.pallas import tpu as pltpu
from jax.sharding import PartitionSpec as P

HEADS = 16
HEAD_DIM = 32
C = 512
WIN = 8
RING = 4
OWN = C // RING
SLAB = 128
TOKENS = RING * SLAB
BLOCK = 256
CHUNK = 64
SCALE = HEAD_DIM**-0.5
LOG2E = 1.4426950408889634
F32 = jnp.float32
BF16 = jnp.bfloat16


def move(value, target):
    pairs = []
    for place in range(64):
        for column in range(4):
            to_place, to_column = target(place, column)
            pairs.append((place * 4 + column, (to_place % 64) * 4 + to_column % 4))
    return lax.ppermute(value, ("wide", "narrow"), pairs)


def partner_of(place):
    return place + 4 if (place // 4) % 2 else place - 4


def over_x(mask):
    return lambda p, n: (p ^ mask, n)


def over_y(mask):
    return lambda p, n: (p ^ (4 * mask), n)


def over_z(mask):
    return lambda p, n: (p ^ (16 * mask), n)


def over_narrow(mask):
    return lambda p, n: (p, n ^ mask)


def dot(a, b):
    return lax.dot_general(a, b, (((1,), (0,)), ((), ())), preferred_element_type=F32)


def dot_nt(a, b):
    return lax.dot_general(a, b, (((1,), (1,)), ((), ())), preferred_element_type=F32)


def unit_of(rows):
    floats = rows.astype(F32)
    average = jnp.mean(floats, -1, keepdims=True)
    centered = floats - average
    variance = jnp.mean(centered * centered, -1, keepdims=True)
    inv_scale = lax.rsqrt(variance + 1e-05)
    return centered * inv_scale, inv_scale


def two_terms(value):
    high = value.astype(BF16)
    low = (value - high.astype(F32)).astype(BF16)
    return high, low


def own_columns(w_qkv, x):
    start = pl.multiple_of(OWN * x, OWN)
    return jnp.concatenate(
        [w_qkv[:, pl.ds(pl.multiple_of(start + C * third, OWN), OWN)] for third in range(3)], 1
    )


def project(parts, norm, w_qkv, w_proj, member):
    tokens = jnp.concatenate([part[0] for part in parts], 0)
    unit, inv_scale = unit_of(tokens)
    average = jnp.mean(tokens.astype(F32), -1, keepdims=True)
    lane = lax.broadcasted_iota(jnp.int32, (tokens.shape[0], 128), 1)
    stats = jnp.where(lane == 0, average, inv_scale)
    normed = (unit * norm[0:1, :] + norm[1:2, :]).astype(BF16)
    qkv = dot(normed, own_columns(w_qkv, member)).astype(BF16)
    rows = w_proj[pl.ds(pl.multiple_of(OWN * member, OWN), OWN), :]
    cotangent = dot_nt(jnp.concatenate([part[1] for part in parts], 0), rows).astype(BF16)
    return normed, qkv, cotangent, stats


def first_kernel(
    flags, p0, p1, p2, p3, norm, w_qkv, w_proj, normed_ref, qkv_ref, up_ref, stats
):
    normed_ref[...], qkv_ref[...], up_ref[...], stats[...] = project(
        (p0, p1, p2, p3), norm, w_qkv, w_proj, flags[3]
    )


def attention_kernel(
    flags, p0, p1, p2, p3, normed0, qkv0, up0, norm, w_qkv, w_proj,
    r0, r1, r2, r3, dt_ref, at_ref, normed1, stats,
):
    normed1[...], qkv1, up1, stats[...] = project((p0, p1, p2, p3), norm, w_qkv, w_proj, flags[3])
    qkv = jnp.concatenate([qkv0[...], qkv1], 0)
    cotangent = jnp.concatenate([up0[...], up1], 0)
    queries = qkv[:, :OWN]
    keys = qkv[:, OWN : 2 * OWN]
    values = qkv[:, 2 * OWN :]
    queries_t = queries.T
    cotangent_t = cotangent.T
    keys_t = keys.T
    values_t = values.T

    def label(shape, dim):
        token = lax.broadcasted_iota(jnp.int32, shape, dim)
        row = token // 256
        half = (token // 32) % 2
        low_y = (token // 4) % 2
        return row * flags[0] + half * flags[1] + low_y * flags[2]

    key_label = label((TOKENS, 1), 0)
    query_label = label((1, TOKENS), 1)
    def heads_of(rows):
        lane_head = lax.broadcasted_iota(jnp.int32, rows.shape, 1) // HEAD_DIM
        return [jnp.where(lane_head == head, rows, jnp.zeros_like(rows)) for head in range(RING)]

    key_heads, value_heads = heads_of(keys), heads_of(values)
    d_key = jnp.zeros((TOKENS, OWN), F32)
    d_value = jnp.zeros((TOKENS, OWN), F32)
    for block in range(TOKENS // BLOCK):
        span = slice(block * BLOCK, (block + 1) * BLOCK)
        allowed = key_label == query_label[:, span]
        block_scores, block_probs = [], []
        for head in range(RING):
            rows = slice(head * HEAD_DIM, (head + 1) * HEAD_DIM)
            key_head, value_head = key_heads[head], value_heads[head]
            scores = jnp.where(allowed, dot(key_head, queries_t[:, span]), -1e30)
            highest = jnp.max(scores, 0, keepdims=True)
            d_probs = dot(value_head, cotangent_t[:, span])
            weights = []
            total = jnp.zeros((8, BLOCK), F32)
            inner = jnp.zeros((8, BLOCK), F32)
            for start in range(0, TOKENS, CHUNK):
                part = slice(start, start + CHUNK)
                weight = jnp.exp2((scores[part] - highest) * (SCALE * LOG2E))
                total += jnp.sum(weight.reshape(CHUNK // 8, 8, BLOCK), 0)
                inner += jnp.sum((weight * d_probs[part]).reshape(CHUNK // 8, 8, BLOCK), 0)
                weights.append(weight)
            over = 1.0 / jnp.sum(total, 0, keepdims=True)
            inner = jnp.sum(inner, 0, keepdims=True) * over
            over_scaled = over * SCALE
            probs_low, d_scores = [], []
            for index, weight in enumerate(weights):
                part = slice(index * CHUNK, (index + 1) * CHUNK)
                probs_low.append((weight * over).astype(BF16))
                d_scores.append(((weight * over_scaled) * (d_probs[part] - inner)).astype(BF16))
            probs_low = jnp.concatenate(probs_low, 0)
            d_scores = jnp.concatenate(d_scores, 0)
            at_ref[rows, span] = dot(values_t[rows], probs_low).astype(BF16)
            dt_ref[rows, span] = dot(keys_t[rows], d_scores)
            block_scores.append(d_scores)
            block_probs.append(probs_low)
        query_heads = jnp.concatenate(heads_of(queries[span]), 0)
        cotangent_heads = jnp.concatenate(heads_of(cotangent[span]), 0)
        d_key += dot(jnp.concatenate(block_scores, 1), query_heads)
        d_value += dot(jnp.concatenate(block_probs, 1), cotangent_heads)
    dt_ref[OWN : 2 * OWN, :] = d_key.T
    dt_ref[2 * OWN :, :] = d_value.T
    d_query = dt_ref[:OWN, :].T.astype(BF16)
    attended = at_ref[...].T
    for member, r_ref in enumerate((r0, r1, r2, r3)):
        for part in range(2):
            rows = slice(256 * part + 64 * member, 256 * part + 64 * member + 64)
            to = slice(64 * part, 64 * part + 64)
            r_ref[to, :OWN] = d_query[rows]
            r_ref[to, OWN : 2 * OWN] = d_key[rows].astype(BF16)
            r_ref[to, 2 * OWN : 3 * OWN] = d_value[rows].astype(BF16)
            r_ref[to, 3 * OWN :] = attended[rows]


def gradient_kernel(
    spot, p0, p1, p2, p3, p4, p5, p6, p7, r0, r1, r2, r3, dt_ref, at_ref, normed0, normed1,
    stats0, stats1, w_qkv, keep, send, g_ref, p_ref, n_ref,
):
    x, y, core = spot[0], spot[1], spot[2]
    parts = (p0, p1, p2, p3, p4, p5, p6, p7)
    d_high, d_low = two_terms(dt_ref[...])
    normed = jnp.concatenate([normed0[...], normed1[...]], 0)
    g_ref[...] = dot(d_high, normed) + dot(d_low, normed)
    p_ref[...] = dot(at_ref[...], jnp.concatenate([part[1] for part in parts], 0)).T
    columns = own_columns(w_qkv, x)
    gain_row = jnp.zeros((1, C), F32)
    offset_row = jnp.zeros((1, C), F32)
    for member, r_ref in enumerate((r0, r1, r2, r3)):
        rows = jnp.concatenate([parts[member][0], parts[4 + member][0]], 0).astype(F32)
        place = slice(64 * member, 64 * member + 64)
        stats = jnp.concatenate([stats0[place, :], stats1[place, :]], 0)
        unit = (rows - stats[:, 0:1]) * stats[:, 1:2]
        d_normed = dot_nt(r_ref[:, : 3 * OWN], columns)
        gain_row += jnp.sum(d_normed * unit, 0, keepdims=True)
        offset_row += jnp.sum(d_normed, 0, keepdims=True)
    row = lax.broadcasted_iota(jnp.int32, (128, C), 0)
    n_ref[...] = jnp.where(row == 0, gain_row, jnp.where(row == 1, offset_row, 0.0)).T
    for ahead, out in ((0, keep), (1, send)):
        to_core = core if ahead == 0 else 1 - core
        for across in range(4):
            to_y = y ^ across
            for across_x in range(4):
                to_x = x ^ across_x
                block = 4 * across + across_x
                for side in range(2):
                    lanes = pl.ds(pl.multiple_of(256 * to_core + 128 * side, 128), 128)
                    for slot in range(3):
                        residue = 12 * to_y + 3 * to_x + slot
                        third_of = lax.rem(residue // 16 - x + 6, 3)
                        start = pl.multiple_of(128 * third_of + 8 * lax.rem(residue, 16), 8)
                        top = 24 * side + 8 * slot
                        out[block, top : top + 8, :] = g_ref[pl.ds(start, 8), lanes]
                for z in range(4):
                    rows = pl.ds(pl.multiple_of(128 * z + 32 * to_y + 8 * to_x, 8), 8)
                    piece = p_ref[rows, :]
                    top = 48 + 8 * (z // 2)
                    out[block, top : top + 8, 64 * (z % 2) : 64 * (z % 2) + 64] = jnp.where(
                        to_core == 0, piece[:, :64], piece[:, 64:]
                    )
                    if ahead == 0:
                        out[block, 64:, 32 * z : 32 * z + 32] = n_ref[rows, :32]
                if ahead == 1:
                    out[block, 64:, :] = jnp.zeros((8, 128), F32)


def z_parts_kernel(spot, m0, m1, m2, m3, mark, *outs):
    x, y, z = spot[0], spot[1], spot[3]
    pieces = (m0, m1, m2, m3)

    def from_member(member, rows):
        across = member ^ x
        picked = pieces[0][rows, :]
        for index in range(1, 4):
            picked = jnp.where(across == index, pieces[index][rows, :], picked)
        return picked

    total = (m0[64:, :] + m1[64:, :]) + (m2[64:, :] + m3[64:, :])
    proj = [from_member(member, slice(48, 64)) for member in range(4)]
    for to_z in range(4):
        block = []
        for side in range(2):
            for slot in range(3):
                owner = lax.rem(48 * to_z + 12 * y + 3 * x + slot, 64) // 16
                top = 24 * side + 8 * slot
                block.append(from_member(owner, slice(top, top + 8)))
        rows = slice(8 * (to_z // 2), 8 * (to_z // 2) + 8)
        lanes = slice(64 * (to_z % 2), 64 * (to_z % 2) + 64)
        for pair in range(2):
            block.append(
                jnp.concatenate([proj[2 * pair][rows, lanes], proj[2 * pair + 1][rows, lanes]], 1)
            )
        lanes = slice(32 * to_z, 32 * to_z + 32)
        block.append(jnp.concatenate([total[:, lanes], jnp.zeros((8, 96), F32)], 1))
        block = jnp.concatenate(block, 0)
        for across in range(4):
            ahead = (to_z ^ z) == across
            outs[across][...] = jnp.where(ahead, block, outs[across][...]) if to_z else block


def last_kernel(spot, near, core_in, z_in, both_in, g_out, p_out, n_out):
    mine = near[...] + z_in[...]
    theirs = core_in[...] + both_in[...]
    swap = spot[2] == 1
    shares = (jnp.where(swap, theirs, mine), jnp.where(swap, mine, theirs))
    for core in range(2):
        for side in range(2):
            lanes = slice(256 * core + 128 * side, 256 * core + 128 * side + 128)
            g_out[:, lanes] = shares[core][24 * side : 24 * side + 24]
    for member in range(4):
        rows = slice(48 + 8 * (member // 2), 56 + 8 * (member // 2))
        lanes = slice(64 * (member % 2), 64 * (member % 2) + 64)
        p_out[:, 128 * member : 128 * member + 128] = jnp.concatenate(
            [share[rows, lanes] for share in shares], 1
        )
    n_out[...] = (mine[64:] + theirs[64:]).T[:2]


def upper_rows(row):
    return (lax.broadcasted_iota(jnp.int32, (4, 8, C), 1) < 4) != (row == 1)


def merge_kernel(
    spot, inputs, upstream, mine_high, mine_low, other_high, other_low, output, grad_inputs
):
    upper = upper_rows(spot[4])
    for array, (source, out) in enumerate(((inputs, output), (upstream, grad_inputs))):
        for start, other, mine in ((4, other_high, mine_high), (0, other_low, mine_low)):
            rows = source[start : start + 4].astype(F32)
            from_other = other[array].astype(F32)
            from_mine = mine[array].astype(F32)
            first = rows[:, :8] + jnp.where(upper, from_other, from_mine)
            second = rows[:, 8:] + jnp.where(upper, from_mine, from_other)
            out[start : start + 4] = jnp.concatenate([first, second], 1).astype(BF16)


def token_kernel(
    spot, r0, r1, r2, r3, own0, own1, w_qkv, w_proj, norm, out, mark
):
    x = spot[0]
    projected = jnp.zeros((SLAB, C), F32)
    d_normed = jnp.zeros((SLAB, C), F32)
    for across, r_ref in enumerate((r0, r1, r2, r3)):
        rows = r_ref[...]
        member = x ^ across
        start = pl.multiple_of(OWN * member, OWN)
        projected += dot(rows[:, 3 * OWN :], w_proj[pl.ds(start, OWN), :])
        for third in range(3):
            lanes = slice(third * OWN, (third + 1) * OWN)
            columns = w_qkv[:, pl.ds(pl.multiple_of(start + C * third, OWN), OWN)]
            d_normed += dot_nt(rows[:, lanes], columns)
    mark[...] = projected[:8, :128]
    out[0] = projected.astype(BF16)
    unit, inv_scale = unit_of(jnp.concatenate([own0[0], own1[0]], 0))
    d_unit = d_normed * norm[0:1, :]
    first_mean = jnp.mean(d_unit, -1, keepdims=True)
    second_mean = jnp.mean(d_unit * unit, -1, keepdims=True)
    out[1] = (inv_scale * (d_unit - first_mean - unit * second_mean)).astype(BF16)


def call(kernel, scalars, arrays, outs, scratch=(), flops=0, moved=0):
    smem = pl.BlockSpec(memory_space=pltpu.SMEM)
    vmem = pl.BlockSpec(memory_space=pltpu.VMEM)
    return pl.pallas_call(
        kernel,
        out_shape=[jax.ShapeDtypeStruct(shape, dtype) for shape, dtype in outs],
        in_specs=[smem] + [vmem] * len(arrays),
        out_specs=[vmem] * len(outs),
        scratch_shapes=list(scratch),
        compiler_params=pltpu.CompilerParams(vmem_limit_bytes=8 * 2**20),
        cost_estimate=pl.CostEstimate(flops=flops, bytes_accessed=moved, transcendentals=0),
        name=kernel.__name__,
    )(scalars, *arrays)


def on_device(inputs, norm_params, w_qkv, w_proj, upstream):
    place = lax.axis_index("wide")
    column = lax.axis_index("narrow")
    x, y, z = place % 4, place // 4 % 4, place // 16
    core = column % 2
    row = 1 - y % 2
    window = (place - 4) % 64 // 8
    spot = jnp.stack([x, y, core, z, row]).astype(jnp.int32)
    flags = jnp.stack([4 * (window == 7), 2 * (column == 3), row, x]).astype(jnp.int32)

    own_inputs, own_upstream = inputs[0, 0], upstream[0, 0]
    upper_y = (jnp.arange(8)[:, None] < 4) != (row == 1)
    both = jnp.stack([own_inputs, own_upstream]).reshape(2, 8, 2, 8, C)
    mine = jnp.where(upper_y, both[:, :, 1], both[:, :, 0])
    other = jnp.where(upper_y, both[:, :, 0], both[:, :, 1])
    lower_in = move(mine[:, :4], lambda p, n: (p, n - 1))
    other_in = move(other[:, 4:], lambda p, n: (partner_of(p), n))
    cross_in = move(other[:, :4], lambda p, n: (partner_of(p), n - 1))

    part0 = jnp.stack([mine[:, 4:], lower_in], 1).reshape(2, SLAB // 2, C)
    parts0 = [part0] + [move(part0, over_x(mask)) for mask in (1, 2, 3)]
    part1 = jnp.stack([other_in, cross_in], 1).reshape(2, SLAB // 2, C)
    parts1 = [part1] + [move(part1, over_x(mask)) for mask in (1, 2, 3)]
    half = TOKENS // 2
    normed0, qkv0, up0, stats0 = call(
        first_kernel,
        flags,
        (*parts0, norm_params, w_qkv, w_proj),
        [((half, C), BF16), ((half, 3 * OWN), BF16), ((half, OWN), BF16), ((half, 128), F32)],
        flops=10_000_000_000,
        moved=3_000_000,
    )
    r0, r1, r2, r3, d_t, a_t, normed1, stats1 = call(
        attention_kernel,
        flags,
        (*parts1, normed0, qkv0, up0, norm_params, w_qkv, w_proj),
        [((SLAB, C), BF16)] * 4
        + [((3 * OWN, TOKENS), F32), ((OWN, TOKENS), BF16), ((half, C), BF16), ((half, 128), F32)],
        flops=1_200_000_000,
        moved=6_000_000,
    )

    keep, send = call(
        gradient_kernel,
        spot,
        (*parts0, *parts1, r0, r1, r2, r3, d_t, a_t, normed0, normed1, stats0, stats1, w_qkv),
        [((16, 72, 128), F32)] * 2,
        scratch=[
            pltpu.VMEM((3 * OWN, C), F32),
            pltpu.VMEM((C, OWN), F32),
            pltpu.VMEM((C, 128), F32),
        ],
        flops=20_000_000_000,
        moved=6_000_000,
    )
    received = move(send, over_narrow(1))
    blocks = [slice(4 * mask, 4 * mask + 4) for mask in range(4)]
    halves = [keep[block] + received[block] for block in blocks]
    halves[1:] = [half.astype(BF16) for half in halves[1:]]
    from_y = [halves[0]] + [move(halves[mask], over_y(mask)) for mask in (1, 2, 3)]
    returned = [r0] + [
        move(rows, over_x(mask)) for mask, rows in ((1, r1), (2, r2), (3, r3))
    ]
    *from_y, returned[1], returned[2] = lax.optimization_barrier(
        (*from_y, returned[1], returned[2])
    )
    back, mark = call(
        token_kernel,
        spot,
        (*returned, part0, part1, w_qkv, w_proj, norm_params),
        [((2, SLAB, C), BF16), ((8, 128), F32)],
        flops=500_000_000,
        moved=4_000_000,
    )
    share = ((72, 128), F32)
    sums = [piece.astype(F32) for piece in from_y]
    x_parts = [(sums[0][k] + sums[1][k]) + (sums[2][k] + sums[3][k]) for k in range(4)]
    from_x = [x_parts[0]] + [move(x_parts[mask], over_x(mask)) for mask in (1, 2, 3)]
    from_x[1], from_x[2], from_x[3], mark = lax.optimization_barrier(
        (from_x[1], from_x[2], from_x[3], mark)
    )
    back = back.reshape(2, 4, 4, 8, C)
    crossed = move(back[:, 2:], lambda p, n: (partner_of(p), n))
    z_parts = call(z_parts_kernel, spot, (*from_x, mark), [share] * 4)
    line = [z_parts[0]] + [move(z_parts[mask], over_z(mask)) for mask in (1, 2, 3)]
    line[1], line[2], line[3], crossed = lax.optimization_barrier(
        (line[1], line[2], line[3], crossed)
    )
    line = (line[0] + line[1]) + (line[2] + line[3])
    last = [line] + [move(line, over_narrow(mask)) for mask in (1, 2, 3)]
    lower = move(jnp.stack([back[:, 1], crossed[:, 1]], 1), lambda p, n: (p, n + 1))
    output, grad_inputs = call(
        merge_kernel,
        spot,
        (own_inputs, own_upstream, back[:, 0], lower[:, 0], crossed[:, 0], lower[:, 1]),
        [((8, 16, C), BF16)] * 2,
    )
    last[1], last[2], last[3], output, grad_inputs = lax.optimization_barrier(
        (last[1], last[2], last[3], output, grad_inputs)
    )
    grad_qkv, grad_proj, grad_norm = call(
        last_kernel, spot, last, [((24, C), F32), ((8, C), F32), ((2, 8), F32)]
    )
    return (
        output[None, None], grad_inputs[None, None], grad_qkv.T, grad_proj.T, grad_norm
    )


def solution(mesh):
    in_specs = (
        P(None, "wide", "narrow", None, None),
        P(),
        P(),
        P(),
        P(None, "wide", "narrow", None, None),
    )
    out_specs = (
        P(None, "wide", "narrow", None, None),
        P(None, "wide", "narrow", None, None),
        P(None, "wide"),
        P(None, "wide"),
        P(None, "wide"),
    )
    return jax.shard_map(
        on_device, mesh=mesh, in_specs=in_specs, out_specs=out_specs, check_vma=False
    )
```
